32 devices in a mesh: pipe: 4 (over z), dp: 8 (over y, x, core).
Axes of the slice: x: 2, y: 2, z: 4, core: 2. Of those that a mesh axis runs over, the one named last changes fastest.
Arguments:
- hidden: bfloat16 [256, 2048], P('dp', 'pipe'), may hold values from -6 to 6
- lengths: int32 [32, 4], P('dp'), may hold values from 1 to 3, as said below
- route: int32 [32, 2], P('dp'), may hold values from 0 to 7, as said below
- gain: float32 [8, 2048], P('pipe'), may hold values from 0.5 to 1.5
- key_weight: bfloat16 [8, 2048, 128], P('pipe'), may hold values from -0.125 to 0.125
- value_weight: bfloat16 [8, 2048, 128], P('pipe'), may hold values from -0.125 to 0.125
- cotangent: bfloat16 [256, 2048], P('dp'), may hold values from -6 to 6
Outputs:
- input_grad: bfloat16 [256, 2048], P('dp', 'pipe')
- key_grad: float32 [8, 2048, 128], P('pipe', 'dp')
- value_grad: float32 [8, 2048, 128], P('pipe', 'dp')
The draws below stay inside these ranges and needn't reach their ends.
Inputs may be any that keep to these rules, and one draw needn't show every extreme that they name: `lengths`: in every micro-batch the first 2 documents fill exactly the first 4 rows, and the others the rest. `route`: for each micro-batch index and each column, the destinations of the 8 groups are all different; and the 8 halves of one group go to 8 different groups.
All inputs are finite; a program needn't handle non-finite values.
Results may differ from the reference program's by a relative error of at most 0.035.
Values may be sent and summed in bfloat16 or wider, within the bound.
No kernel may reach another device: no remote copies, remote signals or barrier semaphores. Data moves between devices by JAX's collectives and lax.ppermute only.
A program may use at most 64 MiB of HBM per device.

```python
import jax
import jax.numpy as jnp
from jax import lax

DH = 128
S = 8
DOCS = 4
MB = 4
F = 2048
GROUPS = 8
LAYERS = 8
N_PIPE = 4
N_DP = 8


def draw_lengths(key, part):
    key = jax.random.fold_in(key, 11)
    half_rows = S // 2
    per_half = DOCS // 2
    row_keys = jax.random.split(key, GROUPS * MB * 2)

    def one_half(row_key):
        shuffled = jax.random.permutation(row_key, half_rows - 1) + 1
        cuts = jnp.sort(shuffled[:per_half - 1]).astype(jnp.int32)
        bounds = jnp.concatenate([jnp.zeros((1,), jnp.int32), cuts, jnp.full((1,), half_rows, jnp.int32)])
        return bounds[1:] - bounds[:-1]
    halves = jax.vmap(one_half)(row_keys)
    forced = jnp.concatenate([jnp.ones((per_half - 1,), jnp.int32), jnp.full((1,), half_rows - per_half + 1, jnp.int32)])
    halves = halves.at[0].set(forced)
    return halves.reshape(GROUPS * MB, DOCS).astype(jnp.int32)


def draw_route(key, part):
    key = jax.random.fold_in(key, 12)
    first_key, second_key, third_key = jax.random.split(key, 3)
    row_shift = jax.random.permutation(first_key, GROUPS).astype(jnp.int32)
    column_shift = jax.random.permutation(second_key, GROUPS).astype(jnp.int32)
    relabel = jax.random.permutation(third_key, GROUPS).astype(jnp.int32)
    square = (row_shift[:, None] + column_shift[None, :]) % GROUPS
    return relabel[square].reshape(GROUPS * MB, 2).astype(jnp.int32)


def block_levels(key, extent, cuts, low, top_value):
    level, own = 1.0, jax.random.fold_in(key, 6)
    for dim, parts in cuts:
        heights = jnp.exp(jax.random.uniform(jax.random.fold_in(own, dim), (parts,), jnp.float32, low / len(cuts), top_value / len(cuts)))
        level = level * jnp.repeat(heights, extent[dim] // parts).reshape([-1 if axis == dim else 1 for axis in range(len(extent))])
    return level


def normal_values(stream_key, extent, spread, limit, shards=(), kind=jnp.bfloat16):
    drawn = jax.random.normal(stream_key, extent, jnp.float32) * spread
    if len(shards) > 0:
        drawn = block_levels(stream_key, extent, shards, -0.22, 0.18) * drawn
    return jnp.clip(drawn, min=-limit, max=limit).astype(kind)


def setup_inputs(seed: int = 0) -> dict:
    key_of = jax.random.split(jax.random.key(seed), 8)
    return {
        "hidden": normal_values(key_of[0], (GROUPS * MB * S, F), 1.0, 6.0, ((0, 8), (1, 4))),
        "lengths": draw_lengths(jax.random.fold_in(key_of[7], 71), 0),
        "route": draw_route(jax.random.fold_in(key_of[7], 71), 0),
        "gain": jnp.clip(1.0 + 0.1 * jax.random.normal(key_of[3], (LAYERS, F), jnp.float32), 0.5, 1.5),
        "key_weight": normal_values(key_of[4], (LAYERS, F, DH), F ** -0.5, 0.125, ((0, 4),)),
        "value_weight": normal_values(key_of[5], (LAYERS, F, DH), F ** -0.5, 0.125, ((0, 4),)),
        "cotangent": normal_values(key_of[6], (GROUPS * MB * S, F), 1.0, 6.0, ((0, 8),)),
    }


ROPE_BASE = 500000.0
EPSILON = 1e-05
NEGATIVE = -1e+30

def document_positions(lengths, row_count):
    doc_ends = jnp.cumsum(lengths, axis=-1).astype(jnp.int32)
    doc_starts = doc_ends - lengths
    row_numbers = jnp.arange(row_count, dtype=jnp.int32)
    document = lax.optimization_barrier(jnp.sum((row_numbers[None, :, None] >= doc_ends[:, None, :-1]).astype(jnp.int32), axis=-1, dtype=jnp.int32))
    picked = document[:, :, None] == jnp.arange(lengths.shape[1], dtype=jnp.int32)[None, None, :]
    opening = lax.optimization_barrier(jnp.sum(jnp.where(picked, doc_starts[:, None, :], 0), axis=-1, dtype=jnp.int32))
    return (document, row_numbers[None, :] - opening)

def rotary_tables(position, head_size):
    frequency = ROPE_BASE ** (-(jnp.arange(head_size // 2, dtype=jnp.float32) * 2.0 / head_size))
    angles = position.astype(jnp.float32)[..., None] * frequency
    return (jnp.cos(angles), jnp.sin(angles))

def rotate(vectors, cosine_table, sine_table):
    midpoint = vectors.shape[-1] // 2
    front_half = vectors[..., :midpoint]
    rear_half = vectors[..., midpoint:]
    return jnp.concatenate([front_half * cosine_table - rear_half * sine_table, rear_half * cosine_table + front_half * sine_table], axis=-1)

def normalize(hidden_in, gain_row):
    widened = hidden_in.astype(jnp.float32)
    return widened * lax.rsqrt(lax.optimization_barrier(jnp.mean(widened * widened, axis=-1, keepdims=True)) + EPSILON) * gain_row

def attend_layer(hidden_in, gain_row, key_proj, value_proj, key_zero, value_zero, document, position, cosine_table, sine_table):
    batch_count, row_count, feature_count = hidden_in.shape
    head_size = key_proj.shape[1]
    head_count = feature_count // head_size
    widened = hidden_in.astype(jnp.float32)
    normed = normalize(hidden_in, gain_row)
    packed = normed.astype(jnp.bfloat16)
    flattened = packed.reshape(batch_count * row_count, feature_count)
    key_pre = jnp.dot(flattened, key_proj, preferred_element_type=jnp.float32).reshape(batch_count, row_count, head_size) + key_zero
    value_pre = jnp.dot(flattened, value_proj, preferred_element_type=jnp.float32).reshape(batch_count, row_count, head_size) + value_zero
    queries = rotate(normed.reshape(batch_count, row_count, head_count, head_size), cosine_table[:, :, None, :], sine_table[:, :, None, :]).astype(jnp.bfloat16)
    key_vecs = rotate(key_pre, cosine_table, sine_table).astype(jnp.bfloat16)
    values = value_pre.astype(jnp.bfloat16)
    scores = jnp.einsum('bshd,btd->bhst', queries.astype(jnp.float32), key_vecs.astype(jnp.float32)) * head_size ** (-0.5)
    allowed = (document[:, :, None] == document[:, None, :]) & (position[:, None, :] <= position[:, :, None])
    scores = jnp.where(allowed[:, None, :, :], scores, NEGATIVE)
    ceiling = lax.stop_gradient(lax.optimization_barrier(jnp.max(scores, axis=-1, keepdims=True)))
    raised = jnp.exp(scores - ceiling)
    weights = (raised / lax.optimization_barrier(jnp.sum(raised, axis=-1, keepdims=True))).astype(jnp.bfloat16)
    mixture = jnp.einsum('bhst,btd->bshd', weights.astype(jnp.float32), values.astype(jnp.float32)).reshape(batch_count, row_count, feature_count)
    return widened + mixture

def reference(hidden, lengths, route, gain, key_weight, value_weight, cotangent):
    groups = N_DP
    sections = N_PIPE
    layers = 2 * sections
    half_rows = S // 2
    document, position = document_positions(lengths, S)
    document = document.reshape(groups, MB, S)
    position = position.reshape(groups, MB, S)
    source_of = jnp.argsort(route.reshape(groups, MB, 2), axis=0).astype(jnp.int32)
    batch_numbers = jnp.arange(MB, dtype=jnp.int32)[None, :]

    def arrange(source):
        leading = source[:, :, :half_rows][source_of[:, :, 0], batch_numbers]
        trailing = source[:, :, half_rows:][source_of[:, :, 1], batch_numbers]
        return jnp.concatenate([leading, trailing], axis=2)
    recv_document = arrange(document).reshape(groups * MB, S)
    recv_position = arrange(position).reshape(groups * MB, S)
    cosine_table, sine_table = rotary_tables(recv_position, DH)

    def slot_of(layer_index):
        return 2 * (layer_index % sections) + layer_index // sections

    def network(source, key_zeros, value_zeros):
        current = arrange(source.reshape(groups, MB, S, F)).reshape(groups * MB, S, F).astype(jnp.float32)
        inputs = []
        for layer_index in range(layers):
            weight_slot = slot_of(layer_index)
            inputs.append(current)
            current = attend_layer(current, gain[weight_slot], key_weight[weight_slot], value_weight[weight_slot], key_zeros[layer_index], value_zeros[layer_index], recv_document, recv_position, cosine_table, sine_table)
        return (current, inputs)
    zero_terms = jnp.zeros((layers, groups * MB, S, DH), jnp.float32)
    final_rows, pullback, inputs = jax.vjp(network, hidden, zero_terms, zero_terms, has_aux=True)
    source_grad, key_pre_grad, value_pre_grad = pullback(cotangent.astype(jnp.float32).reshape(groups * MB, S, F))
    key_rows = [None] * layers
    value_rows = [None] * layers
    for layer_index in range(layers):
        weight_slot = slot_of(layer_index)
        packed = normalize(inputs[layer_index], gain[weight_slot]).astype(jnp.bfloat16).reshape(groups * MB * S, F)
        key_rows[weight_slot] = jnp.dot(packed.T, key_pre_grad[layer_index].astype(jnp.bfloat16).reshape(groups * MB * S, DH), preferred_element_type=jnp.float32)
        value_rows[weight_slot] = jnp.dot(packed.T, value_pre_grad[layer_index].astype(jnp.bfloat16).reshape(groups * MB * S, DH), preferred_element_type=jnp.float32)
    return (source_grad.astype(jnp.bfloat16).reshape(groups * MB * S, F), jnp.stack(key_rows), jnp.stack(value_rows))
```

```python
import functools

import jax
import jax.numpy as jnp
from jax import lax
from jax.experimental import pallas as pl
from jax.experimental.pallas import tpu as pltpu
from jax.sharding import PartitionSpec as P

ROPE_BASE = 500000.0
EPSILON = 1e-05
NEGATIVE = -1e30
LANES = 128
SAVED = 5
VMEM_BYTES = 56 * 1024 * 1024


def iota(shape, dim):
    return lax.broadcasted_iota(jnp.int32, shape, dim)


def as_float(flags):
    return jnp.where(flags, 1.0, 0.0).astype(jnp.float32)


def contract(left, right, left_dim, right_dim):
    return lax.dot_general(
        left, right, (((left_dim,), (right_dim,)), ((), ())), preferred_element_type=jnp.float32
    )


def pieces_of(column_count):
    return 2 if column_count % (2 * LANES) == 0 else 1


def pack_kernel(lengths_ref, route_ref, hidden_ref, out_ref, *, groups):
    micro_count, doc_count = lengths_ref.shape
    source_rows, column_count = hidden_ref.shape
    row_count = source_rows // micro_count
    half = row_count // 2
    pieces = pieces_of(column_count)
    width = column_count // pieces
    total = out_ref.shape[0]

    shape = (source_rows, LANES)
    batch, offset = iota(shape, 0) // row_count, iota(shape, 0) % row_count
    document = jnp.zeros(shape, jnp.int32)
    opening = jnp.zeros(shape, jnp.int32)
    for micro in range(micro_count):
        end = jnp.int32(0)
        for doc in range(doc_count - 1):
            end = end + lengths_ref[micro, doc]
            passed = (batch == micro) & (offset >= end)
            document = document + jnp.where(passed, 1, 0)
            opening = jnp.where(passed, end, opening)
    lane = iota(shape, 1)
    first = offset < half
    tags = jnp.where(
        lane == 0,
        jnp.where(first, 1, 0),
        jnp.where(
            lane == 1,
            jnp.where(first, 0, 1),
            jnp.where(lane == 2, document, jnp.where(lane == 3, offset - opening, 0)),
        ),
    )
    tags = tags.astype(jnp.float32).astype(jnp.bfloat16)

    shape = (total, source_rows)
    row, source = iota(shape, 0), iota(shape, 1)
    slot = source // half
    target = jnp.full(shape, -1, jnp.int32)
    for micro in range(micro_count):
        for side in range(2):
            target = jnp.where(
                slot == 2 * micro + side, micro * groups + route_ref[micro, side], target
            )
    going = target == row // row_count
    inner, wanted = row % row_count, source % half
    packed = jnp.zeros((total, width), jnp.float32)
    for piece in range(pieces):
        chosen = as_float(going & (inner == piece * half + wanted)).astype(jnp.bfloat16)
        packed += contract(chosen, hidden_ref[:, piece * width : (piece + 1) * width], 1, 0)
    chosen = as_float(going & (inner % half == wanted)).astype(jnp.bfloat16)
    out_ref[:, :width] = packed.astype(jnp.bfloat16)
    out_ref[:, width:] = contract(chosen, tags, 1, 0).astype(jnp.bfloat16)


def choosers(tags, row_count, pieces):
    half = row_count // 2
    shape = (tags.shape[0], row_count)
    inner, wanted = iota(shape, 0) % row_count, iota(shape, 1)
    came = jnp.where(wanted < half, tags[:, 0:1], tags[:, 1:2])
    return [
        jnp.where(inner == piece * half + wanted % half, came, 0.0).astype(jnp.bfloat16)
        for piece in range(pieces)
    ]


def turned(vector, cosine, sine):
    return vector * cosine + pltpu.roll(vector, vector.shape[1] // 2, 1) * sine


def heads_down(rows, head_size):
    count = rows.shape[1] // head_size
    return jnp.concatenate(
        [rows[:, head * head_size : (head + 1) * head_size] for head in range(count)], axis=0
    )


def heads_across(stacked, row_count):
    count = stacked.shape[0] // row_count
    return jnp.concatenate(
        [stacked[head * row_count : (head + 1) * row_count] for head in range(count)], axis=1
    )


def forward_layer(rows, gain_row, weight, cosine, sine, allowed):
    row_count, feature_count = rows.shape
    head_size = cosine.shape[1]
    scale = lax.rsqrt(jnp.sum(rows * rows, axis=1, keepdims=True) / feature_count + EPSILON)
    normed = rows * scale * gain_row
    pair = jnp.dot(normed.astype(jnp.bfloat16), weight, preferred_element_type=jnp.float32)
    stacked = heads_down(normed, head_size)
    repeats = stacked.shape[0] // row_count
    queries = turned(
        stacked, jnp.tile(cosine, (repeats, 1)), jnp.tile(sine, (repeats, 1))
    ).astype(jnp.bfloat16)
    keys = turned(pair[:, :head_size], cosine, sine).astype(jnp.bfloat16)
    values = pair[:, head_size:].astype(jnp.bfloat16)
    scores = contract(keys, queries, 1, 1) * head_size ** (-0.5)
    scores = jnp.where(allowed, scores, NEGATIVE)
    raised = jnp.exp(scores - jnp.max(scores, axis=0, keepdims=True))
    weights = raised / jnp.sum(raised, axis=0, keepdims=True)
    mixed = contract(weights.astype(jnp.bfloat16), values, 0, 0)
    kept = (scale, queries, keys, values, weights)
    return rows + heads_across(mixed, row_count), kept


def backward_layer(upstream, rows, gain_row, weight, cosine, sine, kept):
    scale, queries, keys, values, weights = kept
    row_count, feature_count = rows.shape
    head_size = cosine.shape[1]
    stacked = heads_down(upstream, head_size).astype(jnp.bfloat16)
    d_weights = contract(values, stacked, 1, 1).astype(jnp.bfloat16).astype(jnp.float32)
    d_values = contract(weights.astype(jnp.bfloat16), stacked, 1, 0)
    d_scores = weights * (d_weights - jnp.sum(d_weights * weights, axis=0, keepdims=True))
    d_scores = (d_scores * head_size ** (-0.5)).astype(jnp.bfloat16)
    d_keys = contract(d_scores, queries, 1, 0)
    terms = jnp.concatenate([turned(d_keys, cosine, -sine), d_values], axis=1)
    terms = terms.astype(jnp.bfloat16)
    d_queries = contract(d_scores, keys, 0, 0)
    repeats = stacked.shape[0] // row_count
    d_queries = turned(d_queries, jnp.tile(cosine, (repeats, 1)), jnp.tile(-sine, (repeats, 1)))
    d_normed = contract(terms, weight, 1, 1) + heads_across(d_queries, row_count)
    scaled = d_normed * gain_row
    inner = jnp.sum(scaled * rows, axis=1, keepdims=True) / feature_count
    return upstream + scale * scaled - rows * (scale * scale * scale * inner), terms


def save_layer(index, rows, kept, rows_ref, scale_ref, queries_ref, pair_ref, weights_ref):
    scale, queries, keys, values, weights = kept
    rows_ref[index] = rows
    scale_ref[index] = jnp.broadcast_to(scale, scale_ref.shape[1:])
    queries_ref[index] = queries
    pair_ref[index] = jnp.concatenate([keys, values], axis=1).astype(jnp.float32)
    weights_ref[index] = weights


def load_layer(index, rows_ref, scale_ref, queries_ref, pair_ref, weights_ref):
    pair = pair_ref[index].astype(jnp.bfloat16)
    head_size = pair.shape[1] // 2
    kept = (
        scale_ref[index][:, 0:1],
        queries_ref[index],
        pair[:, :head_size],
        pair[:, head_size:],
        weights_ref[index],
    )
    return rows_ref[index], kept


def saved_shapes(count, row_count, feature_count, head_size):
    heads = feature_count // head_size
    return [
        jax.ShapeDtypeStruct((count, row_count, feature_count), jnp.float32),
        jax.ShapeDtypeStruct((count, row_count, LANES), jnp.float32),
        jax.ShapeDtypeStruct((count, heads * row_count, head_size), jnp.bfloat16),
        jax.ShapeDtypeStruct((count, row_count, 2 * head_size), jnp.float32),
        jax.ShapeDtypeStruct((count, row_count, heads * row_count), jnp.float32),
    ]


def repeat_steps(count, step, carry):
    if count <= 8:
        for index in range(count):
            carry = step(index, carry)
        return carry
    return lax.fori_loop(0, count, step, carry)


def forward_steps(rows, own, gain_ref, weight_ref, tables, saved):
    cosine, sine, allowed = tables

    def step(index, rows):
        place = lax.bitwise_xor(own, index)
        gain_row = gain_ref[pl.ds(place, 1), :]
        after, kept = forward_layer(rows, gain_row, weight_ref[place], cosine, sine, allowed)
        save_layer(index, rows, kept, *saved)
        return after

    return repeat_steps(weight_ref.shape[0], step, rows)


def backward_steps(upstream, own, gain_ref, weight_ref, tables, saved, out_ref, groups):
    cosine, sine, _ = tables
    count = weight_ref.shape[0]
    share = weight_ref.shape[1] // groups
    term_width = weight_ref.shape[2]
    grad_width = out_ref.shape[3] - share - term_width

    def step(back, upstream):
        index = count - 1 - back
        place = lax.bitwise_xor(own, index)
        gain_row = gain_ref[pl.ds(place, 1), :]
        rows, kept = load_layer(index, *saved)
        before, terms = backward_layer(
            upstream, rows, gain_row, weight_ref[place], cosine, sine, kept
        )
        packed = (rows * kept[0] * gain_row).astype(jnp.bfloat16)
        for group in range(groups):
            out_ref[index, group, :, :term_width] = terms
            out_ref[index, group, :, term_width + grad_width :] = packed[
                :, group * share : (group + 1) * share
            ]
        return before

    return repeat_steps(count, step, upstream)


def fill(turn, pieces, gain_ref, weight_ref, sems):
    gains, key_ref, value_ref, shares = pieces
    groups = len(shares)
    share = weight_ref.shape[1] // groups
    head_size = key_ref.shape[2]
    own = lax.axis_index("dp")
    copies = [
        pltpu.make_async_copy(key_ref.at[turn], weight_ref.at[0, :, :head_size], sems.at[groups]),
        pltpu.make_async_copy(
            value_ref.at[turn], weight_ref.at[0, :, head_size:], sems.at[groups + 1]
        ),
    ]
    for offset, ref in enumerate(shares):
        start = pl.multiple_of(lax.bitwise_xor(own, offset) * share, share)
        copies.append(
            pltpu.make_async_copy(
                ref, weight_ref.at[pl.ds(1, ref.shape[0]), pl.ds(start, share)], sems.at[offset]
            )
        )
    for copy in copies:
        copy.start()
    for place, ref in enumerate(gains):
        gain_ref[pl.ds(place, 1), :] = ref[pl.ds(turn, 1), :]
    return copies


def first_kernel(arrived_ref, *rest, sections, groups, turn):
    pieces, rest = split_pieces(rest, sections, groups)
    rows_ref, table_ref, tags_ref, *saved, gain_ref, weight_ref, sems = rest
    copies = fill(turn, pieces, gain_ref, weight_ref, sems)
    row_count, feature_count = rows_ref.shape
    head_size = weight_ref.shape[2] // 2
    column_count = feature_count // sections
    pieces = pieces_of(column_count)
    width = column_count // pieces
    block = arrived_ref.shape[0] // sections
    tags = arrived_ref[:block, width:].astype(jnp.float32)
    tags_ref[...] = tags
    chosen = choosers(tags, row_count, pieces)
    cuts = []
    for section in range(sections):
        part = arrived_ref[section * block : (section + 1) * block, :width]
        cuts += [contract(chooser, part, 0, 0) for chooser in chosen]
    rows = jnp.concatenate(cuts, axis=1)
    own = contract(chosen[0], tags.astype(jnp.bfloat16), 0, 0)
    document, position = own[:, 2:3], own[:, 3:4]
    lane = iota((1, head_size), 1)
    middle = head_size // 2
    exponent = (lane % middle).astype(jnp.float32) * (2.0 / head_size)
    angles = position * jnp.exp(exponent * -jnp.log(jnp.float32(ROPE_BASE)))
    cosine = jnp.cos(angles)
    sine = jnp.where(lane < middle, -jnp.sin(angles), jnp.sin(angles))
    shape = (row_count, row_count * feature_count // head_size)
    pick = as_float(iota(shape, 1) % row_count == iota(shape, 0))
    document_across = jnp.sum(document * pick, axis=0, keepdims=True)
    position_across = jnp.sum(position * pick, axis=0, keepdims=True)
    allowed = (document == document_across) & (position <= position_across)
    table_ref[0, :, :head_size] = cosine
    table_ref[1, :, :head_size] = sine
    table_ref[2] = as_float(allowed)
    for copy in copies:
        copy.wait()
    own = lax.axis_index("pipe")
    tables = (cosine, sine, allowed)
    rows_ref[...] = forward_steps(rows, own, gain_ref, weight_ref, tables, saved)


def tables_of(table_ref, head_size):
    return table_ref[0, :, :head_size], table_ref[1, :, :head_size], table_ref[2] > 0.5


def split_pieces(refs, sections, groups):
    gains, rest = refs[:sections], refs[sections:]
    return (gains, rest[0], rest[1], rest[2 : 2 + groups]), rest[2 + groups :]


def second_kernel(rows_ref, upstream_ref, table_ref, *rest, sections, groups, turn):
    pieces, rest = split_pieces(rest, sections, groups)
    upstream_out, out_ref, *saved, gain_ref, weight_ref, sems = rest
    copies = fill(turn, pieces, gain_ref, weight_ref, sems)
    own = lax.axis_index("pipe")
    tables = tables_of(table_ref, weight_ref.shape[2] // 2)
    for copy in copies:
        copy.wait()
    forward_steps(rows_ref[...], own, gain_ref, weight_ref, tables, saved)
    upstream_out[...] = backward_steps(
        upstream_ref[...], own, gain_ref, weight_ref, tables, saved, out_ref, groups
    )


def third_kernel(upstream_ref, table_ref, tags_ref, *rest, sections, groups, turn):
    saved, rest = rest[:SAVED], rest[SAVED:]
    pieces, rest = split_pieces(rest, sections, groups)
    out_ref, gain_ref, weight_ref, sems = rest
    copies = fill(turn, pieces, gain_ref, weight_ref, sems)
    own = lax.axis_index("pipe")
    sections, feature_count, term_width = weight_ref.shape
    tables = tables_of(table_ref, term_width // 2)
    for copy in copies:
        copy.wait()
    grads = backward_steps(
        upstream_ref[...], own, gain_ref, weight_ref, tables, saved, out_ref, groups
    ).astype(jnp.bfloat16)
    row_count = grads.shape[0]
    column_count = feature_count // sections
    pieces = pieces_of(column_count)
    width = column_count // pieces
    chosen = choosers(tags_ref[...], row_count, pieces)
    for section in range(sections):
        start = section * column_count
        going = contract(chosen[0], grads[:, start : start + width], 1, 0)
        for piece in range(1, pieces):
            left = start + piece * width
            going += contract(chosen[piece], grads[:, left : left + width], 1, 0)
        going = going.astype(jnp.bfloat16)
        for group in range(groups):
            out_ref[section, group, :, term_width : term_width + width] = going[
                group * row_count : (group + 1) * row_count
            ]


def last_kernel(
    route_ref, late_ref, early_ref, grad_ref, key_ref, value_ref, *, groups, width
):
    micro_count = route_ref.shape[0]
    source_rows, column_count = grad_ref.shape
    row_count = source_rows // micro_count
    half = row_count // 2
    pieces = column_count // width
    head_size = key_ref.shape[2]
    term_width = 2 * head_size
    for index, (ref, gap) in enumerate(((late_ref, width), (early_ref, 0))):
        total = contract(ref[:, term_width + gap :], ref[:, :term_width], 0, 0)
        key_ref[index] = total[:, :head_size]
        value_ref[index] = total[:, head_size:]
    shape = (source_rows, late_ref.shape[0])
    row, source = iota(shape, 1), iota(shape, 0)
    slot = source // half
    target = jnp.full(shape, -1, jnp.int32)
    for micro in range(micro_count):
        for side in range(2):
            target = jnp.where(
                slot == 2 * micro + side, micro * groups + route_ref[micro, side], target
            )
    going = target == row // row_count
    inner, wanted = row % row_count, source % half
    for piece in range(pieces):
        chosen = as_float(going & (inner == piece * half + wanted)).astype(jnp.bfloat16)
        grad_ref[:, piece * width : (piece + 1) * width] = contract(
            chosen, late_ref[:, term_width : term_width + width], 1, 0
        ).astype(jnp.bfloat16)


def call(kernel, outs, operands, scalars=0, whole=0, scratch=()):
    spaces = [pltpu.SMEM] * scalars + [pltpu.VMEM] * (len(operands) - scalars - whole)
    spaces += [pl.ANY] * whole
    return pl.pallas_call(
        kernel,
        out_shape=outs,
        in_specs=[pl.BlockSpec(memory_space=space) for space in spaces],
        out_specs=[pl.BlockSpec(memory_space=pltpu.VMEM)] * len(outs),
        scratch_shapes=scratch,
        compiler_params=pltpu.CompilerParams(vmem_limit_bytes=VMEM_BYTES),
    )(*operands)


def exchange(blocks):
    return lax.all_to_all(blocks, ("pipe", "dp"), split_axis=0, concat_axis=0, tiled=True)


def swapped(value, axis, mask):
    pairs = [(source, source ^ mask) for source in range(lax.axis_size(axis))]
    return lax.ppermute(value, axis, pairs)


def gather_shares(own_share):
    sections, groups = lax.axis_size("pipe"), lax.axis_size("dp")
    column = jnp.stack([swapped(own_share, "pipe", mask) for mask in range(1, sections)])
    plane = [column] + [swapped(column, "dp", 2 * mask) for mask in range(1, groups // 2)]
    shares = []
    for part in plane:
        shares += [part, swapped(part, "dp", 1)]
    return shares


def body(hidden, lengths, route, gain, key_weight, value_weight, cotangent):
    groups = lax.axis_size("dp")
    sections = lax.axis_size("pipe")
    group_index = lax.axis_index("dp")
    section_index = lax.axis_index("pipe")
    micro_count = lengths.shape[0]
    assert micro_count == sections
    source_rows, column_count = hidden.shape
    row_count = source_rows // micro_count
    feature_count = gain.shape[1]
    head_size = key_weight.shape[2]
    heads = feature_count // head_size
    share = feature_count // groups
    width = column_count // pieces_of(column_count)
    devices = sections * groups

    shares = []
    for turn in range(2):
        parts = [
            lax.dynamic_slice(array, (turn, group_index * share, 0), (1, share, head_size))[0]
            for array in (key_weight, value_weight)
        ]
        shares.append(gather_shares(jnp.concatenate(parts, axis=1)))
    gains = [gain] + [swapped(gain, "pipe", mask) for mask in range(1, sections)]

    def layers_call(kernel, turn, outs, operands):
        return call(
            functools.partial(kernel, sections=sections, groups=groups, turn=turn),
            outs,
            (*operands, *gains, key_weight, value_weight, *shares[turn]),
            whole=2 + groups,
            scratch=[
                pltpu.VMEM((sections, feature_count), jnp.float32),
                pltpu.VMEM((sections, feature_count, 2 * head_size), jnp.bfloat16),
                pltpu.SemaphoreType.DMA((groups + 2,)),
            ],
        )

    (outgoing,) = call(
        functools.partial(pack_kernel, groups=groups),
        [jax.ShapeDtypeStruct((devices * row_count, width + LANES), jnp.bfloat16)],
        (lengths, route, hidden),
        scalars=2,
    )
    arrived = exchange(outgoing.reshape(devices, row_count, width + LANES)).reshape(
        devices * row_count, width + LANES
    )
    upstream = lax.dynamic_slice_in_dim(
        cotangent, section_index * row_count, row_count, 0
    ).astype(jnp.float32)

    saved = saved_shapes(sections, row_count, feature_count, head_size)
    rows_shape = jax.ShapeDtypeStruct((row_count, feature_count), jnp.float32)
    middle, tables, tags, *kept = layers_call(
        first_kernel,
        0,
        [
            rows_shape,
            jax.ShapeDtypeStruct((3, row_count, heads * row_count), jnp.float32),
            jax.ShapeDtypeStruct((groups * row_count, LANES), jnp.float32),
            *saved,
        ],
        (arrived,),
    )
    early_shape = (sections, groups, row_count, 2 * head_size + share)
    late_shape = early_shape[:3] + (early_shape[3] + width,)
    upstream, early, *_ = layers_call(
        second_kernel,
        1,
        [rows_shape, jax.ShapeDtypeStruct(early_shape, jnp.bfloat16), *saved],
        (middle, upstream, tables),
    )
    early = exchange(early.reshape((devices,) + early_shape[2:]))
    (late,) = layers_call(
        third_kernel,
        0,
        [jax.ShapeDtypeStruct(late_shape, jnp.bfloat16)],
        (upstream, tables, tags, *kept),
    )
    late = exchange(late.reshape((devices,) + late_shape[2:]))
    grad_shape = jax.ShapeDtypeStruct((2, share, head_size), jnp.float32)
    return tuple(
        call(
            functools.partial(last_kernel, groups=groups, width=width),
            [jax.ShapeDtypeStruct((source_rows, column_count), jnp.bfloat16)] + [grad_shape] * 2,
            (
                route,
                late.reshape(devices * row_count, late_shape[3]),
                early.reshape(devices * row_count, early_shape[3]),
            ),
            scalars=1,
        )
    )


def solution(mesh):
    placed = (
        P("dp", "pipe"),
        P("dp", None),
        P("dp", None),
        P("pipe", None),
        P("pipe", None, None),
        P("pipe", None, None),
        P("dp", None),
    )
    return jax.shard_map(
        body,
        mesh=mesh,
        in_specs=placed,
        out_specs=(P("dp", "pipe"), P("pipe", "dp", None), P("pipe", "dp", None)),
        check_vma=False,
    )
```

```python
import functools

import jax
import jax.numpy as jnp
from jax import lax
from jax.experimental import pallas as pl
from jax.experimental.pallas import tpu as pltpu
from jax.sharding import PartitionSpec as P

ROPE_BASE = 500000.0
EPSILON = 1e-05
NEGATIVE = -1e30
LANES = 128


def iota(shape, dim):
    return lax.broadcasted_iota(jnp.int32, shape, dim)


def as_float(flags):
    return jnp.where(flags, 1.0, 0.0).astype(jnp.float32)


def contract(left, right, left_dim, right_dim):
    return lax.dot_general(
        left, right, (((left_dim,), (right_dim,)), ((), ())), preferred_element_type=jnp.float32
    )


def pieces_of(column_count):
    return 2 if column_count % (2 * LANES) == 0 else 1


def pack_kernel(lengths_ref, route_ref, hidden_ref, out_ref, *, groups):
    micro_count, doc_count = lengths_ref.shape
    source_rows, column_count = hidden_ref.shape
    row_count = source_rows // micro_count
    half = row_count // 2
    pieces = pieces_of(column_count)
    width = column_count // pieces
    total = out_ref.shape[0]

    shape = (source_rows, LANES)
    batch, offset = iota(shape, 0) // row_count, iota(shape, 0) % row_count
    document = jnp.zeros(shape, jnp.int32)
    opening = jnp.zeros(shape, jnp.int32)
    for micro in range(micro_count):
        end = jnp.int32(0)
        for doc in range(doc_count - 1):
            end = end + lengths_ref[micro, doc]
            passed = (batch == micro) & (offset >= end)
            document = document + jnp.where(passed, 1, 0)
            opening = jnp.where(passed, end, opening)
    lane = iota(shape, 1)
    first = offset < half
    tags = jnp.where(
        lane == 0,
        jnp.where(first, 1, 0),
        jnp.where(
            lane == 1,
            jnp.where(first, 0, 1),
            jnp.where(lane == 2, document, jnp.where(lane == 3, offset - opening, 0)),
        ),
    )
    tags = tags.astype(jnp.float32).astype(jnp.bfloat16)

    shape = (total, source_rows)
    row, source = iota(shape, 0), iota(shape, 1)
    slot = source // half
    target = jnp.full(shape, -1, jnp.int32)
    for micro in range(micro_count):
        for side in range(2):
            target = jnp.where(
                slot == 2 * micro + side, micro * groups + route_ref[micro, side], target
            )
    going = target == row // row_count
    inner, wanted = row % row_count, source % half
    packed = jnp.zeros((total, width), jnp.float32)
    for piece in range(pieces):
        chosen = as_float(going & (inner == piece * half + wanted)).astype(jnp.bfloat16)
        packed += contract(chosen, hidden_ref[:, piece * width : (piece + 1) * width], 1, 0)
    chosen = as_float(going & (inner % half == wanted)).astype(jnp.bfloat16)
    out_ref[:, :width] = packed.astype(jnp.bfloat16)
    out_ref[:, width:] = contract(chosen, tags, 1, 0).astype(jnp.bfloat16)


def choosers(tags, row_count, pieces):
    half = row_count // 2
    shape = (tags.shape[0], row_count)
    inner, wanted = iota(shape, 0) % row_count, iota(shape, 1)
    came = jnp.where(wanted < half, tags[:, 0:1], tags[:, 1:2])
    return [
        jnp.where(inner == piece * half + wanted % half, came, 0.0).astype(jnp.bfloat16)
        for piece in range(pieces)
    ]


def turned(vector, cosine, sine):
    return vector * cosine + pltpu.roll(vector, vector.shape[1] // 2, 1) * sine


def heads_down(rows, head_size):
    count = rows.shape[1] // head_size
    return jnp.concatenate(
        [rows[:, head * head_size : (head + 1) * head_size] for head in range(count)], axis=0
    )


def heads_across(stacked, row_count):
    count = stacked.shape[0] // row_count
    return jnp.concatenate(
        [stacked[head * row_count : (head + 1) * row_count] for head in range(count)], axis=1
    )


def turned_heads(rows, cosine, sine):
    stacked = heads_down(rows, cosine.shape[1])
    repeats = stacked.shape[0] // rows.shape[0]
    return turned(stacked, jnp.tile(cosine, (repeats, 1)), jnp.tile(sine, (repeats, 1)))


def forward_layer(rows, gain_row, weight, cosine, sine, allowed):
    row_count, feature_count = rows.shape
    head_size = cosine.shape[1]
    scale = lax.rsqrt(jnp.sum(rows * rows, axis=1, keepdims=True) / feature_count + EPSILON)
    normed = rows * scale * gain_row
    packed = normed.astype(jnp.bfloat16)
    pair = jnp.dot(packed, weight, preferred_element_type=jnp.float32)
    queries = turned_heads(normed, cosine, sine).astype(jnp.bfloat16)
    keys = turned(pair[:, :head_size], cosine, sine).astype(jnp.bfloat16)
    values = pair[:, head_size:].astype(jnp.bfloat16)
    scores = contract(keys, queries, 1, 1) * head_size ** (-0.5)
    scores = jnp.where(allowed, scores, NEGATIVE)
    raised = jnp.exp(scores - jnp.max(scores, axis=0, keepdims=True))
    weights = raised / jnp.sum(raised, axis=0, keepdims=True)
    mixed = contract(weights.astype(jnp.bfloat16), values, 0, 0)
    kept = (scale, keys, values, weights)
    return rows + heads_across(mixed, row_count), packed, kept


def backward_layer(upstream, rows, gain_row, weight, cosine, sine, kept):
    scale, keys, values, weights = kept
    row_count, feature_count = rows.shape
    head_size = cosine.shape[1]
    queries = turned_heads(rows * scale * gain_row, cosine, sine).astype(jnp.bfloat16)
    stacked = heads_down(upstream, head_size).astype(jnp.bfloat16)
    d_weights = contract(values, stacked, 1, 1).astype(jnp.bfloat16).astype(jnp.float32)
    d_values = contract(weights.astype(jnp.bfloat16), stacked, 1, 0)
    d_scores = weights * (d_weights - jnp.sum(d_weights * weights, axis=0, keepdims=True))
    d_scores = (d_scores * head_size ** (-0.5)).astype(jnp.bfloat16)
    d_keys = contract(d_scores, queries, 1, 0)
    terms = jnp.concatenate([turned(d_keys, cosine, -sine), d_values], axis=1)
    terms = terms.astype(jnp.bfloat16)
    d_queries = contract(d_scores, keys, 0, 0)
    repeats = stacked.shape[0] // row_count
    d_queries = turned(d_queries, jnp.tile(cosine, (repeats, 1)), jnp.tile(-sine, (repeats, 1)))
    d_normed = contract(terms, weight, 1, 1) + heads_across(d_queries, row_count)
    scaled = d_normed * gain_row
    inner = jnp.sum(scaled * rows, axis=1, keepdims=True) / feature_count
    return upstream + scale * scaled - rows * (scale * scale * scale * inner), terms


def state_width(feature_count, head_size):
    return feature_count + 4 * head_size


def save_layer(index, rows, kept, state_ref):
    scale, keys, values, weights = kept
    feature_count, head_size = rows.shape[1], keys.shape[1]
    state_ref[index, :, :feature_count] = rows
    parts = (weights, keys, values, jnp.broadcast_to(scale, keys.shape))
    for place, part in enumerate(parts):
        start = feature_count + place * head_size
        state_ref[index, :, start : start + head_size] = part.astype(jnp.float32)


def load_layer(index, state_ref, feature_count):
    head_size = (state_ref.shape[2] - feature_count) // 4
    parts = []
    for place in range(4):
        start = feature_count + place * head_size
        parts.append(state_ref[index, :, start : start + head_size])
    weights, keys, values, scale = parts
    kept = (scale[:, 0:1], keys.astype(jnp.bfloat16), values.astype(jnp.bfloat16), weights)
    return state_ref[index, :, :feature_count], kept


def repeat_steps(count, step, carry):
    if count <= 8:
        for index in range(count):
            carry = step(index, carry)
        return carry
    return lax.fori_loop(0, count, step, carry)


def forward_steps(rows, own, gain_ref, weight_ref, tables, state_ref, packed_ref):
    cosine, sine, allowed = tables
    groups = packed_ref.shape[1]
    share = weight_ref.shape[1] // groups

    def step(index, rows):
        place = lax.bitwise_xor(own, index)
        gain_row = gain_ref[pl.ds(place, 1), :]
        after, packed, kept = forward_layer(
            rows, gain_row, weight_ref[place], cosine, sine, allowed
        )
        for group in range(groups):
            packed_ref[index, group, :, :share] = packed[:, group * share : (group + 1) * share]
        save_layer(index, rows, kept, state_ref)
        return after

    return repeat_steps(weight_ref.shape[0], step, rows)


def backward_steps(upstream, own, gain_ref, weight_ref, tables, state_ref, terms_ref, start):
    cosine, sine, _ = tables
    count = weight_ref.shape[0]
    width = weight_ref.shape[2]

    def step(back, upstream):
        index = count - 1 - back
        place = lax.bitwise_xor(own, index)
        gain_row = gain_ref[pl.ds(place, 1), :]
        rows, kept = load_layer(index, state_ref, weight_ref.shape[1])
        before, terms = backward_layer(
            upstream, rows, gain_row, weight_ref[place], cosine, sine, kept
        )
        for group in range(terms_ref.shape[1]):
            terms_ref[index, group, :, start : start + width] = terms
        return before

    return repeat_steps(count, step, upstream)


def fill(turn, key_ref, value_ref, shares, weight_ref, sems, start):
    share = shares[0].shape[2]
    sections = shares[0].shape[1] + 1
    head_size = key_ref.shape[2]
    own = lax.axis_index("dp")
    copies = [
        (key_ref.at[turn], weight_ref.at[start, :, :head_size]),
        (value_ref.at[turn], weight_ref.at[start, :, head_size:]),
    ]
    for core, ref in enumerate(shares):
        for chip in range(ref.shape[0]):
            place = lax.bitwise_xor(own, 2 * chip + core) * share
            rows = pl.ds(pl.multiple_of(place, share), share)
            copies.append(
                (ref.at[chip], weight_ref.at[pl.ds(start + 1, sections - 1), rows])
            )
    copies = [
        pltpu.make_async_copy(*pair, sems.at[turn, index]) for index, pair in enumerate(copies)
    ]
    for copy in copies:
        copy.start()
    return copies


def unpack_gains(own_ref, tails_ref, gain_ref):
    sections = tails_ref.shape[0] + 1
    width = tails_ref.shape[2]
    lines = gain_ref.shape[1] // width
    for turn in range(2):
        start = sections * turn
        gain_ref[start : start + 1, :] = own_ref[turn : turn + 1, :]
        for place in range(1, sections):
            tail = tails_ref[place - 1].astype(jnp.float32)
            first = 3 * lines * turn
            terms = [tail[first + lines * term : first + lines * (term + 1)] for term in range(3)]
            total = terms[0] + terms[1] + terms[2]
            for line in range(lines):
                gain_ref[
                    start + place : start + place + 1, line * width : (line + 1) * width
                ] = total[line : line + 1]


def gain_terms(gain, width):
    first = lax.reduce_precision(gain, 8, 7)
    second = lax.reduce_precision(gain - first, 8, 7)
    third = gain - first - second
    terms = jnp.stack([first, second, third], axis=1).astype(jnp.bfloat16)
    return terms.reshape(-1, width)


def first_kernel(
    arrived_ref,
    upstream_ref,
    own_gain_ref,
    tails_ref,
    key_ref,
    value_ref,
    share_ref,
    other_ref,
    state_ref,
    aux_ref,
    gain_ref,
    packed_ref,
    weight_ref,
    sems,
    *,
    sections
):
    copies = fill(0, key_ref, value_ref, (share_ref, other_ref), weight_ref, sems, 0)
    unpack_gains(own_gain_ref, tails_ref, gain_ref)
    state_ref[sections + 1, :, : upstream_ref.shape[1]] = upstream_ref[...]
    row_count, feature_count = upstream_ref.shape
    head_size = weight_ref.shape[2] // 2
    column_count = feature_count // sections
    pieces = pieces_of(column_count)
    width = column_count // pieces
    block = arrived_ref.shape[0] // sections
    tags = arrived_ref[:block, width:].astype(jnp.float32)
    chosen = choosers(tags, row_count, pieces)
    cuts = []
    for section in range(sections):
        part = arrived_ref[section * block : (section + 1) * block, :width]
        cuts += [contract(chooser, part, 0, 0) for chooser in chosen]
    rows = jnp.concatenate(cuts, axis=1)
    own = contract(chosen[0], tags.astype(jnp.bfloat16), 0, 0)
    document, position = own[:, 2:3], own[:, 3:4]
    lane = iota((1, head_size), 1)
    middle = head_size // 2
    exponent = (lane % middle).astype(jnp.float32) * (2.0 / head_size)
    angles = position * jnp.exp(exponent * -jnp.log(jnp.float32(ROPE_BASE)))
    cosine = jnp.cos(angles)
    sine = jnp.where(lane < middle, -jnp.sin(angles), jnp.sin(angles))
    shape = (row_count, row_count * feature_count // head_size)
    pick = as_float(iota(shape, 1) % row_count == iota(shape, 0))
    document_across = jnp.sum(document * pick, axis=0, keepdims=True)
    position_across = jnp.sum(position * pick, axis=0, keepdims=True)
    allowed = (document == document_across) & (position <= position_across)
    for place, table in enumerate((cosine, sine, as_float(allowed))):
        aux_ref[place * row_count : (place + 1) * row_count] = table
    aux_ref[3 * row_count :] = tags
    for copy in copies:
        copy.wait()
    own = lax.axis_index("pipe")
    tables = (cosine, sine, allowed)
    state_ref[sections, :, :feature_count] = forward_steps(
        rows, own, gain_ref, weight_ref, tables, state_ref, packed_ref
    )


def second_kernel(
    first_ref,
    aux_ref,
    gain_ref,
    key_ref,
    value_ref,
    share_ref,
    other_ref,
    late_share_ref,
    late_other_ref,
    out_ref,
    state_ref,
    weight_ref,
    sems,
    *,
    sections
):
    late_copies = fill(
        1, key_ref, value_ref, (late_share_ref, late_other_ref), weight_ref, sems, sections
    )
    copies = fill(0, key_ref, value_ref, (share_ref, other_ref), weight_ref, sems, 0)
    own = lax.axis_index("pipe")
    _, feature_count, term_width = weight_ref.shape
    row_count = first_ref.shape[1]
    groups = out_ref.shape[1]
    share = feature_count // groups
    cosine, sine, allowed = [
        aux_ref[place * row_count : (place + 1) * row_count] for place in range(3)
    ]
    tables = (cosine, sine, allowed > 0.5)
    late_gain = gain_ref.at[pl.ds(sections, sections)]
    late_weight = weight_ref.at[pl.ds(sections, sections)]
    for copy in late_copies:
        copy.wait()
    forward_steps(
        first_ref[sections, :, :feature_count],
        own,
        late_gain,
        late_weight,
        tables,
        state_ref,
        out_ref,
    )
    upstream = backward_steps(
        first_ref[sections + 1, :, :feature_count],
        own,
        late_gain,
        late_weight,
        tables,
        state_ref,
        out_ref,
        share + term_width,
    )
    for copy in copies:
        copy.wait()
    grads = backward_steps(
        upstream,
        own,
        gain_ref.at[pl.ds(0, sections)],
        weight_ref.at[pl.ds(0, sections)],
        tables,
        first_ref,
        out_ref,
        share,
    ).astype(jnp.bfloat16)
    column_count = feature_count // sections
    pieces = pieces_of(column_count)
    width = column_count // pieces
    chosen = choosers(aux_ref[3 * row_count :, :], row_count, pieces)
    for section in range(sections):
        start = section * column_count
        going = contract(chosen[0], grads[:, start : start + width], 1, 0)
        for piece in range(1, pieces):
            left = start + piece * width
            going += contract(chosen[piece], grads[:, left : left + width], 1, 0)
        going = going.astype(jnp.bfloat16)
        for group in range(groups):
            out_ref[section, group, :, share + 2 * term_width :] = going[
                group * row_count : (group + 1) * row_count
            ]


def last_kernel(
    route_ref, first_ref, late_ref, grad_ref, key_ref, value_ref, *, groups
):
    micro_count = route_ref.shape[0]
    source_rows, column_count = grad_ref.shape
    row_count = source_rows // micro_count
    half = row_count // 2
    share, head_size = key_ref.shape[1:]
    term_width = 2 * head_size
    width = late_ref.shape[1] - share - 2 * term_width
    pieces = column_count // width
    for index, packed in enumerate((first_ref[...], late_ref[:, :share])):
        start = share + index * term_width
        total = contract(packed, late_ref[:, start : start + term_width], 0, 0)
        key_ref[index] = total[:, :head_size]
        value_ref[index] = total[:, head_size:]
    shape = (source_rows, late_ref.shape[0])
    row, source = iota(shape, 1), iota(shape, 0)
    slot = source // half
    target = jnp.full(shape, -1, jnp.int32)
    for micro in range(micro_count):
        for side in range(2):
            target = jnp.where(
                slot == 2 * micro + side, micro * groups + route_ref[micro, side], target
            )
    going = target == row // row_count
    inner, wanted = row % row_count, source % half
    for piece in range(pieces):
        chosen = as_float(going & (inner == piece * half + wanted)).astype(jnp.bfloat16)
        grad_ref[:, piece * width : (piece + 1) * width] = contract(
            chosen, late_ref[:, share + 2 * term_width :], 1, 0
        ).astype(jnp.bfloat16)


def call(kernel, outs, operands, scalars=0, whole=0, scratch=(), vmem_bytes=24 << 20, cost=0):
    spaces = [pltpu.SMEM] * scalars + [pltpu.VMEM] * (len(operands) - scalars - whole)
    spaces += [pl.ANY] * whole
    return pl.pallas_call(
        kernel,
        out_shape=outs,
        in_specs=[pl.BlockSpec(memory_space=space) for space in spaces],
        out_specs=[pl.BlockSpec(memory_space=pltpu.VMEM)] * len(outs),
        scratch_shapes=scratch,
        compiler_params=pltpu.CompilerParams(vmem_limit_bytes=vmem_bytes),
        cost_estimate=pl.CostEstimate(flops=0, bytes_accessed=cost, transcendentals=0),
    )(*operands)


def exchange(blocks):
    return lax.all_to_all(blocks, ("pipe", "dp"), split_axis=0, concat_axis=0, tiled=True)


def swapped(value, axis, mask):
    pairs = [(source, source ^ mask) for source in range(lax.axis_size(axis))]
    return lax.ppermute(value, axis, pairs)


def section_pieces(payload):
    return [swapped(payload, "pipe", mask) for mask in range(1, lax.axis_size("pipe"))]


def plane_pieces(column):
    return [swapped(column, "dp", 2 * mask) for mask in range(1, lax.axis_size("dp") // 2)]


def body(hidden, lengths, route, gain, key_weight, value_weight, cotangent):
    groups = lax.axis_size("dp")
    sections = lax.axis_size("pipe")
    group_index = lax.axis_index("dp")
    section_index = lax.axis_index("pipe")
    micro_count = lengths.shape[0]
    assert micro_count == sections
    source_rows, column_count = hidden.shape
    row_count = source_rows // micro_count
    feature_count = gain.shape[1]
    head_size = key_weight.shape[2]
    assert row_count * feature_count == head_size * head_size
    share = feature_count // groups
    width = column_count // pieces_of(column_count)
    devices = sections * groups

    (outgoing,) = call(
        functools.partial(pack_kernel, groups=groups),
        [jax.ShapeDtypeStruct((devices * row_count, width + LANES), jnp.bfloat16)],
        (lengths, route, hidden),
        scalars=2,
    )
    arrived = exchange(outgoing.reshape(devices, row_count, width + LANES)).reshape(
        devices * row_count, width + LANES
    )
    def own_share(turn):
        parts = [
            lax.dynamic_slice(array, (turn, group_index * share, 0), (1, share, head_size))[0]
            for array in (key_weight, value_weight)
        ]
        return jnp.concatenate(parts, axis=1)

    column = jnp.stack(section_pieces(own_share(0)))
    payload = jnp.concatenate([own_share(1), gain_terms(gain, 2 * head_size)], axis=0)
    upstream = lax.dynamic_slice_in_dim(
        cotangent, section_index * row_count, row_count, 0
    ).astype(jnp.float32)
    column, payload, upstream = lax.optimization_barrier((column, payload, upstream))
    plane = jnp.stack([column] + plane_pieces(column))
    came = section_pieces(payload)
    plane, came, arrived = lax.optimization_barrier((plane, came, arrived))
    first_shares = (plane, swapped(plane, "dp", 1))
    column = jnp.stack([piece[:share] for piece in came])
    tails = jnp.stack([piece[share:] for piece in came])
    planes = [column] + plane_pieces(column)

    def layers_call(kernel, turns, outs, operands, shares, scratch, cost):
        places = turns * sections
        return call(
            functools.partial(kernel, sections=sections),
            outs,
            (*operands, key_weight, value_weight, *shares),
            whole=2 + len(shares),
            scratch=[
                *scratch,
                pltpu.VMEM((places, feature_count, 2 * head_size), jnp.bfloat16),
                pltpu.SemaphoreType.DMA((2, groups + 2)),
            ],
            vmem_bytes=(14 << 20) + 5 * places * feature_count * head_size,
            cost=cost,
        )

    def blocks_shape(columns):
        return jax.ShapeDtypeStruct((sections, groups, row_count, columns), jnp.bfloat16)

    def exchanged(blocks):
        columns = blocks.shape[3]
        got = exchange(blocks.reshape(devices, row_count, columns))
        return got.reshape(devices * row_count, columns)

    line = (row_count, state_width(feature_count, head_size))
    state, aux, gains, packed = layers_call(
        first_kernel,
        1,
        [
            jax.ShapeDtypeStruct((sections + 2, *line), jnp.float32),
            jax.ShapeDtypeStruct(((3 + groups) * row_count, head_size), jnp.float32),
            jax.ShapeDtypeStruct((2 * sections, feature_count), jnp.float32),
            blocks_shape(share),
        ],
        (arrived, upstream, gain, tails),
        first_shares,
        (),
        18 << 20,
    )
    state, packed, planes = lax.optimization_barrier((state, packed, planes))
    packed = exchanged(packed)
    plane = jnp.stack(planes)
    second_shares = (plane, swapped(plane, "dp", 1))
    (late,) = layers_call(
        second_kernel,
        2,
        [blocks_shape(share + 4 * head_size + width)],
        (state, aux, gains),
        (*first_shares, *second_shares),
        (pltpu.VMEM((sections, *line), jnp.float32),),
        48 << 20,
    )
    late, packed = lax.optimization_barrier((late, packed))
    late = exchanged(late)
    grad_shape = jax.ShapeDtypeStruct((2, share, head_size), jnp.float32)
    return tuple(
        call(
            functools.partial(last_kernel, groups=groups),
            [jax.ShapeDtypeStruct((source_rows, column_count), jnp.bfloat16)] + [grad_shape] * 2,
            (route, packed, late),
            scalars=1,
        )
    )


def solution(mesh):
    placed = (
        P("dp", "pipe"),
        P("dp", None),
        P("dp", None),
        P("pipe", None),
        P("pipe", None, None),
        P("pipe", None, None),
        P("dp", None),
    )
    return jax.shard_map(
        body,
        mesh=mesh,
        in_specs=placed,
        out_specs=(P("dp", "pipe"), P("pipe", "dp", None), P("pipe", "dp", None)),
        check_vma=False,
    )
```

```python
import functools

import jax
import jax.numpy as jnp
from jax import lax
from jax.experimental import pallas as pl
from jax.experimental.pallas import tpu as pltpu
from jax.sharding import PartitionSpec as P

ROPE_BASE = 500000.0
EPSILON = 1e-05
NEGATIVE = -1e30
LANES = 128
GAIN_LINES = 8


def iota(shape, dim):
    return lax.broadcasted_iota(jnp.int32, shape, dim)


def as_float(flags):
    return jnp.where(flags, 1.0, 0.0).astype(jnp.float32)


def contract(left, right, left_dim, right_dim):
    return lax.dot_general(
        left, right, (((left_dim,), (right_dim,)), ((), ())), preferred_element_type=jnp.float32
    )


def pieces_of(column_count):
    return 2 if column_count % (2 * LANES) == 0 else 1


def fold(rows, width):
    row_count, columns = rows.shape
    if columns >= width:
        return jnp.concatenate(
            [rows[:, start : start + width] for start in range(0, columns, width)], axis=0
        )
    lines = row_count * columns // width
    return jnp.concatenate(
        [rows[start : start + lines] for start in range(0, row_count, lines)], axis=1
    )


def unfold(lines, row_count, columns):
    width = lines.shape[1]
    if columns >= width:
        return jnp.concatenate(
            [lines[start : start + row_count] for start in range(0, lines.shape[0], row_count)],
            axis=1,
        )
    return jnp.concatenate(
        [lines[:, start : start + columns] for start in range(0, width, columns)], axis=0
    )


def choosers(source, groups, pieces):
    row_count = source.shape[0]
    half = row_count // 2
    shape = (row_count, groups * row_count)
    row, line = iota(shape, 0), iota(shape, 1)
    back = source.astype(jnp.int32) == line // row_count
    return [
        as_float(back & (line % row_count == piece * half + row % half)).astype(jnp.bfloat16)
        for piece in range(pieces)
    ]


def turned(vector, cosine, sine):
    return vector * cosine + pltpu.roll(vector, vector.shape[1] // 2, 1) * sine


def heads_down(rows, head_size):
    count = rows.shape[1] // head_size
    return jnp.concatenate(
        [rows[:, head * head_size : (head + 1) * head_size] for head in range(count)], axis=0
    )


def heads_across(stacked, row_count):
    count = stacked.shape[0] // row_count
    return jnp.concatenate(
        [stacked[head * row_count : (head + 1) * row_count] for head in range(count)], axis=1
    )


def turned_heads(rows, cosine, sine):
    stacked = heads_down(rows, cosine.shape[1])
    repeats = stacked.shape[0] // rows.shape[0]
    return turned(stacked, jnp.tile(cosine, (repeats, 1)), jnp.tile(sine, (repeats, 1)))


def forward_layer(rows, gain_row, weight, cosine, sine, allowed):
    row_count, feature_count = rows.shape
    head_size = cosine.shape[1]
    scale = lax.rsqrt(jnp.sum(rows * rows, axis=1, keepdims=True) / feature_count + EPSILON)
    normed = rows * scale * gain_row
    packed = normed.astype(jnp.bfloat16)
    share = feature_count // len(weight)
    pair = jnp.zeros((row_count, 2 * head_size), jnp.float32)
    for owner, part in enumerate(weight):
        pair += contract(packed[:, owner * share : (owner + 1) * share], part[...], 1, 0)
    queries = turned_heads(normed, cosine, sine).astype(jnp.bfloat16)
    keys = turned(pair[:, :head_size], cosine, sine).astype(jnp.bfloat16)
    values = pair[:, head_size:].astype(jnp.bfloat16)
    scores = contract(keys, queries, 1, 1) * head_size ** (-0.5)
    scores = jnp.where(allowed, scores, NEGATIVE)
    raised = jnp.exp(scores - jnp.max(scores, axis=0, keepdims=True))
    weights = raised / jnp.sum(raised, axis=0, keepdims=True)
    mixed = contract(weights.astype(jnp.bfloat16), values, 0, 0)
    kept = (scale, keys, values, weights)
    return rows + heads_across(mixed, row_count), packed, kept


def backward_layer(upstream, rows, gain_row, weight, cosine, sine, kept):
    scale, keys, values, weights = kept
    row_count, feature_count = rows.shape
    head_size = cosine.shape[1]
    queries = turned_heads(rows * scale * gain_row, cosine, sine).astype(jnp.bfloat16)
    stacked = heads_down(upstream, head_size).astype(jnp.bfloat16)
    d_weights = contract(values, stacked, 1, 1).astype(jnp.bfloat16).astype(jnp.float32)
    d_values = contract(weights.astype(jnp.bfloat16), stacked, 1, 0)
    d_scores = weights * (d_weights - jnp.sum(d_weights * weights, axis=0, keepdims=True))
    d_scores = (d_scores * head_size ** (-0.5)).astype(jnp.bfloat16)
    d_keys = contract(d_scores, queries, 1, 0)
    terms = jnp.concatenate([turned(d_keys, cosine, -sine), d_values], axis=1)
    terms = terms.astype(jnp.bfloat16)
    d_queries = contract(d_scores, keys, 0, 0)
    repeats = stacked.shape[0] // row_count
    d_queries = turned(d_queries, jnp.tile(cosine, (repeats, 1)), jnp.tile(-sine, (repeats, 1)))
    d_packed = jnp.concatenate([contract(terms, part[...], 1, 1) for part in weight], axis=1)
    d_normed = d_packed + heads_across(d_queries, row_count)
    scaled = d_normed * gain_row
    inner = jnp.sum(scaled * rows, axis=1, keepdims=True) / feature_count
    return upstream + scale * scaled - rows * (scale * scale * scale * inner), terms


def state_width(feature_count, head_size):
    return feature_count + 4 * head_size


def save_layer(index, rows, kept, state_ref):
    scale, keys, values, weights = kept
    feature_count, head_size = rows.shape[1], keys.shape[1]
    state_ref[index, :, :feature_count] = rows
    parts = (weights, keys, values, jnp.broadcast_to(scale, keys.shape))
    for place, part in enumerate(parts):
        start = feature_count + place * head_size
        state_ref[index, :, start : start + head_size] = part.astype(jnp.float32)


def load_layer(index, state_ref, feature_count):
    head_size = (state_ref.shape[2] - feature_count) // 4
    parts = []
    for place in range(4):
        start = feature_count + place * head_size
        parts.append(state_ref[index, :, start : start + head_size])
    weights, keys, values, scale = parts
    kept = (scale[:, 0:1], keys.astype(jnp.bfloat16), values.astype(jnp.bfloat16), weights)
    return state_ref[index, :, :feature_count], kept


def repeat_steps(count, step, carry):
    if count <= 8:
        for index in range(count):
            carry = step(index, carry)
        return carry
    return lax.fori_loop(0, count, step, carry)


def layer_inputs(index, gain_ref, weight_ref, sections):
    place = lax.bitwise_xor(lax.axis_index("pipe"), index)
    share = weight_ref.shape[1] // sections
    rows = pl.ds(pl.multiple_of(place * share, share), share)
    weight = [weight_ref.at[owner, rows] for owner in range(weight_ref.shape[0])]
    return gain_ref[pl.ds(place, 1), :], weight


def forward_steps(rows, gain_ref, weight_ref, tables, state_ref, packed_ref):
    cosine, sine, allowed = tables
    sections, groups = packed_ref.shape[:2]
    share = weight_ref.shape[1] // sections

    def step(index, rows):
        gain_row, weight = layer_inputs(index, gain_ref, weight_ref, sections)
        after, packed, kept = forward_layer(rows, gain_row, weight, cosine, sine, allowed)
        for group in range(groups):
            packed_ref[index, group, :, :share] = packed[:, group * share : (group + 1) * share]
        save_layer(index, rows, kept, state_ref)
        return after

    return repeat_steps(sections, step, rows)


def backward_steps(upstream, gain_ref, weight_ref, tables, state_ref, terms_ref, start):
    cosine, sine, _ = tables
    sections, groups = terms_ref.shape[:2]
    width = weight_ref.shape[2]

    def step(back, upstream):
        index = sections - 1 - back
        gain_row, weight = layer_inputs(index, gain_ref, weight_ref, sections)
        rows, kept = load_layer(index, state_ref, upstream.shape[1])
        before, terms = backward_layer(upstream, rows, gain_row, weight, cosine, sine, kept)
        for group in range(groups):
            terms_ref[index, group, :, start : start + width] = terms
        return before

    return repeat_steps(sections, step, upstream)


def fill(turn, key_ref, value_ref, shares, weight_ref, sems):
    groups, share, head_size = key_ref.shape[1:]
    moved = weight_ref.shape[1] - share
    group = lax.axis_index("dp")
    copies = [
        (key_ref.at[turn], weight_ref.at[:, :share, :head_size]),
        (value_ref.at[turn], weight_ref.at[:, :share, head_size:]),
    ]
    for core, ref in enumerate(shares):
        for chip in range(groups // 2):
            owner = lax.bitwise_xor(group, 2 * chip + core)
            copies.append(
                (ref.at[chip, pl.ds(0, moved)], weight_ref.at[owner, pl.ds(share, moved)])
            )
    copies = [
        pltpu.make_async_copy(*pair, sems.at[turn, index]) for index, pair in enumerate(copies)
    ]
    for copy in copies:
        copy.start()
    return copies


def first_kernel(
    upstream_ref,
    key_ref,
    value_ref,
    share_ref,
    other_ref,
    state_ref,
    packed_ref,
    lines_ref,
    rows_ref,
    gains_ref,
    gain_ref,
    line_sems,
    weight_ref,
    sems,
    *,
    doc_count
):
    sections = packed_ref.shape[0]
    groups, share, head_size = key_ref.shape[1:]
    row_count, feature_count = upstream_ref.shape
    column_count = feature_count // sections
    chips, line_count, width = lines_ref.shape[1:]
    used = share_ref.shape[1] - line_count
    section, group = lax.axis_index("pipe"), lax.axis_index("dp")
    shares = (share_ref, other_ref)
    line_copies = [
        pltpu.make_async_copy(
            ref.at[:, pl.ds(used, line_count)], lines_ref.at[core], line_sems.at[core]
        )
        for core, ref in enumerate(shares)
    ]
    for copy in line_copies:
        copy.start()
    copies = fill(0, key_ref, value_ref, shares, weight_ref, sems)
    state_ref[sections + 1, :, :feature_count] = upstream_ref[...]
    for copy in line_copies:
        copy.wait()

    row = iota((row_count, 1), 0)
    offset = row.astype(jnp.float32)
    document = jnp.zeros((row_count, 1), jnp.float32)
    position = jnp.zeros((row_count, 1), jnp.float32)
    source = jnp.zeros((row_count, 1), jnp.float32)
    parts = [jnp.zeros((row_count, column_count), jnp.float32) for _ in range(sections)]
    folded = row_count * column_count // width
    tail = folded + GAIN_LINES
    for core in range(2):
        for chip in range(chips):
            lines = lines_ref[core, chip].astype(jnp.float32)
            tags = lines[sections * tail :]
            tags = jnp.sum(
                jnp.where(iota(tags.shape, 0) == section, tags, 0.0), axis=0, keepdims=True
            )
            target = jnp.where(
                row < row_count // 2,
                tags[:, doc_count : doc_count + 1],
                tags[:, doc_count + 1 : doc_count + 2],
            )
            came = as_float(target.astype(jnp.int32) == group)
            end = jnp.zeros((1, 1), jnp.float32)
            number = jnp.zeros((row_count, 1), jnp.float32)
            opening = jnp.zeros((row_count, 1), jnp.float32)
            for doc in range(doc_count - 1):
                end = end + tags[:, doc : doc + 1]
                passed = offset >= end
                number = number + as_float(passed)
                opening = jnp.where(passed, end, opening)
            owner = lax.bitwise_xor(group, 2 * chip + core)
            document += came * number
            position += came * (offset - opening)
            source += came * owner.astype(jnp.float32)
            gain_rows = []
            for mask in range(sections):
                piece = lines[mask * tail : mask * tail + folded]
                parts[mask] += came * unfold(piece, row_count, column_count)
                terms = lines[mask * tail + folded : (mask + 1) * tail, :share]
                gain_rows += [
                    terms[3 * turn : 3 * turn + 1]
                    + terms[3 * turn + 1 : 3 * turn + 2]
                    + terms[3 * turn + 2 : 3 * turn + 3]
                    for turn in range(2)
                ]
            gains_ref[owner] = jnp.concatenate(gain_rows[0::2] + gain_rows[1::2], axis=0)
    for owner in range(groups):
        gain_ref[:, owner * share : (owner + 1) * share] = gains_ref[owner]
    for start in range(0, 2 * sections, row_count):
        state_ref[sections + 2 + start // row_count, :, :feature_count] = gain_ref[
            start : start + row_count
        ]
    for mask in range(sections):
        rows_ref[lax.bitwise_xor(section, mask)] = parts[mask]
    rows = jnp.concatenate([rows_ref[index] for index in range(sections)], axis=1)

    lane = iota((1, head_size), 1)
    middle = head_size // 2
    exponent = (lane % middle).astype(jnp.float32) * (2.0 / head_size)
    angles = position * jnp.exp(exponent * -jnp.log(jnp.float32(ROPE_BASE)))
    cosine = jnp.cos(angles)
    sine = jnp.where(lane < middle, -jnp.sin(angles), jnp.sin(angles))
    shape = (row_count, row_count * feature_count // head_size)
    pick = as_float(iota(shape, 1) % row_count == iota(shape, 0))
    document_across = jnp.sum(document * pick, axis=0, keepdims=True)
    position_across = jnp.sum(position * pick, axis=0, keepdims=True)
    allowed = (document == document_across) & (position <= position_across)
    kept = (cosine, sine, as_float(allowed), jnp.broadcast_to(source, cosine.shape))
    for place, table in enumerate(kept):
        start = feature_count + place * head_size
        state_ref[sections, :, start : start + head_size] = table
    tables = (cosine, sine, allowed)
    for copy in copies:
        copy.wait()
    state_ref[sections, :, :feature_count] = forward_steps(
        rows, gain_ref.at[pl.ds(0, sections)], weight_ref, tables, state_ref, packed_ref
    )


def second_kernel(
    first_ref,
    key_ref,
    value_ref,
    share_ref,
    other_ref,
    late_share_ref,
    late_other_ref,
    out_ref,
    state_ref,
    gain_ref,
    late_weight_ref,
    weight_ref,
    sems
):
    sections, groups, row_count, _ = out_ref.shape
    share, head_size = key_ref.shape[2:]
    feature_count, term_width = groups * share, 2 * head_size
    late_shares = (late_share_ref, late_other_ref)
    late_copies = fill(1, key_ref, value_ref, late_shares, late_weight_ref, sems)
    copies = fill(0, key_ref, value_ref, (share_ref, other_ref), weight_ref, sems)
    kept = []
    for place in range(4):
        start = feature_count + place * head_size
        kept.append(first_ref[sections, :, start : start + head_size])
    cosine, sine, allowed, source = kept
    tables = (cosine, sine, allowed > 0.5)
    for start in range(0, 2 * sections, row_count):
        gain_ref[start : start + row_count] = first_ref[
            sections + 2 + start // row_count, :, :feature_count
        ]
    late_gain = gain_ref.at[pl.ds(sections, sections)]
    for copy in late_copies:
        copy.wait()
    forward_steps(
        first_ref[sections, :, :feature_count],
        late_gain,
        late_weight_ref,
        tables,
        state_ref,
        out_ref,
    )
    upstream = backward_steps(
        first_ref[sections + 1, :, :feature_count],
        late_gain,
        late_weight_ref,
        tables,
        state_ref,
        out_ref,
        share + term_width,
    )
    for copy in copies:
        copy.wait()
    grads = backward_steps(
        upstream,
        gain_ref.at[pl.ds(0, sections)],
        weight_ref,
        tables,
        first_ref,
        out_ref,
        share,
    ).astype(jnp.bfloat16)
    column_count = feature_count // sections
    pieces = pieces_of(column_count)
    width = column_count // pieces
    chosen = choosers(source[:, 0:1], groups, pieces)
    for section in range(sections):
        start = section * column_count
        going = contract(chosen[0], grads[:, start : start + width], 0, 0)
        for piece in range(1, pieces):
            left = start + piece * width
            going += contract(chosen[piece], grads[:, left : left + width], 0, 0)
        going = going.astype(jnp.bfloat16)
        for group in range(groups):
            out_ref[section, group, :, share + 2 * term_width :] = going[
                group * row_count : (group + 1) * row_count
            ]


def last_kernel(
    route_ref, first_ref, late_ref, grad_ref, key_ref, value_ref, *, groups
):
    micro_count = route_ref.shape[0]
    source_rows, column_count = grad_ref.shape
    row_count = source_rows // micro_count
    half = row_count // 2
    share, head_size = key_ref.shape[1:]
    term_width = 2 * head_size
    width = late_ref.shape[1] - share - 2 * term_width
    pieces = column_count // width
    for index, packed in enumerate((first_ref[...], late_ref[:, :share])):
        start = share + index * term_width
        total = contract(packed, late_ref[:, start : start + term_width], 0, 0)
        key_ref[index] = total[:, :head_size]
        value_ref[index] = total[:, head_size:]
    shape = (source_rows, late_ref.shape[0])
    row, source = iota(shape, 1), iota(shape, 0)
    slot = source // half
    target = jnp.full(shape, -1, jnp.int32)
    for micro in range(micro_count):
        for side in range(2):
            target = jnp.where(
                slot == 2 * micro + side, micro * groups + route_ref[micro, side], target
            )
    going = target == row // row_count
    inner, wanted = row % row_count, source % half
    for piece in range(pieces):
        chosen = as_float(going & (inner == piece * half + wanted)).astype(jnp.bfloat16)
        grad_ref[:, piece * width : (piece + 1) * width] = contract(
            chosen, late_ref[:, share + 2 * term_width :], 1, 0
        ).astype(jnp.bfloat16)


def call(kernel, outs, operands, scalars=0, whole=0, scratch=(), vmem_bytes=0, cost=0):
    spaces = [pltpu.SMEM] * scalars + [pltpu.VMEM] * (len(operands) - scalars - whole)
    spaces += [pl.ANY] * whole
    return pl.pallas_call(
        kernel,
        out_shape=outs,
        in_specs=[pl.BlockSpec(memory_space=space) for space in spaces],
        out_specs=[pl.BlockSpec(memory_space=pltpu.VMEM)] * len(outs),
        scratch_shapes=scratch,
        compiler_params=pltpu.CompilerParams(vmem_limit_bytes=vmem_bytes),
        cost_estimate=pl.CostEstimate(flops=0, bytes_accessed=cost, transcendentals=0),
    )(*operands)


def exchange(blocks):
    return lax.all_to_all(blocks, ("pipe", "dp"), split_axis=0, concat_axis=0, tiled=True)


def swapped(value, axis, mask):
    pairs = [(source, source ^ mask) for source in range(lax.axis_size(axis))]
    return lax.ppermute(value, axis, pairs)


def relayed(payload, sections):
    pieces = [payload]
    for mask in range(1, sections):
        low = mask & -mask
        pieces.append(swapped(pieces[mask - low], "pipe", low))
    return pieces[1:]


def body(hidden, lengths, route, gain, key_weight, value_weight, cotangent):
    groups = lax.axis_size("dp")
    sections = lax.axis_size("pipe")
    group_index = lax.axis_index("dp")
    section_index = lax.axis_index("pipe")
    micro_count = lengths.shape[0]
    assert micro_count == sections
    source_rows, column_count = hidden.shape
    row_count = source_rows // micro_count
    feature_count = gain.shape[1]
    head_size = key_weight.shape[2]
    assert row_count * feature_count == head_size * head_size
    share = feature_count // groups
    width = column_count // pieces_of(column_count)
    devices = sections * groups

    line_width = 2 * head_size

    def own_share(turn):
        parts = [
            lax.dynamic_slice(array, (turn, group_index * share, 0), (1, share, head_size))[0]
            for array in (key_weight, value_weight)
        ]
        return jnp.concatenate(parts, axis=1)

    def own_rows(mask):
        start = lax.bitwise_xor(section_index, mask) * row_count
        rows = lax.dynamic_slice(hidden, (start, 0), (row_count, column_count))
        return fold(rows, line_width)

    slice_ = lax.dynamic_slice(gain, (0, group_index * share), (2, share))
    high = lax.reduce_precision(slice_, 8, 7)
    middle = lax.reduce_precision(slice_ - high, 8, 7)
    terms = jnp.stack([high, middle, slice_ - high - middle], axis=1).reshape(6, share)
    terms = jnp.pad(
        terms.astype(jnp.bfloat16), ((0, GAIN_LINES - 6), (0, line_width - share))
    )

    first = own_share(0)
    came = [
        swapped(jnp.concatenate([first, own_rows(mask), terms], axis=0), "pipe", mask)
        for mask in range(1, sections)
    ]
    tags = jnp.concatenate([lengths, route], axis=1).astype(jnp.bfloat16)
    tags = jnp.pad(tags, ((0, -micro_count % 16), (0, line_width - tags.shape[1])))
    upstream = lax.dynamic_slice_in_dim(
        cotangent, section_index * row_count, row_count, 0
    ).astype(jnp.float32)
    tags, own_tail, upstream = lax.optimization_barrier(
        (tags, jnp.concatenate([own_rows(0), terms], axis=0), upstream)
    )
    column = jnp.concatenate(
        [piece[:share] for piece in came]
        + [own_tail]
        + [piece[share:] for piece in came]
        + [tags],
        axis=0,
    )
    column, second = lax.optimization_barrier((column, own_share(1)))
    chips = range(1, groups // 2)
    plane = jnp.stack([column] + [swapped(column, "dp", 2 * chip) for chip in chips])
    came = relayed(second, sections)
    plane, came = lax.optimization_barrier((plane, came))
    first_shares = (plane, swapped(plane, "dp", 1))
    column = jnp.concatenate(came, axis=0)
    planes = [column] + [swapped(column, "dp", 2 * chip) for chip in chips]

    key_parts = key_weight.reshape(2, groups, share, head_size)
    value_parts = value_weight.reshape(2, groups, share, head_size)

    def layers_call(kernel, turns, outs, operands, shares, scratch, cost, columns):
        weight = pltpu.VMEM((groups, sections * share, line_width), jnp.bfloat16)
        return call(
            kernel,
            outs,
            (*operands, key_parts, value_parts, *shares),
            whole=2 + len(shares),
            scratch=[
                *scratch,
                *[weight] * turns,
                pltpu.SemaphoreType.DMA((2, groups + 2)),
            ],
            vmem_bytes=(6 << 20)
            + 2 * turns * sections * feature_count * line_width
            + 4 * devices * row_count * columns,
            cost=cost,
        )

    def blocks_shape(columns):
        return jax.ShapeDtypeStruct((sections, groups, row_count, columns), jnp.bfloat16)

    def exchanged(blocks):
        columns = blocks.shape[3]
        got = exchange(blocks.reshape(devices, row_count, columns))
        return got.reshape(devices * row_count, columns)

    line = (row_count, state_width(feature_count, head_size))
    line_count = plane.shape[1] - (sections - 1) * share
    gain_scratch = pltpu.VMEM((2 * sections, feature_count), jnp.float32)
    state, packed = layers_call(
        functools.partial(first_kernel, doc_count=lengths.shape[1]),
        1,
        [
            jax.ShapeDtypeStruct(
                (sections + 2 + 2 * sections // row_count, *line), jnp.float32
            ),
            blocks_shape(share),
        ],
        (upstream,),
        first_shares,
        (
            pltpu.VMEM((2, groups // 2, line_count, line_width), jnp.bfloat16),
            pltpu.VMEM((sections, row_count, column_count), jnp.float32),
            pltpu.VMEM((groups, 2 * sections, share), jnp.float32),
            gain_scratch,
            pltpu.SemaphoreType.DMA((2,)),
        ),
        18 << 20,
        2 * LANES,
    )
    packed = exchanged(packed)
    state, packed, planes = lax.optimization_barrier((state, packed, planes))
    plane = jnp.stack(planes)
    second_shares = (plane, swapped(plane, "dp", 1))
    columns = share + 4 * head_size + width
    (late,) = layers_call(
        second_kernel,
        2,
        [blocks_shape(columns)],
        (state,),
        (*first_shares, *second_shares),
        (pltpu.VMEM((sections, *line), jnp.float32), gain_scratch),
        48 << 20,
        columns,
    )
    late, packed = lax.optimization_barrier((late, packed))
    late = exchanged(late)
    grad_shape = jax.ShapeDtypeStruct((2, share, head_size), jnp.float32)
    return tuple(
        call(
            functools.partial(last_kernel, groups=groups),
            [jax.ShapeDtypeStruct((source_rows, column_count), jnp.bfloat16)] + [grad_shape] * 2,
            (route, packed, late),
            scalars=1,
            vmem_bytes=(4 << 20) + 10000 * devices * row_count,
        )
    )


def solution(mesh):
    placed = (
        P("dp", "pipe"),
        P("dp", None),
        P("dp", None),
        P("pipe", None),
        P("pipe", None, None),
        P("pipe", None, None),
        P("dp", None),
    )
    return jax.shard_map(
        body,
        mesh=mesh,
        in_specs=placed,
        out_specs=(P("dp", "pipe"), P("pipe", "dp", None), P("pipe", "dp", None)),
        check_vma=False,
    )
```

```python
import functools

import jax
import jax.numpy as jnp
from jax import lax
from jax.experimental import pallas as pl
from jax.experimental.pallas import tpu as pltpu
from jax.sharding import PartitionSpec as P

ROPE_BASE = 500000.0
EPSILON = 1e-05
NEGATIVE = -1e30
LANES = 128
GAIN_LINES = 8


def iota(shape, dim):
    return lax.broadcasted_iota(jnp.int32, shape, dim)


def as_float(flags):
    return jnp.where(flags, 1.0, 0.0).astype(jnp.float32)


def contract(left, right, left_dim, right_dim):
    return lax.dot_general(
        left, right, (((left_dim,), (right_dim,)), ((), ())), preferred_element_type=jnp.float32
    )


def pieces_of(column_count):
    return 2 if column_count % (2 * LANES) == 0 else 1


def fold(rows, width):
    row_count, columns = rows.shape
    if columns >= width:
        return jnp.concatenate(
            [rows[:, start : start + width] for start in range(0, columns, width)], axis=0
        )
    lines = row_count * columns // width
    return jnp.concatenate(
        [rows[start : start + lines] for start in range(0, row_count, lines)], axis=1
    )


def unfold(lines, row_count, columns):
    width = lines.shape[1]
    if columns >= width:
        return jnp.concatenate(
            [lines[start : start + row_count] for start in range(0, lines.shape[0], row_count)],
            axis=1,
        )
    return jnp.concatenate(
        [lines[:, start : start + columns] for start in range(0, width, columns)], axis=0
    )


def choosers(source, groups, pieces):
    row_count = source.shape[0]
    half = row_count // 2
    shape = (row_count, groups * row_count)
    row, line = iota(shape, 0), iota(shape, 1)
    back = source.astype(jnp.int32) == line // row_count
    return [
        as_float(back & (line % row_count == piece * half + row % half)).astype(jnp.bfloat16)
        for piece in range(pieces)
    ]


def turned(vector, cosine, sine):
    return vector * cosine + pltpu.roll(vector, vector.shape[1] // 2, 1) * sine


def heads_down(rows, head_size):
    count = rows.shape[1] // head_size
    return jnp.concatenate(
        [rows[:, head * head_size : (head + 1) * head_size] for head in range(count)], axis=0
    )


def heads_across(stacked, row_count):
    count = stacked.shape[0] // row_count
    return jnp.concatenate(
        [stacked[head * row_count : (head + 1) * row_count] for head in range(count)], axis=1
    )


def turned_heads(rows, cosine, sine):
    stacked = heads_down(rows, cosine.shape[1])
    repeats = stacked.shape[0] // rows.shape[0]
    return turned(stacked, jnp.tile(cosine, (repeats, 1)), jnp.tile(sine, (repeats, 1)))


def forward_layer(rows, gain_row, weight, cosine, sine, allowed):
    row_count, feature_count = rows.shape
    head_size = cosine.shape[1]
    scale = lax.rsqrt(jnp.sum(rows * rows, axis=1, keepdims=True) / feature_count + EPSILON)
    normed = rows * scale * gain_row
    packed = normed.astype(jnp.bfloat16)
    pair = contract(packed, weight, 1, 0)
    queries = turned_heads(normed, cosine, sine).astype(jnp.bfloat16)
    keys = turned(pair[:, :head_size], cosine, sine).astype(jnp.bfloat16)
    values = pair[:, head_size:].astype(jnp.bfloat16)
    scores = contract(keys, queries, 1, 1) * head_size ** (-0.5)
    scores = jnp.where(allowed, scores, NEGATIVE)
    raised = jnp.exp(scores - jnp.max(scores, axis=0, keepdims=True))
    weights = raised / jnp.sum(raised, axis=0, keepdims=True)
    mixed = contract(weights.astype(jnp.bfloat16), values, 0, 0)
    kept = (scale, keys, values, weights)
    return rows + heads_across(mixed, row_count), packed, kept


def backward_layer(upstream, rows, gain_row, weight, cosine, sine, kept):
    scale, keys, values, weights = kept
    row_count, feature_count = rows.shape
    head_size = cosine.shape[1]
    queries = turned_heads(rows * scale * gain_row, cosine, sine).astype(jnp.bfloat16)
    stacked = heads_down(upstream, head_size).astype(jnp.bfloat16)
    d_weights = contract(values, stacked, 1, 1).astype(jnp.bfloat16).astype(jnp.float32)
    d_values = contract(weights.astype(jnp.bfloat16), stacked, 1, 0)
    d_scores = weights * (d_weights - jnp.sum(d_weights * weights, axis=0, keepdims=True))
    d_scores = (d_scores * head_size ** (-0.5)).astype(jnp.bfloat16)
    d_keys = contract(d_scores, queries, 1, 0)
    terms = jnp.concatenate([turned(d_keys, cosine, -sine), d_values], axis=1)
    terms = terms.astype(jnp.bfloat16)
    d_queries = contract(d_scores, keys, 0, 0)
    repeats = stacked.shape[0] // row_count
    d_queries = turned(d_queries, jnp.tile(cosine, (repeats, 1)), jnp.tile(-sine, (repeats, 1)))
    d_normed = contract(terms, weight, 1, 1) + heads_across(d_queries, row_count)
    scaled = d_normed * gain_row
    inner = jnp.sum(scaled * rows, axis=1, keepdims=True) / feature_count
    return upstream + scale * scaled - rows * (scale * scale * scale * inner), terms


def state_width(feature_count, head_size):
    return feature_count + 4 * head_size


def save_layer(index, rows, kept, state_ref):
    scale, keys, values, weights = kept
    feature_count, head_size = rows.shape[1], keys.shape[1]
    state_ref[index, :, :feature_count] = rows
    parts = (weights, keys, values, jnp.broadcast_to(scale, keys.shape))
    for place, part in enumerate(parts):
        start = feature_count + place * head_size
        state_ref[index, :, start : start + head_size] = part.astype(jnp.float32)


def load_layer(index, state_ref, feature_count):
    head_size = (state_ref.shape[2] - feature_count) // 4
    parts = []
    for place in range(4):
        start = feature_count + place * head_size
        parts.append(state_ref[index, :, start : start + head_size])
    weights, keys, values, scale = parts
    kept = (scale[:, 0:1], keys.astype(jnp.bfloat16), values.astype(jnp.bfloat16), weights)
    return state_ref[index, :, :feature_count], kept


def repeat_steps(count, step, carry):
    if count <= 8:
        for index in range(count):
            carry = step(index, carry)
        return carry
    return lax.fori_loop(0, count, step, carry)


def layer_inputs(index, gain_ref, weight_ref, sections):
    place = lax.bitwise_xor(lax.axis_index("pipe"), index)
    groups = weight_ref.shape[0]
    share = weight_ref.shape[1] // sections
    rows = pl.ds(pl.multiple_of(place * share, share), share)
    weight = []
    for owner in range(groups):
        mask = lax.bitwise_xor(lax.axis_index("dp"), owner)
        line = lax.rem(mask, 2) * (groups // 2) + lax.div(mask, 2)
        weight.append(weight_ref[jnp.where(place == 0, owner, line), rows, :])
    return gain_ref[pl.ds(place, 1), :], jnp.concatenate(weight, axis=0)


def forward_steps(rows, gain_ref, weight_ref, tables, state_ref, packed_ref):
    cosine, sine, allowed = tables
    sections, groups = packed_ref.shape[:2]
    share = weight_ref.shape[1] // sections

    def step(index, rows):
        gain_row, weight = layer_inputs(index, gain_ref, weight_ref, sections)
        after, packed, kept = forward_layer(rows, gain_row, weight, cosine, sine, allowed)
        for group in range(groups):
            packed_ref[index, group, :, :share] = packed[:, group * share : (group + 1) * share]
        save_layer(index, rows, kept, state_ref)
        return after

    return repeat_steps(sections, step, rows)


def backward_steps(upstream, gain_ref, weight_ref, tables, state_ref, terms_ref, start):
    cosine, sine, _ = tables
    sections, groups = terms_ref.shape[:2]
    width = weight_ref.shape[2]

    def step(back, upstream):
        index = sections - 1 - back
        gain_row, weight = layer_inputs(index, gain_ref, weight_ref, sections)
        rows, kept = load_layer(index, state_ref, upstream.shape[1])
        before, terms = backward_layer(upstream, rows, gain_row, weight, cosine, sine, kept)
        for group in range(groups):
            terms_ref[index, group, :, start : start + width] = terms
        return before

    return repeat_steps(sections, step, upstream)


def fill(turn, key_ref, value_ref, shares, weight_ref, sems):
    groups, share, head_size = key_ref.shape[1:]
    moved = weight_ref.shape[1] - share
    copies = [
        (key_ref.at[turn], weight_ref.at[:, :share, :head_size]),
        (value_ref.at[turn], weight_ref.at[:, :share, head_size:]),
    ]
    for core, ref in enumerate(shares):
        lines = pl.ds(core * (groups // 2), groups // 2)
        copies.append((ref.at[:, pl.ds(0, moved)], weight_ref.at[lines, pl.ds(share, moved)]))
    copies = [
        pltpu.make_async_copy(*pair, sems.at[turn, index]) for index, pair in enumerate(copies)
    ]
    for copy in copies:
        copy.start()
    return copies


def first_kernel(
    upstream_ref,
    key_ref,
    value_ref,
    share_ref,
    other_ref,
    state_out,
    packed_ref,
    state_ref,
    lines_ref,
    rows_ref,
    gains_ref,
    gain_ref,
    line_sems,
    weight_ref,
    sems,
    *,
    doc_count
):
    sections = packed_ref.shape[0]
    groups, share, head_size = key_ref.shape[1:]
    row_count, feature_count = upstream_ref.shape
    column_count = feature_count // sections
    chips, line_count, width = lines_ref.shape[1:]
    used = share_ref.shape[1] - line_count
    section, group = lax.axis_index("pipe"), lax.axis_index("dp")
    shares = (share_ref, other_ref)
    line_copies = [
        pltpu.make_async_copy(
            ref.at[:, pl.ds(used, line_count)], lines_ref.at[core], line_sems.at[core]
        )
        for core, ref in enumerate(shares)
    ]
    for copy in line_copies:
        copy.start()
    copies = fill(0, key_ref, value_ref, shares, weight_ref, sems)
    state_ref[sections + 1, :, :feature_count] = upstream_ref[...]
    for copy in line_copies:
        copy.wait()

    row = iota((row_count, 1), 0)
    offset = row.astype(jnp.float32)
    document = jnp.zeros((row_count, 1), jnp.float32)
    position = jnp.zeros((row_count, 1), jnp.float32)
    source = jnp.zeros((row_count, 1), jnp.float32)
    parts = [jnp.zeros((row_count, column_count), jnp.float32) for _ in range(sections)]
    folded = row_count * column_count // width
    tail = folded + GAIN_LINES
    for core in range(2):
        for chip in range(chips):
            lines = lines_ref[core, chip].astype(jnp.float32)
            tags = lines[sections * tail :]
            tags = jnp.sum(
                jnp.where(iota(tags.shape, 0) == section, tags, 0.0), axis=0, keepdims=True
            )
            target = jnp.where(
                row < row_count // 2,
                tags[:, doc_count : doc_count + 1],
                tags[:, doc_count + 1 : doc_count + 2],
            )
            came = as_float(target.astype(jnp.int32) == group)
            end = jnp.zeros((1, 1), jnp.float32)
            number = jnp.zeros((row_count, 1), jnp.float32)
            opening = jnp.zeros((row_count, 1), jnp.float32)
            for doc in range(doc_count - 1):
                end = end + tags[:, doc : doc + 1]
                passed = offset >= end
                number = number + as_float(passed)
                opening = jnp.where(passed, end, opening)
            owner = lax.bitwise_xor(group, 2 * chip + core)
            document += came * number
            position += came * (offset - opening)
            source += came * owner.astype(jnp.float32)
            gain_rows = []
            for mask in range(sections):
                piece = lines[mask * tail : mask * tail + folded]
                parts[mask] += came * unfold(piece, row_count, column_count)
                terms = lines[mask * tail + folded : (mask + 1) * tail, :share]
                gain_rows += [
                    terms[3 * turn : 3 * turn + 1]
                    + terms[3 * turn + 1 : 3 * turn + 2]
                    + terms[3 * turn + 2 : 3 * turn + 3]
                    for turn in range(2)
                ]
            gains_ref[owner] = jnp.concatenate(gain_rows[0::2] + gain_rows[1::2], axis=0)
    for owner in range(groups):
        gain_ref[:, owner * share : (owner + 1) * share] = gains_ref[owner]
    for start in range(0, 2 * sections, row_count):
        state_ref[sections + 2 + start // row_count, :, :feature_count] = gain_ref[
            start : start + row_count
        ]
    for mask in range(sections):
        rows_ref[lax.bitwise_xor(section, mask)] = parts[mask]
    rows = jnp.concatenate([rows_ref[index] for index in range(sections)], axis=1)

    lane = iota((1, head_size), 1)
    middle = head_size // 2
    exponent = (lane % middle).astype(jnp.float32) * (2.0 / head_size)
    angles = position * jnp.exp(exponent * -jnp.log(jnp.float32(ROPE_BASE)))
    cosine = jnp.cos(angles)
    sine = jnp.where(lane < middle, -jnp.sin(angles), jnp.sin(angles))
    shape = (row_count, row_count * feature_count // head_size)
    pick = as_float(iota(shape, 1) % row_count == iota(shape, 0))
    document_across = jnp.sum(document * pick, axis=0, keepdims=True)
    position_across = jnp.sum(position * pick, axis=0, keepdims=True)
    allowed = (document == document_across) & (position <= position_across)
    kept = (cosine, sine, as_float(allowed), jnp.broadcast_to(source, cosine.shape))
    for place, table in enumerate(kept):
        start = feature_count + place * head_size
        state_ref[sections, :, start : start + head_size] = table
    tables = (cosine, sine, allowed)
    for copy in copies:
        copy.wait()
    state_ref[sections, :, :feature_count] = forward_steps(
        rows, gain_ref.at[pl.ds(0, sections)], weight_ref, tables, state_ref, packed_ref
    )
    state_copy = pltpu.make_async_copy(state_ref, state_out, line_sems.at[2])
    state_copy.start()
    state_copy.wait()


def second_kernel(
    state_in,
    key_ref,
    value_ref,
    share_ref,
    other_ref,
    late_share_ref,
    late_other_ref,
    out_ref,
    first_ref,
    state_ref,
    gain_ref,
    state_sem,
    late_weight_ref,
    weight_ref,
    sems
):
    state_copy = pltpu.make_async_copy(state_in, first_ref, state_sem.at[0])
    state_copy.start()
    sections, groups, row_count, _ = out_ref.shape
    share, head_size = key_ref.shape[2:]
    feature_count, term_width = groups * share, 2 * head_size
    late_shares = (late_share_ref, late_other_ref)
    late_copies = fill(1, key_ref, value_ref, late_shares, late_weight_ref, sems)
    state_copy.wait()
    kept = []
    for place in range(4):
        start = feature_count + place * head_size
        kept.append(first_ref[sections, :, start : start + head_size])
    cosine, sine, allowed, source = kept
    tables = (cosine, sine, allowed > 0.5)
    for start in range(0, 2 * sections, row_count):
        gain_ref[start : start + row_count] = first_ref[
            sections + 2 + start // row_count, :, :feature_count
        ]
    late_gain = gain_ref.at[pl.ds(sections, sections)]
    for copy in late_copies:
        copy.wait()
    copies = fill(0, key_ref, value_ref, (share_ref, other_ref), weight_ref, sems)
    forward_steps(
        first_ref[sections, :, :feature_count],
        late_gain,
        late_weight_ref,
        tables,
        state_ref,
        out_ref,
    )
    upstream = backward_steps(
        first_ref[sections + 1, :, :feature_count],
        late_gain,
        late_weight_ref,
        tables,
        state_ref,
        out_ref,
        share + term_width,
    )
    for copy in copies:
        copy.wait()
    grads = backward_steps(
        upstream,
        gain_ref.at[pl.ds(0, sections)],
        weight_ref,
        tables,
        first_ref,
        out_ref,
        share,
    ).astype(jnp.bfloat16)
    column_count = feature_count // sections
    pieces = pieces_of(column_count)
    width = column_count // pieces
    chosen = choosers(source[:, 0:1], groups, pieces)
    for section in range(sections):
        start = section * column_count
        going = contract(chosen[0], grads[:, start : start + width], 0, 0)
        for piece in range(1, pieces):
            left = start + piece * width
            going += contract(chosen[piece], grads[:, left : left + width], 0, 0)
        going = going.astype(jnp.bfloat16)
        for group in range(groups):
            out_ref[section, group, :, share + 2 * term_width :] = going[
                group * row_count : (group + 1) * row_count
            ]


def last_kernel(
    route_ref, first_ref, late_ref, grad_ref, key_ref, value_ref, *, groups
):
    micro_count = route_ref.shape[0]
    source_rows, column_count = grad_ref.shape
    row_count = source_rows // micro_count
    half = row_count // 2
    share, head_size = key_ref.shape[1:]
    term_width = 2 * head_size
    width = late_ref.shape[1] - share - 2 * term_width
    pieces = column_count // width
    for index, packed in enumerate((first_ref[...], late_ref[:, :share])):
        start = share + index * term_width
        total = contract(packed, late_ref[:, start : start + term_width], 0, 0)
        key_ref[index] = total[:, :head_size]
        value_ref[index] = total[:, head_size:]
    shape = (source_rows, late_ref.shape[0])
    row, source = iota(shape, 1), iota(shape, 0)
    slot = source // half
    target = jnp.full(shape, -1, jnp.int32)
    for micro in range(micro_count):
        for side in range(2):
            target = jnp.where(
                slot == 2 * micro + side, micro * groups + route_ref[micro, side], target
            )
    going = target == row // row_count
    inner, wanted = row % row_count, source % half
    for piece in range(pieces):
        chosen = as_float(going & (inner == piece * half + wanted)).astype(jnp.bfloat16)
        grad_ref[:, piece * width : (piece + 1) * width] = contract(
            chosen, late_ref[:, share + 2 * term_width :], 1, 0
        ).astype(jnp.bfloat16)


def call(kernel, outs, operands, scalars=0, whole=0, any_outs=0, scratch=(), vmem_bytes=0, cost=0):
    spaces = [pltpu.SMEM] * scalars + [pltpu.VMEM] * (len(operands) - scalars - whole)
    spaces += [pl.ANY] * whole
    return pl.pallas_call(
        kernel,
        out_shape=outs,
        in_specs=[pl.BlockSpec(memory_space=space) for space in spaces],
        out_specs=[
            pl.BlockSpec(memory_space=pl.ANY if place < any_outs else pltpu.VMEM)
            for place in range(len(outs))
        ],
        scratch_shapes=scratch,
        compiler_params=pltpu.CompilerParams(vmem_limit_bytes=vmem_bytes),
        cost_estimate=pl.CostEstimate(flops=0, bytes_accessed=cost, transcendentals=0),
    )(*operands)


def exchange(blocks):
    return lax.all_to_all(blocks, ("pipe", "dp"), split_axis=0, concat_axis=0, tiled=True)


def swapped(value, axis, mask):
    pairs = [(source, source ^ mask) for source in range(lax.axis_size(axis))]
    return lax.ppermute(value, axis, pairs)


def direct_pieces(payload, sections):
    masks = [mask for mask in range(1, sections) if mask & (mask - 1) == 0]
    return {mask: swapped(payload, "pipe", mask) for mask in masks}


def relayed_pieces(pieces, sections):
    pieces = dict(pieces)
    for mask in range(1, sections):
        low = mask & -mask
        if mask != low:
            pieces[mask] = swapped(pieces[mask - low], "pipe", low)
    return [pieces[mask] for mask in range(1, sections)]


def body(hidden, lengths, route, gain, key_weight, value_weight, cotangent):
    groups = lax.axis_size("dp")
    sections = lax.axis_size("pipe")
    group_index = lax.axis_index("dp")
    section_index = lax.axis_index("pipe")
    micro_count = lengths.shape[0]
    assert micro_count == sections
    source_rows, column_count = hidden.shape
    row_count = source_rows // micro_count
    feature_count = gain.shape[1]
    head_size = key_weight.shape[2]
    assert row_count * feature_count == head_size * head_size
    share = feature_count // groups
    width = column_count // pieces_of(column_count)
    devices = sections * groups

    line_width = 2 * head_size

    def share_of(turn, owner):
        parts = [
            lax.dynamic_slice(array, (turn, owner * share, 0), (1, share, head_size))[0]
            for array in (key_weight, value_weight)
        ]
        return jnp.concatenate(parts, axis=1)

    def own_rows(mask):
        start = lax.bitwise_xor(section_index, mask) * row_count
        rows = lax.dynamic_slice(hidden, (start, 0), (row_count, column_count))
        return fold(rows, line_width)

    slice_ = lax.dynamic_slice(gain, (0, group_index * share), (2, share))
    high = lax.reduce_precision(slice_, 8, 7)
    middle = lax.reduce_precision(slice_ - high, 8, 7)
    terms = jnp.stack([high, middle, slice_ - high - middle], axis=1).reshape(6, share)
    terms = jnp.pad(
        terms.astype(jnp.bfloat16), ((0, GAIN_LINES - 6), (0, line_width - share))
    )

    first = share_of(0, group_index)
    came = [
        swapped(jnp.concatenate([first, own_rows(mask), terms], axis=0), "pipe", mask)
        for mask in range(1, sections)
    ]
    tags = jnp.concatenate([lengths, route], axis=1).astype(jnp.bfloat16)
    tags = jnp.pad(tags, ((0, -micro_count % 16), (0, line_width - tags.shape[1])))
    upstream = lax.dynamic_slice_in_dim(
        cotangent, section_index * row_count, row_count, 0
    ).astype(jnp.float32)
    tags, own_tail, upstream = lax.optimization_barrier(
        (tags, jnp.concatenate([own_rows(0), terms], axis=0), upstream)
    )
    column = jnp.concatenate(
        [piece[:share] for piece in came]
        + [own_tail]
        + [piece[share:] for piece in came]
        + [tags],
        axis=0,
    )
    distant = share_of(1, lax.bitwise_xor(group_index, groups - 2))
    column, second, distant = lax.optimization_barrier(
        (column, share_of(1, group_index), distant)
    )
    chips = range(1, groups // 2)
    plane = jnp.stack([column] + [swapped(column, "dp", 2 * chip) for chip in chips])
    came = direct_pieces(second, sections)
    came[sections // 2], distant = lax.optimization_barrier((came[sections // 2], distant))
    came = relayed_pieces(came, sections)
    far = swapped(distant, "pipe", sections // 2)
    plane, came, far, distant = lax.optimization_barrier((plane, came, far, distant))
    first_shares = (plane, swapped(plane, "dp", 1))
    column = jnp.concatenate(came, axis=0)
    planes = [column] + [swapped(column, "dp", 2 * chip) for chip in chips[:-1]]
    far = relayed_pieces({**direct_pieces(distant, sections // 2), sections // 2: far}, sections)

    key_parts = key_weight.reshape(2, groups, share, head_size)
    value_parts = value_weight.reshape(2, groups, share, head_size)

    def layers_call(kernel, turns, outs, operands, shares, scratch, cost, vmem_bytes, whole, any_outs):
        weight = pltpu.VMEM((groups, sections * share, line_width), jnp.bfloat16)
        return call(
            kernel,
            outs,
            (*operands, key_parts, value_parts, *shares),
            whole=2 + len(shares) + whole,
            any_outs=any_outs,
            scratch=[
                *scratch,
                *[weight] * turns,
                pltpu.SemaphoreType.DMA((2, 4)),
            ],
            vmem_bytes=vmem_bytes,
            cost=cost,
        )

    def blocks_shape(columns):
        return jax.ShapeDtypeStruct((sections, groups, row_count, columns), jnp.bfloat16)

    def exchanged(blocks):
        columns = blocks.shape[3]
        got = exchange(blocks.reshape(devices, row_count, columns))
        return got.reshape(devices * row_count, columns)

    line = (row_count, state_width(feature_count, head_size))
    line_count = plane.shape[1] - (sections - 1) * share
    gain_scratch = pltpu.VMEM((2 * sections, feature_count), jnp.float32)
    state_shape = (sections + 2 + 2 * sections // row_count, *line)
    state, packed = layers_call(
        functools.partial(first_kernel, doc_count=lengths.shape[1]),
        1,
        [jax.ShapeDtypeStruct(state_shape, jnp.float32), blocks_shape(share)],
        (upstream,),
        first_shares,
        (
            pltpu.VMEM(state_shape, jnp.float32),
            pltpu.VMEM((2, groups // 2, line_count, line_width), jnp.bfloat16),
            pltpu.VMEM((sections, row_count, column_count), jnp.float32),
            pltpu.VMEM((groups, 2 * sections, share), jnp.float32),
            gain_scratch,
            pltpu.SemaphoreType.DMA((3,)),
        ),
        18 << 20,
        (8 << 20) + sections * feature_count * 2 * line_width + 1024 * devices * row_count,
        0,
        1,
    )
    state, planes, far = lax.optimization_barrier((state, planes, far))
    plane = jnp.stack(planes + [jnp.concatenate(far, axis=0)])
    plane, packed = lax.optimization_barrier((plane, packed))
    packed = exchanged(packed)
    second_shares = (plane, swapped(plane, "dp", 1))
    columns = share + 4 * head_size + width
    (late,) = layers_call(
        second_kernel,
        2,
        [blocks_shape(columns)],
        (state,),
        (*first_shares, *second_shares),
        (
            pltpu.VMEM(state_shape, jnp.float32),
            pltpu.VMEM((sections, *line), jnp.float32),
            gain_scratch,
            pltpu.SemaphoreType.DMA((1,)),
        ),
        48 << 20,
        60 << 20,
        1,
        0,
    )
    late, packed = lax.optimization_barrier((late, packed))
    late = exchanged(late)
    grad_shape = jax.ShapeDtypeStruct((2, share, head_size), jnp.float32)
    return tuple(
        call(
            functools.partial(last_kernel, groups=groups),
            [jax.ShapeDtypeStruct((source_rows, column_count), jnp.bfloat16)] + [grad_shape] * 2,
            (route, packed, late),
            scalars=1,
            vmem_bytes=(4 << 20) + 10000 * devices * row_count,
        )
    )


def solution(mesh):
    placed = (
        P("dp", "pipe"),
        P("dp", None),
        P("dp", None),
        P("pipe", None),
        P("pipe", None, None),
        P("pipe", None, None),
        P("dp", None),
    )
    return jax.shard_map(
        body,
        mesh=mesh,
        in_specs=placed,
        out_specs=(P("dp", "pipe"), P("pipe", "dp", None), P("pipe", "dp", None)),
        check_vma=False,
    )
```

```python
import functools

import jax
import jax.numpy as jnp
from jax import lax
from jax.experimental import pallas as pl
from jax.experimental.pallas import tpu as pltpu
from jax.sharding import PartitionSpec as P

ROPE_BASE = 500000.0
EPSILON = 1e-05
NEGATIVE = -1e30
LANES = 128
GAIN_LINES = 8


def iota(shape, dim):
    return lax.broadcasted_iota(jnp.int32, shape, dim)


def as_float(flags):
    return jnp.where(flags, 1.0, 0.0).astype(jnp.float32)


def contract(left, right, left_dim, right_dim):
    return lax.dot_general(
        left, right, (((left_dim,), (right_dim,)), ((), ())), preferred_element_type=jnp.float32
    )


def pieces_of(column_count):
    return 2 if column_count % (2 * LANES) == 0 else 1


def fold(rows, width):
    row_count, columns = rows.shape
    if columns >= width:
        return jnp.concatenate(
            [rows[:, start : start + width] for start in range(0, columns, width)], axis=0
        )
    lines = row_count * columns // width
    return jnp.concatenate(
        [rows[start : start + lines] for start in range(0, row_count, lines)], axis=1
    )


def unfold(lines, row_count, columns):
    width = lines.shape[1]
    if columns >= width:
        return jnp.concatenate(
            [lines[start : start + row_count] for start in range(0, lines.shape[0], row_count)],
            axis=1,
        )
    return jnp.concatenate(
        [lines[:, start : start + columns] for start in range(0, width, columns)], axis=0
    )


def choosers(source, groups, pieces):
    row_count = source.shape[0]
    half = row_count // 2
    shape = (row_count, groups * row_count)
    row, line = iota(shape, 0), iota(shape, 1)
    back = source.astype(jnp.int32) == line // row_count
    return [
        as_float(back & (line % row_count == piece * half + row % half)).astype(jnp.bfloat16)
        for piece in range(pieces)
    ]


def turned(vector, cosine, sine):
    return vector * cosine + pltpu.roll(vector, vector.shape[1] // 2, 1) * sine


def heads_down(rows, head_size):
    count = rows.shape[1] // head_size
    return jnp.concatenate(
        [rows[:, head * head_size : (head + 1) * head_size] for head in range(count)], axis=0
    )


def heads_across(stacked, row_count):
    count = stacked.shape[0] // row_count
    return jnp.concatenate(
        [stacked[head * row_count : (head + 1) * row_count] for head in range(count)], axis=1
    )


def turned_heads(rows, cosine, sine):
    stacked = heads_down(rows, cosine.shape[1])
    repeats = stacked.shape[0] // rows.shape[0]
    return turned(stacked, jnp.tile(cosine, (repeats, 1)), jnp.tile(sine, (repeats, 1)))


def forward_layer(rows, gain_row, weight, cosine, sine, allowed):
    row_count, feature_count = rows.shape
    head_size = cosine.shape[1]
    scale = lax.rsqrt(jnp.sum(rows * rows, axis=1, keepdims=True) / feature_count + EPSILON)
    normed = rows * scale * gain_row
    packed = normed.astype(jnp.bfloat16)
    pair = contract(packed, weight, 1, 0)
    queries = turned_heads(normed, cosine, sine).astype(jnp.bfloat16)
    keys = turned(pair[:, :head_size], cosine, sine).astype(jnp.bfloat16)
    values = pair[:, head_size:].astype(jnp.bfloat16)
    scores = contract(keys, queries, 1, 1) * head_size ** (-0.5)
    scores = jnp.where(allowed, scores, NEGATIVE)
    raised = jnp.exp(scores - jnp.max(scores, axis=0, keepdims=True))
    weights = raised / jnp.sum(raised, axis=0, keepdims=True)
    mixed = contract(weights.astype(jnp.bfloat16), values, 0, 0)
    kept = (scale, keys, values, weights)
    return rows + heads_across(mixed, row_count), packed, kept


def backward_layer(upstream, rows, gain_row, weight, cosine, sine, kept):
    scale, keys, values, weights = kept
    row_count, feature_count = rows.shape
    head_size = cosine.shape[1]
    queries = turned_heads(rows * scale * gain_row, cosine, sine).astype(jnp.bfloat16)
    stacked = heads_down(upstream, head_size).astype(jnp.bfloat16)
    d_weights = contract(values, stacked, 1, 1).astype(jnp.bfloat16).astype(jnp.float32)
    d_values = contract(weights.astype(jnp.bfloat16), stacked, 1, 0)
    d_scores = weights * (d_weights - jnp.sum(d_weights * weights, axis=0, keepdims=True))
    d_scores = (d_scores * head_size ** (-0.5)).astype(jnp.bfloat16)
    d_keys = contract(d_scores, queries, 1, 0)
    terms = jnp.concatenate([turned(d_keys, cosine, -sine), d_values], axis=1)
    terms = terms.astype(jnp.bfloat16)
    d_queries = contract(d_scores, keys, 0, 0)
    repeats = stacked.shape[0] // row_count
    d_queries = turned(d_queries, jnp.tile(cosine, (repeats, 1)), jnp.tile(-sine, (repeats, 1)))
    d_normed = contract(terms, weight, 1, 1) + heads_across(d_queries, row_count)
    scaled = d_normed * gain_row
    inner = jnp.sum(scaled * rows, axis=1, keepdims=True) / feature_count
    return upstream + scale * scaled - rows * (scale * scale * scale * inner), terms


def state_width(feature_count, head_size):
    return feature_count + 4 * head_size


def save_layer(index, rows, kept, state_ref):
    scale, keys, values, weights = kept
    feature_count, head_size = rows.shape[1], keys.shape[1]
    state_ref[index, :, :feature_count] = rows
    parts = (weights, keys, values, jnp.broadcast_to(scale, keys.shape))
    for place, part in enumerate(parts):
        start = feature_count + place * head_size
        state_ref[index, :, start : start + head_size] = part.astype(jnp.float32)


def load_layer(index, state_ref, feature_count):
    head_size = (state_ref.shape[2] - feature_count) // 4
    parts = []
    for place in range(4):
        start = feature_count + place * head_size
        parts.append(state_ref[index, :, start : start + head_size])
    weights, keys, values, scale = parts
    kept = (scale[:, 0:1], keys.astype(jnp.bfloat16), values.astype(jnp.bfloat16), weights)
    return state_ref[index, :, :feature_count], kept


def repeat_steps(count, step, carry):
    if count <= 8:
        for index in range(count):
            carry = step(index, carry)
        return carry
    return lax.fori_loop(0, count, step, carry)


def layer_inputs(index, gain_ref, weight_ref, sections):
    place = lax.bitwise_xor(lax.axis_index("pipe"), index)
    groups = weight_ref.shape[0]
    share = weight_ref.shape[1] // sections
    rows = pl.ds(pl.multiple_of(place * share, share), share)
    weight = []
    for owner in range(groups):
        mask = lax.bitwise_xor(lax.axis_index("dp"), owner)
        line = lax.rem(mask, 2) * (groups // 2) + lax.div(mask, 2)
        weight.append(weight_ref[jnp.where(place == 0, owner, line), rows, :])
    return gain_ref[pl.ds(place, 1), :], jnp.concatenate(weight, axis=0)


def forward_steps(rows, gain_ref, weight_ref, tables, state_ref, packed_ref):
    cosine, sine, allowed = tables
    sections, groups = packed_ref.shape[:2]
    share = weight_ref.shape[1] // sections

    def step(index, rows):
        gain_row, weight = layer_inputs(index, gain_ref, weight_ref, sections)
        after, packed, kept = forward_layer(rows, gain_row, weight, cosine, sine, allowed)
        for group in range(groups):
            packed_ref[index, group, :, :share] = packed[:, group * share : (group + 1) * share]
        save_layer(index, rows, kept, state_ref)
        return after

    return repeat_steps(sections, step, rows)


def backward_steps(upstream, gain_ref, weight_ref, tables, state_ref, terms_ref, start):
    cosine, sine, _ = tables
    sections, groups = terms_ref.shape[:2]
    width = weight_ref.shape[2]

    def step(back, upstream):
        index = sections - 1 - back
        gain_row, weight = layer_inputs(index, gain_ref, weight_ref, sections)
        rows, kept = load_layer(index, state_ref, upstream.shape[1])
        before, terms = backward_layer(upstream, rows, gain_row, weight, cosine, sine, kept)
        for group in range(groups):
            terms_ref[index, group, :, start : start + width] = terms
        return before

    return repeat_steps(sections, step, upstream)


def fill(turn, key_ref, value_ref, shares, weight_ref, sems):
    groups, share, head_size = key_ref.shape[1:]
    moved = weight_ref.shape[1] - share
    copies = [
        (key_ref.at[turn], weight_ref.at[:, :share, :head_size]),
        (value_ref.at[turn], weight_ref.at[:, :share, head_size:]),
    ]
    for core, ref in enumerate(shares):
        lines = pl.ds(core * (groups // 2), groups // 2)
        copies.append((ref.at[:, pl.ds(0, moved)], weight_ref.at[lines, pl.ds(share, moved)]))
    copies = [
        pltpu.make_async_copy(*pair, sems.at[turn, index]) for index, pair in enumerate(copies)
    ]
    for copy in copies:
        copy.start()
    return copies


def first_kernel(
    upstream_ref,
    key_ref,
    value_ref,
    share_ref,
    other_ref,
    state_out,
    packed_ref,
    state_ref,
    lines_ref,
    rows_ref,
    gains_ref,
    gain_ref,
    line_sems,
    weight_ref,
    sems,
    *,
    doc_count
):
    sections = packed_ref.shape[0]
    groups, share, head_size = key_ref.shape[1:]
    row_count, feature_count = upstream_ref.shape
    column_count = feature_count // sections
    chips, line_count, width = lines_ref.shape[1:]
    used = share_ref.shape[1] - line_count
    section, group = lax.axis_index("pipe"), lax.axis_index("dp")
    shares = (share_ref, other_ref)
    line_copies = [
        pltpu.make_async_copy(
            ref.at[:, pl.ds(used, line_count)], lines_ref.at[core], line_sems.at[core]
        )
        for core, ref in enumerate(shares)
    ]
    for copy in line_copies:
        copy.start()
    copies = fill(0, key_ref, value_ref, shares, weight_ref, sems)
    state_ref[sections + 1, :, :feature_count] = upstream_ref[...]
    for copy in line_copies:
        copy.wait()

    row = iota((row_count, 1), 0)
    offset = row.astype(jnp.float32)
    document = jnp.zeros((row_count, 1), jnp.float32)
    position = jnp.zeros((row_count, 1), jnp.float32)
    source = jnp.zeros((row_count, 1), jnp.float32)
    parts = [jnp.zeros((row_count, column_count), jnp.float32) for _ in range(sections)]
    folded = row_count * column_count // width
    tail = folded + GAIN_LINES
    for core in range(2):
        for chip in range(chips):
            lines = lines_ref[core, chip].astype(jnp.float32)
            tags = lines[sections * tail :]
            tags = jnp.sum(
                jnp.where(iota(tags.shape, 0) == section, tags, 0.0), axis=0, keepdims=True
            )
            target = jnp.where(
                row < row_count // 2,
                tags[:, doc_count : doc_count + 1],
                tags[:, doc_count + 1 : doc_count + 2],
            )
            came = as_float(target.astype(jnp.int32) == group)
            end = jnp.zeros((1, 1), jnp.float32)
            number = jnp.zeros((row_count, 1), jnp.float32)
            opening = jnp.zeros((row_count, 1), jnp.float32)
            for doc in range(doc_count - 1):
                end = end + tags[:, doc : doc + 1]
                passed = offset >= end
                number = number + as_float(passed)
                opening = jnp.where(passed, end, opening)
            owner = lax.bitwise_xor(group, 2 * chip + core)
            document += came * number
            position += came * (offset - opening)
            source += came * owner.astype(jnp.float32)
            gain_rows = []
            for mask in range(sections):
                piece = lines[mask * tail : mask * tail + folded]
                parts[mask] += came * unfold(piece, row_count, column_count)
                terms = lines[mask * tail + folded : (mask + 1) * tail, :share]
                gain_rows += [
                    terms[3 * turn : 3 * turn + 1]
                    + terms[3 * turn + 1 : 3 * turn + 2]
                    + terms[3 * turn + 2 : 3 * turn + 3]
                    for turn in range(2)
                ]
            gains_ref[owner] = jnp.concatenate(gain_rows[0::2] + gain_rows[1::2], axis=0)
    for owner in range(groups):
        gain_ref[:, owner * share : (owner + 1) * share] = gains_ref[owner]
    for start in range(0, 2 * sections, row_count):
        state_ref[sections + 2 + start // row_count, :, :feature_count] = gain_ref[
            start : start + row_count
        ]
    for mask in range(sections):
        rows_ref[lax.bitwise_xor(section, mask)] = parts[mask]
    rows = jnp.concatenate([rows_ref[index] for index in range(sections)], axis=1)

    lane = iota((1, head_size), 1)
    middle = head_size // 2
    exponent = (lane % middle).astype(jnp.float32) * (2.0 / head_size)
    angles = position * jnp.exp(exponent * -jnp.log(jnp.float32(ROPE_BASE)))
    cosine = jnp.cos(angles)
    sine = jnp.where(lane < middle, -jnp.sin(angles), jnp.sin(angles))
    shape = (row_count, row_count * feature_count // head_size)
    pick = as_float(iota(shape, 1) % row_count == iota(shape, 0))
    document_across = jnp.sum(document * pick, axis=0, keepdims=True)
    position_across = jnp.sum(position * pick, axis=0, keepdims=True)
    allowed = (document == document_across) & (position <= position_across)
    kept = (cosine, sine, as_float(allowed), jnp.broadcast_to(source, cosine.shape))
    for place, table in enumerate(kept):
        start = feature_count + place * head_size
        state_ref[sections, :, start : start + head_size] = table
    tables = (cosine, sine, allowed)
    for copy in copies:
        copy.wait()
    state_ref[sections, :, :feature_count] = forward_steps(
        rows, gain_ref.at[pl.ds(0, sections)], weight_ref, tables, state_ref, packed_ref
    )
    state_copy = pltpu.make_async_copy(state_ref, state_out, line_sems.at[2])
    state_copy.start()
    state_copy.wait()


def second_kernel(
    state_in,
    key_ref,
    value_ref,
    share_ref,
    other_ref,
    late_share_ref,
    late_other_ref,
    out_ref,
    first_ref,
    state_ref,
    gain_ref,
    state_sem,
    late_weight_ref,
    weight_ref,
    sems
):
    state_copy = pltpu.make_async_copy(state_in, first_ref, state_sem.at[0])
    state_copy.start()
    sections, groups, row_count, _ = out_ref.shape
    share, head_size = key_ref.shape[2:]
    feature_count, term_width = groups * share, 2 * head_size
    late_shares = (late_share_ref, late_other_ref)
    late_copies = fill(1, key_ref, value_ref, late_shares, late_weight_ref, sems)
    copies = fill(0, key_ref, value_ref, (share_ref, other_ref), weight_ref, sems)
    state_copy.wait()
    kept = []
    for place in range(4):
        start = feature_count + place * head_size
        kept.append(first_ref[sections, :, start : start + head_size])
    cosine, sine, allowed, source = kept
    tables = (cosine, sine, allowed > 0.5)
    for start in range(0, 2 * sections, row_count):
        gain_ref[start : start + row_count] = first_ref[
            sections + 2 + start // row_count, :, :feature_count
        ]
    late_gain = gain_ref.at[pl.ds(sections, sections)]
    for copy in late_copies:
        copy.wait()
    forward_steps(
        first_ref[sections, :, :feature_count],
        late_gain,
        late_weight_ref,
        tables,
        state_ref,
        out_ref,
    )
    upstream = backward_steps(
        first_ref[sections + 1, :, :feature_count],
        late_gain,
        late_weight_ref,
        tables,
        state_ref,
        out_ref,
        share + term_width,
    )
    for copy in copies:
        copy.wait()
    grads = backward_steps(
        upstream,
        gain_ref.at[pl.ds(0, sections)],
        weight_ref,
        tables,
        first_ref,
        out_ref,
        share,
    ).astype(jnp.bfloat16)
    column_count = feature_count // sections
    pieces = pieces_of(column_count)
    width = column_count // pieces
    chosen = choosers(source[:, 0:1], groups, pieces)
    for section in range(sections):
        start = section * column_count
        going = contract(chosen[0], grads[:, start : start + width], 0, 0)
        for piece in range(1, pieces):
            left = start + piece * width
            going += contract(chosen[piece], grads[:, left : left + width], 0, 0)
        going = going.astype(jnp.bfloat16)
        for group in range(groups):
            out_ref[section, group, :, share + 2 * term_width :] = going[
                group * row_count : (group + 1) * row_count
            ]


def last_kernel(
    route_ref, first_ref, late_ref, grad_ref, key_ref, value_ref, *, groups
):
    micro_count = route_ref.shape[0]
    source_rows, column_count = grad_ref.shape
    row_count = source_rows // micro_count
    half = row_count // 2
    share, head_size = key_ref.shape[1:]
    term_width = 2 * head_size
    width = late_ref.shape[1] - share - 2 * term_width
    pieces = column_count // width
    for index, packed in enumerate((first_ref[...], late_ref[:, :share])):
        start = share + index * term_width
        total = contract(packed, late_ref[:, start : start + term_width], 0, 0)
        key_ref[index] = total[:, :head_size]
        value_ref[index] = total[:, head_size:]
    shape = (source_rows, late_ref.shape[0])
    row, source = iota(shape, 1), iota(shape, 0)
    slot = source // half
    target = jnp.full(shape, -1, jnp.int32)
    for micro in range(micro_count):
        for side in range(2):
            target = jnp.where(
                slot == 2 * micro + side, micro * groups + route_ref[micro, side], target
            )
    going = target == row // row_count
    inner, wanted = row % row_count, source % half
    for piece in range(pieces):
        chosen = as_float(going & (inner == piece * half + wanted)).astype(jnp.bfloat16)
        grad_ref[:, piece * width : (piece + 1) * width] = contract(
            chosen, late_ref[:, share + 2 * term_width :], 1, 0
        ).astype(jnp.bfloat16)


def call(kernel, outs, operands, scalars=0, whole=0, any_outs=0, scratch=(), vmem_bytes=0, cost=0):
    spaces = [pltpu.SMEM] * scalars + [pltpu.VMEM] * (len(operands) - scalars - whole)
    spaces += [pl.ANY] * whole
    return pl.pallas_call(
        kernel,
        out_shape=outs,
        in_specs=[pl.BlockSpec(memory_space=space) for space in spaces],
        out_specs=[
            pl.BlockSpec(memory_space=pl.ANY if place < any_outs else pltpu.VMEM)
            for place in range(len(outs))
        ],
        scratch_shapes=scratch,
        compiler_params=pltpu.CompilerParams(vmem_limit_bytes=vmem_bytes),
        cost_estimate=pl.CostEstimate(flops=0, bytes_accessed=cost, transcendentals=0),
    )(*operands)


def exchange(blocks):
    return lax.all_to_all(blocks, ("pipe", "dp"), split_axis=0, concat_axis=0, tiled=True)


def swapped(value, axis, mask):
    pairs = [(source, source ^ mask) for source in range(lax.axis_size(axis))]
    return lax.ppermute(value, axis, pairs)


def direct_pieces(payload, sections):
    masks = [mask for mask in range(1, sections) if mask & (mask - 1) == 0]
    return {mask: swapped(payload, "pipe", mask) for mask in masks}


def relayed_pieces(pieces, sections):
    pieces = dict(pieces)
    for mask in range(1, sections):
        low = mask & -mask
        if mask != low:
            pieces[mask] = swapped(pieces[mask - low], "pipe", low)
    return [pieces[mask] for mask in range(1, sections)]


def body(hidden, lengths, route, gain, key_weight, value_weight, cotangent):
    groups = lax.axis_size("dp")
    sections = lax.axis_size("pipe")
    group_index = lax.axis_index("dp")
    section_index = lax.axis_index("pipe")
    micro_count = lengths.shape[0]
    assert micro_count == sections
    source_rows, column_count = hidden.shape
    row_count = source_rows // micro_count
    feature_count = gain.shape[1]
    head_size = key_weight.shape[2]
    assert row_count * feature_count == head_size * head_size
    share = feature_count // groups
    width = column_count // pieces_of(column_count)
    devices = sections * groups

    line_width = 2 * head_size

    def share_of(turn, owner):
        parts = [
            lax.dynamic_slice(array, (turn, owner * share, 0), (1, share, head_size))[0]
            for array in (key_weight, value_weight)
        ]
        return jnp.concatenate(parts, axis=1)

    def own_rows(mask):
        start = lax.bitwise_xor(section_index, mask) * row_count
        rows = lax.dynamic_slice(hidden, (start, 0), (row_count, column_count))
        return fold(rows, line_width)

    slice_ = lax.dynamic_slice(gain, (0, group_index * share), (2, share))
    high = lax.reduce_precision(slice_, 8, 7)
    middle = lax.reduce_precision(slice_ - high, 8, 7)
    terms = jnp.stack([high, middle, slice_ - high - middle], axis=1).reshape(6, share)
    terms = jnp.pad(
        terms.astype(jnp.bfloat16), ((0, GAIN_LINES - 6), (0, line_width - share))
    )

    first = share_of(0, group_index)
    came = [
        swapped(jnp.concatenate([first, own_rows(mask), terms], axis=0), "pipe", mask)
        for mask in range(1, sections)
    ]
    tags = jnp.concatenate([lengths, route], axis=1).astype(jnp.bfloat16)
    tags = jnp.pad(tags, ((0, -micro_count % 16), (0, line_width - tags.shape[1])))
    upstream = lax.dynamic_slice_in_dim(
        cotangent, section_index * row_count, row_count, 0
    ).astype(jnp.float32)
    tags, own_tail, upstream = lax.optimization_barrier(
        (tags, jnp.concatenate([own_rows(0), terms], axis=0), upstream)
    )
    column = jnp.concatenate(
        [piece[:share] for piece in came]
        + [own_tail]
        + [piece[share:] for piece in came]
        + [tags],
        axis=0,
    )
    distant = share_of(1, lax.bitwise_xor(group_index, groups - 2))
    column, second, distant = lax.optimization_barrier(
        (column, share_of(1, group_index), distant)
    )
    chips = range(1, groups // 2)
    plane = jnp.stack([column] + [swapped(column, "dp", 2 * chip) for chip in chips])
    came = direct_pieces(second, sections)
    came[sections // 2], distant = lax.optimization_barrier((came[sections // 2], distant))
    came = relayed_pieces(came, sections)
    far = swapped(distant, "pipe", sections // 2)
    plane, came, far, distant = lax.optimization_barrier((plane, came, far, distant))
    first_shares = (plane, swapped(plane, "dp", 1))
    column = jnp.concatenate(came, axis=0)
    planes = [column] + [swapped(column, "dp", 2 * chip) for chip in chips[:-1]]
    far = relayed_pieces({**direct_pieces(distant, sections // 2), sections // 2: far}, sections)

    key_parts = key_weight.reshape(2, groups, share, head_size)
    value_parts = value_weight.reshape(2, groups, share, head_size)

    def layers_call(kernel, turns, outs, operands, shares, scratch, cost, vmem_bytes, whole, any_outs):
        weight = pltpu.VMEM((groups, sections * share, line_width), jnp.bfloat16)
        return call(
            kernel,
            outs,
            (*operands, key_parts, value_parts, *shares),
            whole=2 + len(shares) + whole,
            any_outs=any_outs,
            scratch=[
                *scratch,
                *[weight] * turns,
                pltpu.SemaphoreType.DMA((2, 4)),
            ],
            vmem_bytes=vmem_bytes,
            cost=cost,
        )

    def blocks_shape(columns):
        return jax.ShapeDtypeStruct((sections, groups, row_count, columns), jnp.bfloat16)

    def exchanged(blocks):
        columns = blocks.shape[3]
        got = exchange(blocks.reshape(devices, row_count, columns))
        return got.reshape(devices * row_count, columns)

    line = (row_count, state_width(feature_count, head_size))
    line_count = plane.shape[1] - (sections - 1) * share
    gain_scratch = pltpu.VMEM((2 * sections, feature_count), jnp.float32)
    state_shape = (sections + 2 + 2 * sections // row_count, *line)
    state, packed = layers_call(
        functools.partial(first_kernel, doc_count=lengths.shape[1]),
        1,
        [jax.ShapeDtypeStruct(state_shape, jnp.float32), blocks_shape(share)],
        (upstream,),
        first_shares,
        (
            pltpu.VMEM(state_shape, jnp.float32),
            pltpu.VMEM((2, groups // 2, line_count, line_width), jnp.bfloat16),
            pltpu.VMEM((sections, row_count, column_count), jnp.float32),
            pltpu.VMEM((groups, 2 * sections, share), jnp.float32),
            gain_scratch,
            pltpu.SemaphoreType.DMA((3,)),
        ),
        18 << 20,
        (8 << 20) + sections * feature_count * 2 * line_width + 1024 * devices * row_count,
        0,
        1,
    )
    state, planes, far = lax.optimization_barrier((state, planes, far))
    plane = jnp.stack(planes + [jnp.concatenate(far, axis=0)])
    plane, packed = lax.optimization_barrier((plane, packed))
    packed = exchanged(packed)
    second_shares = (plane, swapped(plane, "dp", 1))
    columns = share + 4 * head_size + width
    (late,) = layers_call(
        second_kernel,
        2,
        [blocks_shape(columns)],
        (state,),
        (*first_shares, *second_shares),
        (
            pltpu.VMEM(state_shape, jnp.float32),
            pltpu.VMEM((sections, *line), jnp.float32),
            gain_scratch,
            pltpu.SemaphoreType.DMA((1,)),
        ),
        48 << 20,
        58 << 20,
        1,
        0,
    )
    late, packed = lax.optimization_barrier((late, packed))
    late = exchanged(late)
    grad_shape = jax.ShapeDtypeStruct((2, share, head_size), jnp.float32)
    return tuple(
        call(
            functools.partial(last_kernel, groups=groups),
            [jax.ShapeDtypeStruct((source_rows, column_count), jnp.bfloat16)] + [grad_shape] * 2,
            (route, packed, late),
            scalars=1,
            vmem_bytes=(4 << 20) + 10000 * devices * row_count,
        )
    )


def solution(mesh):
    placed = (
        P("dp", "pipe"),
        P("dp", None),
        P("dp", None),
        P("pipe", None),
        P("pipe", None, None),
        P("pipe", None, None),
        P("dp", None),
    )
    return jax.shard_map(
        body,
        mesh=mesh,
        in_specs=placed,
        out_specs=(P("dp", "pipe"), P("pipe", "dp", None), P("pipe", "dp", None)),
        check_vma=False,
    )
```

```python
import functools

import jax
import jax.numpy as jnp
from jax import lax
from jax.experimental import pallas as pl
from jax.experimental.pallas import tpu as pltpu
from jax.sharding import PartitionSpec as P

ROPE_BASE = 500000.0
EPSILON = 1e-05
NEGATIVE = -1e30
LANES = 128
GAIN_LINES = 8


def iota(shape, dim):
    return lax.broadcasted_iota(jnp.int32, shape, dim)


def as_float(flags):
    return jnp.where(flags, 1.0, 0.0).astype(jnp.float32)


def contract(left, right, left_dim, right_dim):
    return lax.dot_general(
        left, right, (((left_dim,), (right_dim,)), ((), ())), preferred_element_type=jnp.float32
    )


def pieces_of(column_count):
    return 2 if column_count % (2 * LANES) == 0 else 1


def fold(rows, width):
    row_count, columns = rows.shape
    if columns >= width:
        return jnp.concatenate(
            [rows[:, start : start + width] for start in range(0, columns, width)], axis=0
        )
    lines = row_count * columns // width
    return jnp.concatenate(
        [rows[start : start + lines] for start in range(0, row_count, lines)], axis=1
    )


def unfold(lines, row_count, columns):
    width = lines.shape[1]
    if columns >= width:
        return jnp.concatenate(
            [lines[start : start + row_count] for start in range(0, lines.shape[0], row_count)],
            axis=1,
        )
    return jnp.concatenate(
        [lines[:, start : start + columns] for start in range(0, width, columns)], axis=0
    )


def choosers(source, groups, pieces):
    row_count = source.shape[0]
    half = row_count // 2
    shape = (row_count, groups * row_count)
    row, line = iota(shape, 0), iota(shape, 1)
    back = source.astype(jnp.int32) == line // row_count
    return [
        as_float(back & (line % row_count == piece * half + row % half)).astype(jnp.bfloat16)
        for piece in range(pieces)
    ]


def turned(vector, cosine, sine):
    return vector * cosine + pltpu.roll(vector, vector.shape[1] // 2, 1) * sine


def heads_down(rows, head_size):
    count = rows.shape[1] // head_size
    return jnp.concatenate(
        [rows[:, head * head_size : (head + 1) * head_size] for head in range(count)], axis=0
    )


def heads_across(stacked, row_count):
    count = stacked.shape[0] // row_count
    return jnp.concatenate(
        [stacked[head * row_count : (head + 1) * row_count] for head in range(count)], axis=1
    )


def turned_heads(rows, cosine, sine):
    stacked = heads_down(rows, cosine.shape[1])
    repeats = stacked.shape[0] // rows.shape[0]
    return turned(stacked, jnp.tile(cosine, (repeats, 1)), jnp.tile(sine, (repeats, 1)))


def forward_layer(rows, gain_row, weight, cosine, sine, allowed):
    row_count, feature_count = rows.shape
    head_size = cosine.shape[1]
    scale = lax.rsqrt(jnp.sum(rows * rows, axis=1, keepdims=True) / feature_count + EPSILON)
    normed = rows * scale * gain_row
    packed = normed.astype(jnp.bfloat16)
    pair = contract(packed, weight, 1, 0)
    queries = turned_heads(normed, cosine, sine).astype(jnp.bfloat16)
    keys = turned(pair[:, :head_size], cosine, sine).astype(jnp.bfloat16)
    values = pair[:, head_size:].astype(jnp.bfloat16)
    scores = contract(keys, queries, 1, 1) * head_size ** (-0.5)
    scores = jnp.where(allowed, scores, NEGATIVE)
    raised = jnp.exp(scores - jnp.max(scores, axis=0, keepdims=True))
    weights = raised / jnp.sum(raised, axis=0, keepdims=True)
    mixed = contract(weights.astype(jnp.bfloat16), values, 0, 0)
    kept = (scale, keys, values, weights)
    return rows + heads_across(mixed, row_count), packed, kept


def backward_layer(upstream, rows, gain_row, weight, cosine, sine, kept):
    scale, keys, values, weights = kept
    row_count, feature_count = rows.shape
    head_size = cosine.shape[1]
    queries = turned_heads(rows * scale * gain_row, cosine, sine).astype(jnp.bfloat16)
    stacked = heads_down(upstream, head_size).astype(jnp.bfloat16)
    d_weights = contract(values, stacked, 1, 1).astype(jnp.bfloat16).astype(jnp.float32)
    d_values = contract(weights.astype(jnp.bfloat16), stacked, 1, 0)
    d_scores = weights * (d_weights - jnp.sum(d_weights * weights, axis=0, keepdims=True))
    d_scores = (d_scores * head_size ** (-0.5)).astype(jnp.bfloat16)
    d_keys = contract(d_scores, queries, 1, 0)
    terms = jnp.concatenate([turned(d_keys, cosine, -sine), d_values], axis=1)
    terms = terms.astype(jnp.bfloat16)
    d_queries = contract(d_scores, keys, 0, 0)
    repeats = stacked.shape[0] // row_count
    d_queries = turned(d_queries, jnp.tile(cosine, (repeats, 1)), jnp.tile(-sine, (repeats, 1)))
    d_normed = contract(terms, weight, 1, 1) + heads_across(d_queries, row_count)
    scaled = d_normed * gain_row
    inner = jnp.sum(scaled * rows, axis=1, keepdims=True) / feature_count
    return upstream + scale * scaled - rows * (scale * scale * scale * inner), terms


def state_width(feature_count, head_size):
    return feature_count + 4 * head_size


def save_layer(index, rows, kept, state_ref):
    scale, keys, values, weights = kept
    feature_count, head_size = rows.shape[1], keys.shape[1]
    state_ref[index, :, :feature_count] = rows
    parts = (weights, keys, values, jnp.broadcast_to(scale, keys.shape))
    for place, part in enumerate(parts):
        start = feature_count + place * head_size
        state_ref[index, :, start : start + head_size] = part.astype(jnp.float32)


def load_layer(index, state_ref, feature_count):
    head_size = (state_ref.shape[2] - feature_count) // 4
    parts = []
    for place in range(4):
        start = feature_count + place * head_size
        parts.append(state_ref[index, :, start : start + head_size])
    weights, keys, values, scale = parts
    kept = (scale[:, 0:1], keys.astype(jnp.bfloat16), values.astype(jnp.bfloat16), weights)
    return state_ref[index, :, :feature_count], kept


def repeat_steps(count, step, carry):
    if count <= 8:
        for index in range(count):
            carry = step(index, carry)
        return carry
    return lax.fori_loop(0, count, step, carry)


def layer_inputs(index, gain_ref, weight_ref, sections):
    place = lax.bitwise_xor(lax.axis_index("pipe"), index)
    groups = weight_ref.shape[0]
    share = weight_ref.shape[1] // sections
    rows = pl.ds(pl.multiple_of(place * share, share), share)
    weight = []
    for owner in range(groups):
        mask = lax.bitwise_xor(lax.axis_index("dp"), owner)
        line = lax.rem(mask, 2) * (groups // 2) + lax.div(mask, 2)
        weight.append(weight_ref[jnp.where(place == 0, owner, line), rows, :])
    return gain_ref[pl.ds(place, 1), :], jnp.concatenate(weight, axis=0)


def forward_steps(rows, gain_ref, weight_ref, tables, state_ref, packed_ref):
    cosine, sine, allowed = tables
    sections, groups = packed_ref.shape[:2]
    share = weight_ref.shape[1] // sections

    def step(index, rows):
        gain_row, weight = layer_inputs(index, gain_ref, weight_ref, sections)
        after, packed, kept = forward_layer(rows, gain_row, weight, cosine, sine, allowed)
        for group in range(groups):
            packed_ref[index, group, :, :share] = packed[:, group * share : (group + 1) * share]
        save_layer(index, rows, kept, state_ref)
        return after

    return repeat_steps(sections, step, rows)


def backward_steps(upstream, gain_ref, weight_ref, tables, state_ref, terms_ref, start):
    cosine, sine, _ = tables
    sections, groups = terms_ref.shape[:2]
    width = weight_ref.shape[2]

    def step(back, upstream):
        index = sections - 1 - back
        gain_row, weight = layer_inputs(index, gain_ref, weight_ref, sections)
        rows, kept = load_layer(index, state_ref, upstream.shape[1])
        before, terms = backward_layer(upstream, rows, gain_row, weight, cosine, sine, kept)
        for group in range(groups):
            terms_ref[index, group, :, start : start + width] = terms
        return before

    return repeat_steps(sections, step, upstream)


def fill(turn, key_ref, value_ref, shares, weight_ref, sems):
    groups, share, head_size = key_ref.shape[1:]
    moved = weight_ref.shape[1] - share
    copies = [
        (key_ref.at[turn], weight_ref.at[:, :share, :head_size]),
        (value_ref.at[turn], weight_ref.at[:, :share, head_size:]),
    ]
    for core, ref in enumerate(shares):
        lines = pl.ds(core * (groups // 2), groups // 2)
        copies.append((ref.at[:, pl.ds(0, moved)], weight_ref.at[lines, pl.ds(share, moved)]))
    copies = [
        pltpu.make_async_copy(*pair, sems.at[turn, index]) for index, pair in enumerate(copies)
    ]
    for copy in copies:
        copy.start()
    return copies


def first_kernel(
    upstream_ref,
    key_ref,
    value_ref,
    share_ref,
    other_ref,
    state_out,
    packed_ref,
    state_ref,
    lines_ref,
    rows_ref,
    gains_ref,
    gain_ref,
    line_sems,
    weight_ref,
    sems,
    *,
    doc_count
):
    sections = packed_ref.shape[0]
    groups, share, head_size = key_ref.shape[1:]
    row_count, feature_count = upstream_ref.shape
    column_count = feature_count // sections
    chips, line_count, width = lines_ref.shape[1:]
    used = share_ref.shape[1] - line_count
    section, group = lax.axis_index("pipe"), lax.axis_index("dp")
    shares = (share_ref, other_ref)
    line_copies = [
        pltpu.make_async_copy(
            ref.at[:, pl.ds(used, line_count)], lines_ref.at[core], line_sems.at[core]
        )
        for core, ref in enumerate(shares)
    ]
    for copy in line_copies:
        copy.start()
    copies = fill(0, key_ref, value_ref, shares, weight_ref, sems)
    state_ref[sections + 1, :, :feature_count] = upstream_ref[...]
    for copy in line_copies:
        copy.wait()

    row = iota((row_count, 1), 0)
    offset = row.astype(jnp.float32)
    document = jnp.zeros((row_count, 1), jnp.float32)
    position = jnp.zeros((row_count, 1), jnp.float32)
    source = jnp.zeros((row_count, 1), jnp.float32)
    parts = [jnp.zeros((row_count, column_count), jnp.float32) for _ in range(sections)]
    folded = row_count * column_count // width
    tail = folded + GAIN_LINES
    for core in range(2):
        for chip in range(chips):
            lines = lines_ref[core, chip].astype(jnp.float32)
            tags = lines[sections * tail :]
            tags = jnp.sum(
                jnp.where(iota(tags.shape, 0) == section, tags, 0.0), axis=0, keepdims=True
            )
            target = jnp.where(
                row < row_count // 2,
                tags[:, doc_count : doc_count + 1],
                tags[:, doc_count + 1 : doc_count + 2],
            )
            came = as_float(target.astype(jnp.int32) == group)
            end = jnp.zeros((1, 1), jnp.float32)
            number = jnp.zeros((row_count, 1), jnp.float32)
            opening = jnp.zeros((row_count, 1), jnp.float32)
            for doc in range(doc_count - 1):
                end = end + tags[:, doc : doc + 1]
                passed = offset >= end
                number = number + as_float(passed)
                opening = jnp.where(passed, end, opening)
            owner = lax.bitwise_xor(group, 2 * chip + core)
            document += came * number
            position += came * (offset - opening)
            source += came * owner.astype(jnp.float32)
            gain_rows = []
            for mask in range(sections):
                piece = lines[mask * tail : mask * tail + folded]
                parts[mask] += came * unfold(piece, row_count, column_count)
                terms = lines[mask * tail + folded : (mask + 1) * tail, :share]
                gain_rows += [
                    terms[3 * turn : 3 * turn + 1]
                    + terms[3 * turn + 1 : 3 * turn + 2]
                    + terms[3 * turn + 2 : 3 * turn + 3]
                    for turn in range(2)
                ]
            gains_ref[owner] = jnp.concatenate(gain_rows[0::2] + gain_rows[1::2], axis=0)
    for owner in range(groups):
        gain_ref[:, owner * share : (owner + 1) * share] = gains_ref[owner]
    for start in range(0, 2 * sections, row_count):
        state_ref[sections + 2 + start // row_count, :, :feature_count] = gain_ref[
            start : start + row_count
        ]
    for mask in range(sections):
        rows_ref[lax.bitwise_xor(section, mask)] = parts[mask]
    rows = jnp.concatenate([rows_ref[index] for index in range(sections)], axis=1)

    lane = iota((1, head_size), 1)
    middle = head_size // 2
    exponent = (lane % middle).astype(jnp.float32) * (2.0 / head_size)
    angles = position * jnp.exp(exponent * -jnp.log(jnp.float32(ROPE_BASE)))
    cosine = jnp.cos(angles)
    sine = jnp.where(lane < middle, -jnp.sin(angles), jnp.sin(angles))
    shape = (row_count, row_count * feature_count // head_size)
    pick = as_float(iota(shape, 1) % row_count == iota(shape, 0))
    document_across = jnp.sum(document * pick, axis=0, keepdims=True)
    position_across = jnp.sum(position * pick, axis=0, keepdims=True)
    allowed = (document == document_across) & (position <= position_across)
    kept = (cosine, sine, as_float(allowed), jnp.broadcast_to(source, cosine.shape))
    for place, table in enumerate(kept):
        start = feature_count + place * head_size
        state_ref[sections, :, start : start + head_size] = table
    tables = (cosine, sine, allowed)
    for copy in copies:
        copy.wait()
    state_ref[sections, :, :feature_count] = forward_steps(
        rows, gain_ref.at[pl.ds(0, sections)], weight_ref, tables, state_ref, packed_ref
    )
    state_copy = pltpu.make_async_copy(state_ref, state_out, line_sems.at[2])
    state_copy.start()
    state_copy.wait()


def second_kernel(
    state_in,
    key_ref,
    value_ref,
    share_ref,
    other_ref,
    late_share_ref,
    late_other_ref,
    out_ref,
    first_ref,
    state_ref,
    gain_ref,
    state_sem,
    late_weight_ref,
    weight_ref,
    sems
):
    state_copy = pltpu.make_async_copy(state_in, first_ref, state_sem.at[0])
    state_copy.start()
    sections, groups, row_count, _ = out_ref.shape
    share, head_size = key_ref.shape[2:]
    feature_count, term_width = groups * share, 2 * head_size
    late_shares = (late_share_ref, late_other_ref)
    late_copies = fill(1, key_ref, value_ref, late_shares, late_weight_ref, sems)
    copies = fill(0, key_ref, value_ref, (share_ref, other_ref), weight_ref, sems)
    state_copy.wait()
    kept = []
    for place in range(4):
        start = feature_count + place * head_size
        kept.append(first_ref[sections, :, start : start + head_size])
    cosine, sine, allowed, source = kept
    tables = (cosine, sine, allowed > 0.5)
    for start in range(0, 2 * sections, row_count):
        gain_ref[start : start + row_count] = first_ref[
            sections + 2 + start // row_count, :, :feature_count
        ]
    late_gain = gain_ref.at[pl.ds(sections, sections)]
    for copy in late_copies:
        copy.wait()
    forward_steps(
        first_ref[sections, :, :feature_count],
        late_gain,
        late_weight_ref,
        tables,
        state_ref,
        out_ref,
    )
    upstream = backward_steps(
        first_ref[sections + 1, :, :feature_count],
        late_gain,
        late_weight_ref,
        tables,
        state_ref,
        out_ref,
        share + term_width,
    )
    for copy in copies:
        copy.wait()
    grads = backward_steps(
        upstream,
        gain_ref.at[pl.ds(0, sections)],
        weight_ref,
        tables,
        first_ref,
        out_ref,
        share,
    ).astype(jnp.bfloat16)
    column_count = feature_count // sections
    pieces = pieces_of(column_count)
    width = column_count // pieces
    chosen = choosers(source[:, 0:1], groups, pieces)
    for section in range(sections):
        start = section * column_count
        going = contract(chosen[0], grads[:, start : start + width], 0, 0)
        for piece in range(1, pieces):
            left = start + piece * width
            going += contract(chosen[piece], grads[:, left : left + width], 0, 0)
        going = going.astype(jnp.bfloat16)
        for group in range(groups):
            out_ref[section, group, :, share + 2 * term_width :] = going[
                group * row_count : (group + 1) * row_count
            ]


def last_kernel(
    route_ref, first_ref, late_ref, grad_ref, key_ref, value_ref, *, groups
):
    micro_count = route_ref.shape[0]
    source_rows, column_count = grad_ref.shape
    row_count = source_rows // micro_count
    half = row_count // 2
    share, head_size = key_ref.shape[1:]
    term_width = 2 * head_size
    width = late_ref.shape[1] - share - 2 * term_width
    pieces = column_count // width
    for index, packed in enumerate((first_ref[...], late_ref[:, :share])):
        start = share + index * term_width
        total = contract(packed, late_ref[:, start : start + term_width], 0, 0)
        key_ref[index] = total[:, :head_size]
        value_ref[index] = total[:, head_size:]
    shape = (source_rows, late_ref.shape[0])
    row, source = iota(shape, 1), iota(shape, 0)
    slot = source // half
    target = jnp.full(shape, -1, jnp.int32)
    for micro in range(micro_count):
        for side in range(2):
            target = jnp.where(
                slot == 2 * micro + side, micro * groups + route_ref[micro, side], target
            )
    going = target == row // row_count
    inner, wanted = row % row_count, source % half
    for piece in range(pieces):
        chosen = as_float(going & (inner == piece * half + wanted)).astype(jnp.bfloat16)
        grad_ref[:, piece * width : (piece + 1) * width] = contract(
            chosen, late_ref[:, share + 2 * term_width :], 1, 0
        ).astype(jnp.bfloat16)


def call(kernel, outs, operands, scalars=0, whole=0, any_outs=0, scratch=(), vmem_bytes=0, cost=0):
    spaces = [pltpu.SMEM] * scalars + [pltpu.VMEM] * (len(operands) - scalars - whole)
    spaces += [pl.ANY] * whole
    return pl.pallas_call(
        kernel,
        out_shape=outs,
        in_specs=[pl.BlockSpec(memory_space=space) for space in spaces],
        out_specs=[
            pl.BlockSpec(memory_space=pl.ANY if place < any_outs else pltpu.VMEM)
            for place in range(len(outs))
        ],
        scratch_shapes=scratch,
        compiler_params=pltpu.CompilerParams(vmem_limit_bytes=vmem_bytes),
        cost_estimate=pl.CostEstimate(flops=0, bytes_accessed=cost, transcendentals=0),
    )(*operands)


def exchange(blocks):
    return lax.all_to_all(blocks, ("pipe", "dp"), split_axis=0, concat_axis=0, tiled=True)


def swapped(value, axis, mask):
    pairs = [(source, source ^ mask) for source in range(lax.axis_size(axis))]
    return lax.ppermute(value, axis, pairs)


def direct_pieces(payload, sections):
    masks = [mask for mask in range(1, sections) if mask & (mask - 1) == 0]
    return {mask: swapped(payload, "pipe", mask) for mask in masks}


def relayed_pieces(pieces, sections):
    pieces = dict(pieces)
    for mask in range(1, sections):
        low = mask & -mask
        if mask != low:
            pieces[mask] = swapped(pieces[mask - low], "pipe", low)
    return [pieces[mask] for mask in range(1, sections)]


def body(hidden, lengths, route, gain, key_weight, value_weight, cotangent):
    groups = lax.axis_size("dp")
    sections = lax.axis_size("pipe")
    group_index = lax.axis_index("dp")
    section_index = lax.axis_index("pipe")
    micro_count = lengths.shape[0]
    assert micro_count == sections
    source_rows, column_count = hidden.shape
    row_count = source_rows // micro_count
    feature_count = gain.shape[1]
    head_size = key_weight.shape[2]
    assert row_count * feature_count == head_size * head_size
    share = feature_count // groups
    width = column_count // pieces_of(column_count)
    devices = sections * groups

    line_width = 2 * head_size

    def share_of(turn, owner):
        parts = [
            lax.dynamic_slice(array, (turn, owner * share, 0), (1, share, head_size))[0]
            for array in (key_weight, value_weight)
        ]
        return jnp.concatenate(parts, axis=1)

    def own_rows(mask):
        start = lax.bitwise_xor(section_index, mask) * row_count
        rows = lax.dynamic_slice(hidden, (start, 0), (row_count, column_count))
        return fold(rows, line_width)

    slice_ = lax.dynamic_slice(gain, (0, group_index * share), (2, share))
    high = lax.reduce_precision(slice_, 8, 7)
    middle = lax.reduce_precision(slice_ - high, 8, 7)
    terms = jnp.stack([high, middle, slice_ - high - middle], axis=1).reshape(6, share)
    terms = jnp.pad(
        terms.astype(jnp.bfloat16), ((0, GAIN_LINES - 6), (0, line_width - share))
    )

    first = share_of(0, group_index)
    came = [
        swapped(jnp.concatenate([first, own_rows(mask), terms], axis=0), "pipe", mask)
        for mask in range(1, sections)
    ]
    tags = jnp.concatenate([lengths, route], axis=1).astype(jnp.bfloat16)
    tags = jnp.pad(tags, ((0, -micro_count % 16), (0, line_width - tags.shape[1])))
    upstream = lax.dynamic_slice_in_dim(
        cotangent, section_index * row_count, row_count, 0
    ).astype(jnp.float32)
    tags, own_tail, upstream = lax.optimization_barrier(
        (tags, jnp.concatenate([own_rows(0), terms], axis=0), upstream)
    )
    column = jnp.concatenate(
        [piece[:share] for piece in came]
        + [own_tail]
        + [piece[share:] for piece in came]
        + [tags],
        axis=0,
    )
    distant = share_of(1, lax.bitwise_xor(group_index, groups - 2))
    column, second, distant = lax.optimization_barrier(
        (column, share_of(1, group_index), distant)
    )
    chips = range(1, groups // 2)
    plane = jnp.stack([column] + [swapped(column, "dp", 2 * chip) for chip in chips])
    came = direct_pieces(second, sections)
    came[sections // 2], distant = lax.optimization_barrier((came[sections // 2], distant))
    came = relayed_pieces(came, sections)
    far = swapped(distant, "pipe", sections // 2)
    plane, came, far, distant = lax.optimization_barrier((plane, came, far, distant))
    first_shares = (plane, swapped(plane, "dp", 1))
    column = jnp.concatenate(came, axis=0)
    planes = [column] + [swapped(column, "dp", 2 * chip) for chip in chips[:-1]]
    far = relayed_pieces({**direct_pieces(distant, sections // 2), sections // 2: far}, sections)

    key_parts = key_weight.reshape(2, groups, share, head_size)
    value_parts = value_weight.reshape(2, groups, share, head_size)

    def layers_call(kernel, turns, outs, operands, shares, scratch, cost, vmem_bytes, whole, any_outs):
        weight = pltpu.VMEM((groups, sections * share, line_width), jnp.bfloat16)
        return call(
            kernel,
            outs,
            (*operands, key_parts, value_parts, *shares),
            whole=2 + len(shares) + whole,
            any_outs=any_outs,
            scratch=[
                *scratch,
                *[weight] * turns,
                pltpu.SemaphoreType.DMA((2, 4)),
            ],
            vmem_bytes=vmem_bytes,
            cost=cost,
        )

    def blocks_shape(columns):
        return jax.ShapeDtypeStruct((sections, groups, row_count, columns), jnp.bfloat16)

    def exchanged(blocks):
        columns = blocks.shape[3]
        got = exchange(blocks.reshape(devices, row_count, columns))
        return got.reshape(devices * row_count, columns)

    line = (row_count, state_width(feature_count, head_size))
    line_count = plane.shape[1] - (sections - 1) * share
    gain_scratch = pltpu.VMEM((2 * sections, feature_count), jnp.float32)
    state_shape = (sections + 2 + 2 * sections // row_count, *line)
    state, packed = layers_call(
        functools.partial(first_kernel, doc_count=lengths.shape[1]),
        1,
        [jax.ShapeDtypeStruct(state_shape, jnp.float32), blocks_shape(share)],
        (upstream,),
        first_shares,
        (
            pltpu.VMEM(state_shape, jnp.float32),
            pltpu.VMEM((2, groups // 2, line_count, line_width), jnp.bfloat16),
            pltpu.VMEM((sections, row_count, column_count), jnp.float32),
            pltpu.VMEM((groups, 2 * sections, share), jnp.float32),
            gain_scratch,
            pltpu.SemaphoreType.DMA((3,)),
        ),
        18 << 20,
        (8 << 20) + sections * feature_count * 2 * line_width + 1024 * devices * row_count,
        0,
        1,
    )
    state, planes, far = lax.optimization_barrier((state, planes, far))
    plane = jnp.stack(planes + [jnp.concatenate(far, axis=0)])
    plane, packed = lax.optimization_barrier((plane, packed))
    packed = exchanged(packed)
    second_shares = (plane, swapped(plane, "dp", 1))
    columns = share + 4 * head_size + width
    (late,) = layers_call(
        second_kernel,
        2,
        [blocks_shape(columns)],
        (state,),
        (*first_shares, *second_shares),
        (
            pltpu.VMEM(state_shape, jnp.float32),
            pltpu.VMEM((sections, *line), jnp.float32),
            gain_scratch,
            pltpu.SemaphoreType.DMA((1,)),
        ),
        48 << 20,
        44 << 20,
        1,
        0,
    )
    late, packed = lax.optimization_barrier((late, packed))
    late = exchanged(late)
    grad_shape = jax.ShapeDtypeStruct((2, share, head_size), jnp.float32)
    return tuple(
        call(
            functools.partial(last_kernel, groups=groups),
            [jax.ShapeDtypeStruct((source_rows, column_count), jnp.bfloat16)] + [grad_shape] * 2,
            (route, packed, late),
            scalars=1,
            vmem_bytes=(4 << 20) + 10000 * devices * row_count,
        )
    )


def solution(mesh):
    placed = (
        P("dp", "pipe"),
        P("dp", None),
        P("dp", None),
        P("pipe", None),
        P("pipe", None, None),
        P("pipe", None, None),
        P("dp", None),
    )
    return jax.shard_map(
        body,
        mesh=mesh,
        in_specs=placed,
        out_specs=(P("dp", "pipe"), P("pipe", "dp", None), P("pipe", "dp", None)),
        check_vma=False,
    )
```

```python
import functools

import jax
import jax.numpy as jnp
from jax import lax
from jax.experimental import pallas as pl
from jax.experimental.pallas import tpu as pltpu
from jax.sharding import PartitionSpec as P

ROPE_BASE = 500000.0
EPSILON = 1e-05
NEGATIVE = -1e30
LANES = 128
GAIN_LINES = 8


def iota(shape, dim):
    return lax.broadcasted_iota(jnp.int32, shape, dim)


def as_float(flags):
    return jnp.where(flags, 1.0, 0.0).astype(jnp.float32)


def contract(left, right, left_dim, right_dim):
    return lax.dot_general(
        left, right, (((left_dim,), (right_dim,)), ((), ())), preferred_element_type=jnp.float32
    )


def pieces_of(column_count):
    return 2 if column_count % (2 * LANES) == 0 else 1


def fold(rows, width):
    row_count, columns = rows.shape
    if columns >= width:
        return jnp.concatenate(
            [rows[:, start : start + width] for start in range(0, columns, width)], axis=0
        )
    lines = row_count * columns // width
    return jnp.concatenate(
        [rows[start : start + lines] for start in range(0, row_count, lines)], axis=1
    )


def unfold(lines, row_count, columns):
    width = lines.shape[1]
    if columns >= width:
        return jnp.concatenate(
            [lines[start : start + row_count] for start in range(0, lines.shape[0], row_count)],
            axis=1,
        )
    return jnp.concatenate(
        [lines[:, start : start + columns] for start in range(0, width, columns)], axis=0
    )


def choosers(source, groups, pieces):
    row_count = source.shape[0]
    half = row_count // 2
    shape = (row_count, groups * row_count)
    row, line = iota(shape, 0), iota(shape, 1)
    back = source.astype(jnp.int32) == line // row_count
    return [
        as_float(back & (line % row_count == piece * half + row % half)).astype(jnp.bfloat16)
        for piece in range(pieces)
    ]


def turned(vector, cosine, sine):
    return vector * cosine + pltpu.roll(vector, vector.shape[1] // 2, 1) * sine


def heads_down(rows, head_size):
    count = rows.shape[1] // head_size
    return jnp.concatenate(
        [rows[:, head * head_size : (head + 1) * head_size] for head in range(count)], axis=0
    )


def heads_across(stacked, row_count):
    count = stacked.shape[0] // row_count
    return jnp.concatenate(
        [stacked[head * row_count : (head + 1) * row_count] for head in range(count)], axis=1
    )


def turned_heads(rows, cosine, sine):
    stacked = heads_down(rows, cosine.shape[1])
    repeats = stacked.shape[0] // rows.shape[0]
    return turned(stacked, jnp.tile(cosine, (repeats, 1)), jnp.tile(sine, (repeats, 1)))


def forward_layer(rows, gain_row, weight, cosine, sine, allowed):
    row_count, feature_count = rows.shape
    head_size = cosine.shape[1]
    scale = lax.rsqrt(jnp.sum(rows * rows, axis=1, keepdims=True) / feature_count + EPSILON)
    normed = rows * scale * gain_row
    packed = normed.astype(jnp.bfloat16)
    pair = contract(packed, weight, 1, 0)
    queries = turned_heads(normed, cosine, sine).astype(jnp.bfloat16)
    keys = turned(pair[:, :head_size], cosine, sine).astype(jnp.bfloat16)
    values = pair[:, head_size:].astype(jnp.bfloat16)
    scores = contract(keys, queries, 1, 1) * head_size ** (-0.5)
    scores = jnp.where(allowed, scores, NEGATIVE)
    raised = jnp.exp(scores - jnp.max(scores, axis=0, keepdims=True))
    weights = raised / jnp.sum(raised, axis=0, keepdims=True)
    mixed = contract(weights.astype(jnp.bfloat16), values, 0, 0)
    kept = (scale, keys, values, weights)
    return rows + heads_across(mixed, row_count), packed, kept


def backward_layer(upstream, rows, gain_row, weight, cosine, sine, kept):
    scale, keys, values, weights = kept
    row_count, feature_count = rows.shape
    head_size = cosine.shape[1]
    queries = turned_heads(rows * scale * gain_row, cosine, sine).astype(jnp.bfloat16)
    stacked = heads_down(upstream, head_size).astype(jnp.bfloat16)
    d_weights = contract(values, stacked, 1, 1).astype(jnp.bfloat16).astype(jnp.float32)
    d_values = contract(weights.astype(jnp.bfloat16), stacked, 1, 0)
    d_scores = weights * (d_weights - jnp.sum(d_weights * weights, axis=0, keepdims=True))
    d_scores = (d_scores * head_size ** (-0.5)).astype(jnp.bfloat16)
    d_keys = contract(d_scores, queries, 1, 0)
    terms = jnp.concatenate([turned(d_keys, cosine, -sine), d_values], axis=1)
    terms = terms.astype(jnp.bfloat16)
    d_queries = contract(d_scores, keys, 0, 0)
    repeats = stacked.shape[0] // row_count
    d_queries = turned(d_queries, jnp.tile(cosine, (repeats, 1)), jnp.tile(-sine, (repeats, 1)))
    d_normed = contract(terms, weight, 1, 1) + heads_across(d_queries, row_count)
    scaled = d_normed * gain_row
    inner = jnp.sum(scaled * rows, axis=1, keepdims=True) / feature_count
    return upstream + scale * scaled - rows * (scale * scale * scale * inner), terms


def state_width(feature_count, head_size):
    return feature_count + 4 * head_size


def save_layer(index, rows, kept, state_ref):
    scale, keys, values, weights = kept
    feature_count, head_size = rows.shape[1], keys.shape[1]
    state_ref[index, :, :feature_count] = rows
    parts = (weights, keys, values, jnp.broadcast_to(scale, keys.shape))
    for place, part in enumerate(parts):
        start = feature_count + place * head_size
        state_ref[index, :, start : start + head_size] = part.astype(jnp.float32)


def load_layer(index, state_ref, feature_count):
    head_size = (state_ref.shape[2] - feature_count) // 4
    parts = []
    for place in range(4):
        start = feature_count + place * head_size
        parts.append(state_ref[index, :, start : start + head_size])
    weights, keys, values, scale = parts
    kept = (scale[:, 0:1], keys.astype(jnp.bfloat16), values.astype(jnp.bfloat16), weights)
    return state_ref[index, :, :feature_count], kept


def repeat_steps(count, step, carry):
    if count <= 8:
        for index in range(count):
            carry = step(index, carry)
        return carry
    return lax.fori_loop(0, count, step, carry)


def layer_inputs(index, gain_ref, weight_ref, sections):
    place = lax.bitwise_xor(lax.axis_index("pipe"), index)
    groups = weight_ref.shape[0]
    share = weight_ref.shape[1] // sections
    rows = pl.ds(pl.multiple_of(place * share, share), share)
    weight = []
    for owner in range(groups):
        mask = lax.bitwise_xor(lax.axis_index("dp"), owner)
        line = lax.rem(mask, 2) * (groups // 2) + lax.div(mask, 2)
        weight.append(weight_ref[jnp.where(place == 0, owner, line), rows, :])
    return gain_ref[pl.ds(place, 1), :], jnp.concatenate(weight, axis=0)


def forward_steps(rows, gain_ref, weight_ref, tables, state_ref, packed_ref):
    cosine, sine, allowed = tables
    sections, groups = packed_ref.shape[:2]
    share = weight_ref.shape[1] // sections

    def step(index, rows):
        gain_row, weight = layer_inputs(index, gain_ref, weight_ref, sections)
        after, packed, kept = forward_layer(rows, gain_row, weight, cosine, sine, allowed)
        for group in range(groups):
            packed_ref[index, group, :, :share] = packed[:, group * share : (group + 1) * share]
        save_layer(index, rows, kept, state_ref)
        return after

    return repeat_steps(sections, step, rows)


def backward_steps(upstream, gain_ref, weight_ref, tables, state_ref, terms_ref, start):
    cosine, sine, _ = tables
    sections, groups = terms_ref.shape[:2]
    width = weight_ref.shape[2]

    def step(back, upstream):
        index = sections - 1 - back
        gain_row, weight = layer_inputs(index, gain_ref, weight_ref, sections)
        rows, kept = load_layer(index, state_ref, upstream.shape[1])
        before, terms = backward_layer(upstream, rows, gain_row, weight, cosine, sine, kept)
        for group in range(groups):
            terms_ref[index, group, :, start : start + width] = terms
        return before

    return repeat_steps(sections, step, upstream)


def fill(turn, key_ref, value_ref, shares, weight_ref, sems):
    groups, share, head_size = key_ref.shape[1:]
    moved = weight_ref.shape[1] - share
    copies = [
        (key_ref.at[turn], weight_ref.at[:, :share, :head_size]),
        (value_ref.at[turn], weight_ref.at[:, :share, head_size:]),
    ]
    for core, ref in enumerate(shares):
        lines = pl.ds(core * (groups // 2), groups // 2)
        copies.append((ref.at[:, pl.ds(0, moved)], weight_ref.at[lines, pl.ds(share, moved)]))
    copies = [
        pltpu.make_async_copy(*pair, sems.at[turn, index]) for index, pair in enumerate(copies)
    ]
    for copy in copies:
        copy.start()
    return copies


def first_kernel(
    upstream_ref,
    key_ref,
    value_ref,
    share_ref,
    other_ref,
    state_out,
    packed_ref,
    state_ref,
    lines_ref,
    rows_ref,
    gains_ref,
    gain_ref,
    line_sems,
    weight_ref,
    sems,
    *,
    doc_count
):
    sections = packed_ref.shape[0]
    groups, share, head_size = key_ref.shape[1:]
    row_count, feature_count = upstream_ref.shape
    column_count = feature_count // sections
    chips, line_count, width = lines_ref.shape[1:]
    used = share_ref.shape[1] - line_count
    section, group = lax.axis_index("pipe"), lax.axis_index("dp")
    shares = (share_ref, other_ref)
    line_copies = [
        pltpu.make_async_copy(
            ref.at[:, pl.ds(used, line_count)], lines_ref.at[core], line_sems.at[core]
        )
        for core, ref in enumerate(shares)
    ]
    for copy in line_copies:
        copy.start()
    copies = fill(0, key_ref, value_ref, shares, weight_ref, sems)
    state_ref[sections + 1, :, :feature_count] = upstream_ref[...]
    for copy in line_copies:
        copy.wait()

    row = iota((row_count, 1), 0)
    offset = row.astype(jnp.float32)
    document = jnp.zeros((row_count, 1), jnp.float32)
    position = jnp.zeros((row_count, 1), jnp.float32)
    source = jnp.zeros((row_count, 1), jnp.float32)
    parts = [jnp.zeros((row_count, column_count), jnp.float32) for _ in range(sections)]
    folded = row_count * column_count // width
    tail = folded + GAIN_LINES
    for core in range(2):
        for chip in range(chips):
            lines = lines_ref[core, chip].astype(jnp.float32)
            tags = lines[sections * tail :]
            tags = jnp.sum(
                jnp.where(iota(tags.shape, 0) == section, tags, 0.0), axis=0, keepdims=True
            )
            target = jnp.where(
                row < row_count // 2,
                tags[:, doc_count : doc_count + 1],
                tags[:, doc_count + 1 : doc_count + 2],
            )
            came = as_float(target.astype(jnp.int32) == group)
            end = jnp.zeros((1, 1), jnp.float32)
            number = jnp.zeros((row_count, 1), jnp.float32)
            opening = jnp.zeros((row_count, 1), jnp.float32)
            for doc in range(doc_count - 1):
                end = end + tags[:, doc : doc + 1]
                passed = offset >= end
                number = number + as_float(passed)
                opening = jnp.where(passed, end, opening)
            owner = lax.bitwise_xor(group, 2 * chip + core)
            document += came * number
            position += came * (offset - opening)
            source += came * owner.astype(jnp.float32)
            gain_rows = []
            for mask in range(sections):
                piece = lines[mask * tail : mask * tail + folded]
                parts[mask] += came * unfold(piece, row_count, column_count)
                terms = lines[mask * tail + folded : (mask + 1) * tail, :share]
                gain_rows += [
                    terms[3 * turn : 3 * turn + 1]
                    + terms[3 * turn + 1 : 3 * turn + 2]
                    + terms[3 * turn + 2 : 3 * turn + 3]
                    for turn in range(2)
                ]
            gains_ref[owner] = jnp.concatenate(gain_rows[0::2] + gain_rows[1::2], axis=0)
    for owner in range(groups):
        gain_ref[:, owner * share : (owner + 1) * share] = gains_ref[owner]
    for start in range(0, 2 * sections, row_count):
        state_ref[sections + 2 + start // row_count, :, :feature_count] = gain_ref[
            start : start + row_count
        ]
    for mask in range(sections):
        rows_ref[lax.bitwise_xor(section, mask)] = parts[mask]
    rows = jnp.concatenate([rows_ref[index] for index in range(sections)], axis=1)

    lane = iota((1, head_size), 1)
    middle = head_size // 2
    exponent = (lane % middle).astype(jnp.float32) * (2.0 / head_size)
    angles = position * jnp.exp(exponent * -jnp.log(jnp.float32(ROPE_BASE)))
    cosine = jnp.cos(angles)
    sine = jnp.where(lane < middle, -jnp.sin(angles), jnp.sin(angles))
    shape = (row_count, row_count * feature_count // head_size)
    pick = as_float(iota(shape, 1) % row_count == iota(shape, 0))
    document_across = jnp.sum(document * pick, axis=0, keepdims=True)
    position_across = jnp.sum(position * pick, axis=0, keepdims=True)
    allowed = (document == document_across) & (position <= position_across)
    kept = (cosine, sine, as_float(allowed), jnp.broadcast_to(source, cosine.shape))
    for place, table in enumerate(kept):
        start = feature_count + place * head_size
        state_ref[sections, :, start : start + head_size] = table
    tables = (cosine, sine, allowed)
    for copy in copies:
        copy.wait()
    state_ref[sections, :, :feature_count] = forward_steps(
        rows, gain_ref.at[pl.ds(0, sections)], weight_ref, tables, state_ref, packed_ref
    )
    state_copy = pltpu.make_async_copy(state_ref, state_out, line_sems.at[2])
    state_copy.start()
    state_copy.wait()


def second_kernel(
    state_in,
    key_ref,
    value_ref,
    share_ref,
    other_ref,
    late_share_ref,
    late_other_ref,
    out_ref,
    first_ref,
    state_ref,
    gain_ref,
    state_sem,
    late_weight_ref,
    weight_ref,
    sems
):
    state_copy = pltpu.make_async_copy(state_in, first_ref, state_sem.at[0])
    state_copy.start()
    sections, groups, row_count, _ = out_ref.shape
    share, head_size = key_ref.shape[2:]
    feature_count, term_width = groups * share, 2 * head_size
    late_shares = (late_share_ref, late_other_ref)
    late_copies = fill(1, key_ref, value_ref, late_shares, late_weight_ref, sems)
    copies = fill(0, key_ref, value_ref, (share_ref, other_ref), weight_ref, sems)
    state_copy.wait()
    kept = []
    for place in range(4):
        start = feature_count + place * head_size
        kept.append(first_ref[sections, :, start : start + head_size])
    cosine, sine, allowed, source = kept
    tables = (cosine, sine, allowed > 0.5)
    for start in range(0, 2 * sections, row_count):
        gain_ref[start : start + row_count] = first_ref[
            sections + 2 + start // row_count, :, :feature_count
        ]
    late_gain = gain_ref.at[pl.ds(sections, sections)]
    for copy in late_copies:
        copy.wait()
    forward_steps(
        first_ref[sections, :, :feature_count],
        late_gain,
        late_weight_ref,
        tables,
        state_ref,
        out_ref,
    )
    upstream = backward_steps(
        first_ref[sections + 1, :, :feature_count],
        late_gain,
        late_weight_ref,
        tables,
        state_ref,
        out_ref,
        share + term_width,
    )
    for copy in copies:
        copy.wait()
    grads = backward_steps(
        upstream,
        gain_ref.at[pl.ds(0, sections)],
        weight_ref,
        tables,
        first_ref,
        out_ref,
        share,
    ).astype(jnp.bfloat16)
    column_count = feature_count // sections
    pieces = pieces_of(column_count)
    width = column_count // pieces
    chosen = choosers(source[:, 0:1], groups, pieces)
    for section in range(sections):
        start = section * column_count
        going = contract(chosen[0], grads[:, start : start + width], 0, 0)
        for piece in range(1, pieces):
            left = start + piece * width
            going += contract(chosen[piece], grads[:, left : left + width], 0, 0)
        going = going.astype(jnp.bfloat16)
        for group in range(groups):
            out_ref[section, group, :, share + 2 * term_width :] = going[
                group * row_count : (group + 1) * row_count
            ]


def last_kernel(
    route_ref, first_ref, late_ref, grad_ref, key_ref, value_ref, *, groups
):
    micro_count = route_ref.shape[0]
    source_rows, column_count = grad_ref.shape
    row_count = source_rows // micro_count
    half = row_count // 2
    share, head_size = key_ref.shape[1:]
    term_width = 2 * head_size
    width = late_ref.shape[1] - share - 2 * term_width
    pieces = column_count // width
    for index, packed in enumerate((first_ref[...], late_ref[:, :share])):
        start = share + index * term_width
        total = contract(packed, late_ref[:, start : start + term_width], 0, 0)
        key_ref[index] = total[:, :head_size]
        value_ref[index] = total[:, head_size:]
    shape = (source_rows, late_ref.shape[0])
    row, source = iota(shape, 1), iota(shape, 0)
    slot = source // half
    target = jnp.full(shape, -1, jnp.int32)
    for micro in range(micro_count):
        for side in range(2):
            target = jnp.where(
                slot == 2 * micro + side, micro * groups + route_ref[micro, side], target
            )
    going = target == row // row_count
    inner, wanted = row % row_count, source % half
    for piece in range(pieces):
        chosen = as_float(going & (inner == piece * half + wanted)).astype(jnp.bfloat16)
        grad_ref[:, piece * width : (piece + 1) * width] = contract(
            chosen, late_ref[:, share + 2 * term_width :], 1, 0
        ).astype(jnp.bfloat16)


def call(kernel, outs, operands, scalars=0, whole=0, any_outs=0, scratch=(), vmem_bytes=0, cost=0):
    spaces = [pltpu.SMEM] * scalars + [pltpu.VMEM] * (len(operands) - scalars - whole)
    spaces += [pl.ANY] * whole
    return pl.pallas_call(
        kernel,
        out_shape=outs,
        in_specs=[pl.BlockSpec(memory_space=space) for space in spaces],
        out_specs=[
            pl.BlockSpec(memory_space=pl.ANY if place < any_outs else pltpu.VMEM)
            for place in range(len(outs))
        ],
        scratch_shapes=scratch,
        compiler_params=pltpu.CompilerParams(vmem_limit_bytes=vmem_bytes),
        cost_estimate=pl.CostEstimate(flops=0, bytes_accessed=cost, transcendentals=0),
    )(*operands)


def exchange(blocks):
    return lax.all_to_all(blocks, ("pipe", "dp"), split_axis=0, concat_axis=0, tiled=True)


def swapped(value, axis, mask):
    pairs = [(source, source ^ mask) for source in range(lax.axis_size(axis))]
    return lax.ppermute(value, axis, pairs)


def direct_pieces(payload, sections):
    masks = [mask for mask in range(1, sections) if mask & (mask - 1) == 0]
    return {mask: swapped(payload, "pipe", mask) for mask in masks}


def relayed_pieces(pieces, sections):
    pieces = dict(pieces)
    for mask in range(1, sections):
        low = mask & -mask
        if mask != low:
            pieces[mask] = swapped(pieces[mask - low], "pipe", low)
    return [pieces[mask] for mask in range(1, sections)]


def body(hidden, lengths, route, gain, key_weight, value_weight, cotangent):
    groups = lax.axis_size("dp")
    sections = lax.axis_size("pipe")
    group_index = lax.axis_index("dp")
    section_index = lax.axis_index("pipe")
    micro_count = lengths.shape[0]
    assert micro_count == sections
    source_rows, column_count = hidden.shape
    row_count = source_rows // micro_count
    feature_count = gain.shape[1]
    head_size = key_weight.shape[2]
    assert row_count * feature_count == head_size * head_size
    share = feature_count // groups
    width = column_count // pieces_of(column_count)
    devices = sections * groups

    line_width = 2 * head_size

    def share_of(turn, owner, arrays):
        parts = [
            lax.dynamic_slice(array, (turn, owner * share, 0), (1, share, head_size))[0]
            for array in arrays
        ]
        return jnp.concatenate(parts, axis=1)

    def own_rows(mask):
        start = lax.bitwise_xor(section_index, mask) * row_count
        rows = lax.dynamic_slice(hidden, (start, 0), (row_count, column_count))
        return fold(rows, line_width)

    slice_ = lax.dynamic_slice(gain, (0, group_index * share), (2, share))
    high = lax.reduce_precision(slice_, 8, 7)
    middle = lax.reduce_precision(slice_ - high, 8, 7)
    terms = jnp.stack([high, middle, slice_ - high - middle], axis=1).reshape(6, share)
    terms = jnp.pad(
        terms.astype(jnp.bfloat16), ((0, GAIN_LINES - 6), (0, line_width - share))
    )

    first = share_of(0, group_index, (key_weight, value_weight))
    came = [
        swapped(jnp.concatenate([first, own_rows(mask), terms], axis=0), "pipe", mask)
        for mask in range(1, sections)
    ]
    tags = jnp.concatenate([lengths, route], axis=1).astype(jnp.bfloat16)
    tags = jnp.pad(tags, ((0, -micro_count % 16), (0, line_width - tags.shape[1])))
    upstream = lax.dynamic_slice_in_dim(
        cotangent, section_index * row_count, row_count, 0
    ).astype(jnp.float32)
    tags, own_tail, upstream = lax.optimization_barrier(
        (tags, jnp.concatenate([own_rows(0), terms], axis=0), upstream)
    )
    _, *arrays = lax.optimization_barrier((tags, key_weight, value_weight))
    column = jnp.concatenate(
        [piece[:share] for piece in came]
        + [own_tail]
        + [piece[share:] for piece in came]
        + [tags],
        axis=0,
    )
    distant = share_of(1, lax.bitwise_xor(group_index, groups - 2), arrays)
    column, second, distant = lax.optimization_barrier(
        (column, share_of(1, group_index, arrays), distant)
    )
    chips = range(1, groups // 2)
    plane = jnp.stack([column] + [swapped(column, "dp", 2 * chip) for chip in chips])
    came = direct_pieces(second, sections)
    came[sections // 2], distant = lax.optimization_barrier((came[sections // 2], distant))
    came = relayed_pieces(came, sections)
    far = swapped(distant, "pipe", sections // 2)
    plane, came, far, distant = lax.optimization_barrier((plane, came, far, distant))
    first_shares = (plane, swapped(plane, "dp", 1))
    column = jnp.concatenate(came, axis=0)
    planes = [column] + [swapped(column, "dp", 2 * chip) for chip in chips[:-1]]
    far = relayed_pieces({**direct_pieces(distant, sections // 2), sections // 2: far}, sections)

    key_parts = key_weight.reshape(2, groups, share, head_size)
    value_parts = value_weight.reshape(2, groups, share, head_size)

    def layers_call(kernel, turns, outs, operands, shares, scratch, cost, vmem_bytes, whole, any_outs):
        weight = pltpu.VMEM((groups, sections * share, line_width), jnp.bfloat16)
        return call(
            kernel,
            outs,
            (*operands, key_parts, value_parts, *shares),
            whole=2 + len(shares) + whole,
            any_outs=any_outs,
            scratch=[
                *scratch,
                *[weight] * turns,
                pltpu.SemaphoreType.DMA((2, 4)),
            ],
            vmem_bytes=vmem_bytes,
            cost=cost,
        )

    def blocks_shape(columns):
        return jax.ShapeDtypeStruct((sections, groups, row_count, columns), jnp.bfloat16)

    def exchanged(blocks):
        columns = blocks.shape[3]
        got = exchange(blocks.reshape(devices, row_count, columns))
        return got.reshape(devices * row_count, columns)

    line = (row_count, state_width(feature_count, head_size))
    line_count = plane.shape[1] - (sections - 1) * share
    gain_scratch = pltpu.VMEM((2 * sections, feature_count), jnp.float32)
    state_shape = (sections + 2 + 2 * sections // row_count, *line)
    state, packed = layers_call(
        functools.partial(first_kernel, doc_count=lengths.shape[1]),
        1,
        [jax.ShapeDtypeStruct(state_shape, jnp.float32), blocks_shape(share)],
        (upstream,),
        first_shares,
        (
            pltpu.VMEM(state_shape, jnp.float32),
            pltpu.VMEM((2, groups // 2, line_count, line_width), jnp.bfloat16),
            pltpu.VMEM((sections, row_count, column_count), jnp.float32),
            pltpu.VMEM((groups, 2 * sections, share), jnp.float32),
            gain_scratch,
            pltpu.SemaphoreType.DMA((3,)),
        ),
        18 << 20,
        (8 << 20) + sections * feature_count * 2 * line_width + 1024 * devices * row_count,
        0,
        1,
    )
    state, planes, far = lax.optimization_barrier((state, planes, far))
    plane = jnp.stack(planes + [jnp.concatenate(far, axis=0)])
    plane, packed = lax.optimization_barrier((plane, packed))
    packed = exchanged(packed)
    second_shares = (plane, swapped(plane, "dp", 1))
    columns = share + 4 * head_size + width
    (late,) = layers_call(
        second_kernel,
        2,
        [blocks_shape(columns)],
        (state,),
        (*first_shares, *second_shares),
        (
            pltpu.VMEM(state_shape, jnp.float32),
            pltpu.VMEM((sections, *line), jnp.float32),
            gain_scratch,
            pltpu.SemaphoreType.DMA((1,)),
        ),
        48 << 20,
        50 << 20,
        1,
        0,
    )
    late, packed = lax.optimization_barrier((late, packed))
    late = exchanged(late)
    grad_shape = jax.ShapeDtypeStruct((2, share, head_size), jnp.float32)
    return tuple(
        call(
            functools.partial(last_kernel, groups=groups),
            [jax.ShapeDtypeStruct((source_rows, column_count), jnp.bfloat16)] + [grad_shape] * 2,
            (route, packed, late),
            scalars=1,
            vmem_bytes=(4 << 20) + 10000 * devices * row_count,
        )
    )


def solution(mesh):
    placed = (
        P("dp", "pipe"),
        P("dp", None),
        P("dp", None),
        P("pipe", None),
        P("pipe", None, None),
        P("pipe", None, None),
        P("dp", None),
    )
    return jax.shard_map(
        body,
        mesh=mesh,
        in_specs=placed,
        out_specs=(P("dp", "pipe"), P("pipe", "dp", None), P("pipe", "dp", None)),
        check_vma=False,
    )
```

```python
import functools

import jax
import jax.numpy as jnp
from jax import lax
from jax.experimental import pallas as pl
from jax.experimental.pallas import tpu as pltpu
from jax.sharding import PartitionSpec as P

ROPE_BASE = 500000.0
EPSILON = 1e-05
NEGATIVE = -1e30
LANES = 128
GAIN_LINES = 8


def iota(shape, dim):
    return lax.broadcasted_iota(jnp.int32, shape, dim)


def as_float(flags):
    return jnp.where(flags, 1.0, 0.0).astype(jnp.float32)


def contract(left, right, left_dim, right_dim):
    return lax.dot_general(
        left, right, (((left_dim,), (right_dim,)), ((), ())), preferred_element_type=jnp.float32
    )


def pieces_of(column_count):
    return 2 if column_count % (2 * LANES) == 0 else 1


def fold(rows, width):
    row_count, columns = rows.shape
    if columns >= width:
        return jnp.concatenate(
            [rows[:, start : start + width] for start in range(0, columns, width)], axis=0
        )
    lines = row_count * columns // width
    return jnp.concatenate(
        [rows[start : start + lines] for start in range(0, row_count, lines)], axis=1
    )


def unfold(lines, row_count, columns):
    width = lines.shape[1]
    if columns >= width:
        return jnp.concatenate(
            [lines[start : start + row_count] for start in range(0, lines.shape[0], row_count)],
            axis=1,
        )
    return jnp.concatenate(
        [lines[:, start : start + columns] for start in range(0, width, columns)], axis=0
    )


def choosers(source, groups, pieces):
    row_count = source.shape[0]
    half = row_count // 2
    shape = (row_count, groups * row_count)
    row, line = iota(shape, 0), iota(shape, 1)
    back = source.astype(jnp.int32) == line // row_count
    return [
        as_float(back & (line % row_count == piece * half + row % half)).astype(jnp.bfloat16)
        for piece in range(pieces)
    ]


def turned(vector, cosine, sine):
    return vector * cosine + pltpu.roll(vector, vector.shape[1] // 2, 1) * sine


def heads_down(rows, head_size):
    count = rows.shape[1] // head_size
    return jnp.concatenate(
        [rows[:, head * head_size : (head + 1) * head_size] for head in range(count)], axis=0
    )


def heads_across(stacked, row_count):
    count = stacked.shape[0] // row_count
    return jnp.concatenate(
        [stacked[head * row_count : (head + 1) * row_count] for head in range(count)], axis=1
    )


def turned_heads(rows, cosine, sine):
    stacked = heads_down(rows, cosine.shape[1])
    repeats = stacked.shape[0] // rows.shape[0]
    return turned(stacked, jnp.tile(cosine, (repeats, 1)), jnp.tile(sine, (repeats, 1)))


def forward_layer(rows, gain_row, weight, cosine, sine, allowed):
    row_count, feature_count = rows.shape
    head_size = cosine.shape[1]
    scale = lax.rsqrt(jnp.sum(rows * rows, axis=1, keepdims=True) / feature_count + EPSILON)
    normed = rows * scale * gain_row
    packed = normed.astype(jnp.bfloat16)
    pair = contract(packed, weight, 1, 0)
    queries = turned_heads(normed, cosine, sine).astype(jnp.bfloat16)
    keys = turned(pair[:, :head_size], cosine, sine).astype(jnp.bfloat16)
    values = pair[:, head_size:].astype(jnp.bfloat16)
    scores = contract(keys, queries, 1, 1) * head_size ** (-0.5)
    scores = jnp.where(allowed, scores, NEGATIVE)
    raised = jnp.exp(scores - jnp.max(scores, axis=0, keepdims=True))
    weights = raised / jnp.sum(raised, axis=0, keepdims=True)
    mixed = contract(weights.astype(jnp.bfloat16), values, 0, 0)
    kept = (scale, keys, values, weights)
    return rows + heads_across(mixed, row_count), packed, kept


def backward_layer(upstream, rows, gain_row, weight, cosine, sine, kept):
    scale, keys, values, weights = kept
    row_count, feature_count = rows.shape
    head_size = cosine.shape[1]
    queries = turned_heads(rows * scale * gain_row, cosine, sine).astype(jnp.bfloat16)
    stacked = heads_down(upstream, head_size).astype(jnp.bfloat16)
    d_weights = contract(values, stacked, 1, 1).astype(jnp.bfloat16).astype(jnp.float32)
    d_values = contract(weights.astype(jnp.bfloat16), stacked, 1, 0)
    d_scores = weights * (d_weights - jnp.sum(d_weights * weights, axis=0, keepdims=True))
    d_scores = (d_scores * head_size ** (-0.5)).astype(jnp.bfloat16)
    d_keys = contract(d_scores, queries, 1, 0)
    terms = jnp.concatenate([turned(d_keys, cosine, -sine), d_values], axis=1)
    terms = terms.astype(jnp.bfloat16)
    d_queries = contract(d_scores, keys, 0, 0)
    repeats = stacked.shape[0] // row_count
    d_queries = turned(d_queries, jnp.tile(cosine, (repeats, 1)), jnp.tile(-sine, (repeats, 1)))
    d_normed = contract(terms, weight, 1, 1) + heads_across(d_queries, row_count)
    scaled = d_normed * gain_row
    inner = jnp.sum(scaled * rows, axis=1, keepdims=True) / feature_count
    return upstream + scale * scaled - rows * (scale * scale * scale * inner), terms


def state_width(feature_count, head_size):
    return feature_count + 4 * head_size


def save_layer(index, rows, kept, state_ref):
    scale, keys, values, weights = kept
    feature_count, head_size = rows.shape[1], keys.shape[1]
    state_ref[index, :, :feature_count] = rows
    parts = (weights, keys, values, jnp.broadcast_to(scale, keys.shape))
    for place, part in enumerate(parts):
        start = feature_count + place * head_size
        state_ref[index, :, start : start + head_size] = part.astype(jnp.float32)


def load_layer(index, state_ref, feature_count):
    head_size = (state_ref.shape[2] - feature_count) // 4
    parts = []
    for place in range(4):
        start = feature_count + place * head_size
        parts.append(state_ref[index, :, start : start + head_size])
    weights, keys, values, scale = parts
    kept = (scale[:, 0:1], keys.astype(jnp.bfloat16), values.astype(jnp.bfloat16), weights)
    return state_ref[index, :, :feature_count], kept


def repeat_steps(count, step, carry):
    if count <= 8:
        for index in range(count):
            carry = step(index, carry)
        return carry
    return lax.fori_loop(0, count, step, carry)


def layer_inputs(index, gain_ref, weight_ref, sections):
    place = lax.bitwise_xor(lax.axis_index("pipe"), index)
    groups = weight_ref.shape[0]
    share = weight_ref.shape[1] // sections
    rows = pl.ds(pl.multiple_of(place * share, share), share)
    weight = []
    for owner in range(groups):
        mask = lax.bitwise_xor(lax.axis_index("dp"), owner)
        line = lax.rem(mask, 2) * (groups // 2) + lax.div(mask, 2)
        weight.append(weight_ref[jnp.where(place == 0, owner, line), rows, :])
    return gain_ref[pl.ds(place, 1), :], jnp.concatenate(weight, axis=0)


def forward_steps(rows, gain_ref, weight_ref, tables, state_ref, packed_ref):
    cosine, sine, allowed = tables
    sections, groups = packed_ref.shape[:2]
    share = weight_ref.shape[1] // sections

    def step(index, rows):
        gain_row, weight = layer_inputs(index, gain_ref, weight_ref, sections)
        after, packed, kept = forward_layer(rows, gain_row, weight, cosine, sine, allowed)
        for group in range(groups):
            packed_ref[index, group, :, :share] = packed[:, group * share : (group + 1) * share]
        save_layer(index, rows, kept, state_ref)
        return after

    return repeat_steps(sections, step, rows)


def backward_steps(upstream, gain_ref, weight_ref, tables, state_ref, terms_ref, start):
    cosine, sine, _ = tables
    sections, groups = terms_ref.shape[:2]
    width = weight_ref.shape[2]

    def step(back, upstream):
        index = sections - 1 - back
        gain_row, weight = layer_inputs(index, gain_ref, weight_ref, sections)
        rows, kept = load_layer(index, state_ref, upstream.shape[1])
        before, terms = backward_layer(upstream, rows, gain_row, weight, cosine, sine, kept)
        for group in range(groups):
            terms_ref[index, group, :, start : start + width] = terms
        return before

    return repeat_steps(sections, step, upstream)


def fill(turn, key_ref, value_ref, shares, weight_ref, sems):
    groups, share, head_size = key_ref.shape[1:]
    moved = weight_ref.shape[1] - share
    copies = [
        (key_ref.at[turn], weight_ref.at[:, :share, :head_size]),
        (value_ref.at[turn], weight_ref.at[:, :share, head_size:]),
    ]
    for core, ref in enumerate(shares):
        lines = pl.ds(core * (groups // 2), groups // 2)
        copies.append((ref.at[:, pl.ds(0, moved)], weight_ref.at[lines, pl.ds(share, moved)]))
    copies = [
        pltpu.make_async_copy(*pair, sems.at[turn, index]) for index, pair in enumerate(copies)
    ]
    for copy in copies:
        copy.start()
    return copies


def first_kernel(
    upstream_ref,
    key_ref,
    value_ref,
    share_ref,
    other_ref,
    state_out,
    packed_ref,
    state_ref,
    lines_ref,
    rows_ref,
    gains_ref,
    gain_ref,
    line_sems,
    weight_ref,
    sems,
    *,
    doc_count
):
    sections = packed_ref.shape[0]
    groups, share, head_size = key_ref.shape[1:]
    row_count, feature_count = upstream_ref.shape
    column_count = feature_count // sections
    chips, line_count, width = lines_ref.shape[1:]
    used = share_ref.shape[1] - line_count
    section, group = lax.axis_index("pipe"), lax.axis_index("dp")
    shares = (share_ref, other_ref)
    line_copies = [
        pltpu.make_async_copy(
            ref.at[:, pl.ds(used, line_count)], lines_ref.at[core], line_sems.at[core]
        )
        for core, ref in enumerate(shares)
    ]
    for copy in line_copies:
        copy.start()
    copies = fill(0, key_ref, value_ref, shares, weight_ref, sems)
    state_ref[sections + 1, :, :feature_count] = upstream_ref[...]
    for copy in line_copies:
        copy.wait()

    row = iota((row_count, 1), 0)
    offset = row.astype(jnp.float32)
    document = jnp.zeros((row_count, 1), jnp.float32)
    position = jnp.zeros((row_count, 1), jnp.float32)
    source = jnp.zeros((row_count, 1), jnp.float32)
    parts = [jnp.zeros((row_count, column_count), jnp.float32) for _ in range(sections)]
    folded = row_count * column_count // width
    tail = folded + GAIN_LINES
    for core in range(2):
        for chip in range(chips):
            lines = lines_ref[core, chip].astype(jnp.float32)
            tags = lines[sections * tail :]
            tags = jnp.sum(
                jnp.where(iota(tags.shape, 0) == section, tags, 0.0), axis=0, keepdims=True
            )
            target = jnp.where(
                row < row_count // 2,
                tags[:, doc_count : doc_count + 1],
                tags[:, doc_count + 1 : doc_count + 2],
            )
            came = as_float(target.astype(jnp.int32) == group)
            end = jnp.zeros((1, 1), jnp.float32)
            number = jnp.zeros((row_count, 1), jnp.float32)
            opening = jnp.zeros((row_count, 1), jnp.float32)
            for doc in range(doc_count - 1):
                end = end + tags[:, doc : doc + 1]
                passed = offset >= end
                number = number + as_float(passed)
                opening = jnp.where(passed, end, opening)
            owner = lax.bitwise_xor(group, 2 * chip + core)
            document += came * number
            position += came * (offset - opening)
            source += came * owner.astype(jnp.float32)
            gain_rows = []
            for mask in range(sections):
                piece = lines[mask * tail : mask * tail + folded]
                parts[mask] += came * unfold(piece, row_count, column_count)
                terms = lines[mask * tail + folded : (mask + 1) * tail, :share]
                gain_rows += [
                    terms[3 * turn : 3 * turn + 1]
                    + terms[3 * turn + 1 : 3 * turn + 2]
                    + terms[3 * turn + 2 : 3 * turn + 3]
                    for turn in range(2)
                ]
            gains_ref[owner] = jnp.concatenate(gain_rows[0::2] + gain_rows[1::2], axis=0)
    for owner in range(groups):
        gain_ref[:, owner * share : (owner + 1) * share] = gains_ref[owner]
    for start in range(0, 2 * sections, row_count):
        state_ref[sections + 2 + start // row_count, :, :feature_count] = gain_ref[
            start : start + row_count
        ]
    for mask in range(sections):
        rows_ref[lax.bitwise_xor(section, mask)] = parts[mask]
    rows = jnp.concatenate([rows_ref[index] for index in range(sections)], axis=1)

    lane = iota((1, head_size), 1)
    middle = head_size // 2
    exponent = (lane % middle).astype(jnp.float32) * (2.0 / head_size)
    angles = position * jnp.exp(exponent * -jnp.log(jnp.float32(ROPE_BASE)))
    cosine = jnp.cos(angles)
    sine = jnp.where(lane < middle, -jnp.sin(angles), jnp.sin(angles))
    shape = (row_count, row_count * feature_count // head_size)
    pick = as_float(iota(shape, 1) % row_count == iota(shape, 0))
    document_across = jnp.sum(document * pick, axis=0, keepdims=True)
    position_across = jnp.sum(position * pick, axis=0, keepdims=True)
    allowed = (document == document_across) & (position <= position_across)
    kept = (cosine, sine, as_float(allowed), jnp.broadcast_to(source, cosine.shape))
    for place, table in enumerate(kept):
        start = feature_count + place * head_size
        state_ref[sections, :, start : start + head_size] = table
    tables = (cosine, sine, allowed)
    for copy in copies:
        copy.wait()
    state_ref[sections, :, :feature_count] = forward_steps(
        rows, gain_ref.at[pl.ds(0, sections)], weight_ref, tables, state_ref, packed_ref
    )
    state_copy = pltpu.make_async_copy(state_ref, state_out, line_sems.at[2])
    state_copy.start()
    state_copy.wait()


def second_kernel(
    state_in,
    key_ref,
    value_ref,
    share_ref,
    other_ref,
    late_share_ref,
    late_other_ref,
    out_ref,
    first_ref,
    state_ref,
    gain_ref,
    state_sem,
    late_weight_ref,
    weight_ref,
    sems
):
    state_copy = pltpu.make_async_copy(state_in, first_ref, state_sem.at[0])
    state_copy.start()
    sections, groups, row_count, _ = out_ref.shape
    share, head_size = key_ref.shape[2:]
    feature_count, term_width = groups * share, 2 * head_size
    late_shares = (late_share_ref, late_other_ref)
    late_copies = fill(1, key_ref, value_ref, late_shares, late_weight_ref, sems)
    copies = fill(0, key_ref, value_ref, (share_ref, other_ref), weight_ref, sems)
    state_copy.wait()
    kept = []
    for place in range(4):
        start = feature_count + place * head_size
        kept.append(first_ref[sections, :, start : start + head_size])
    cosine, sine, allowed, source = kept
    tables = (cosine, sine, allowed > 0.5)
    for start in range(0, 2 * sections, row_count):
        gain_ref[start : start + row_count] = first_ref[
            sections + 2 + start // row_count, :, :feature_count
        ]
    late_gain = gain_ref.at[pl.ds(sections, sections)]
    for copy in late_copies:
        copy.wait()
    forward_steps(
        first_ref[sections, :, :feature_count],
        late_gain,
        late_weight_ref,
        tables,
        state_ref,
        out_ref,
    )
    upstream = backward_steps(
        first_ref[sections + 1, :, :feature_count],
        late_gain,
        late_weight_ref,
        tables,
        state_ref,
        out_ref,
        share + term_width,
    )
    for copy in copies:
        copy.wait()
    grads = backward_steps(
        upstream,
        gain_ref.at[pl.ds(0, sections)],
        weight_ref,
        tables,
        first_ref,
        out_ref,
        share,
    ).astype(jnp.bfloat16)
    column_count = feature_count // sections
    pieces = pieces_of(column_count)
    width = column_count // pieces
    chosen = choosers(source[:, 0:1], groups, pieces)
    for section in range(sections):
        start = section * column_count
        going = contract(chosen[0], grads[:, start : start + width], 0, 0)
        for piece in range(1, pieces):
            left = start + piece * width
            going += contract(chosen[piece], grads[:, left : left + width], 0, 0)
        going = going.astype(jnp.bfloat16)
        for group in range(groups):
            out_ref[section, group, :, share + 2 * term_width :] = going[
                group * row_count : (group + 1) * row_count
            ]


def last_kernel(
    route_ref, first_ref, late_ref, grad_ref, key_ref, value_ref, *, groups
):
    micro_count = route_ref.shape[0]
    source_rows, column_count = grad_ref.shape
    row_count = source_rows // micro_count
    half = row_count // 2
    share, head_size = key_ref.shape[1:]
    term_width = 2 * head_size
    width = late_ref.shape[1] - share - 2 * term_width
    pieces = column_count // width
    for index, packed in enumerate((first_ref[...], late_ref[:, :share])):
        start = share + index * term_width
        total = contract(packed, late_ref[:, start : start + term_width], 0, 0)
        key_ref[index] = total[:, :head_size]
        value_ref[index] = total[:, head_size:]
    shape = (source_rows, late_ref.shape[0])
    row, source = iota(shape, 1), iota(shape, 0)
    slot = source // half
    target = jnp.full(shape, -1, jnp.int32)
    for micro in range(micro_count):
        for side in range(2):
            target = jnp.where(
                slot == 2 * micro + side, micro * groups + route_ref[micro, side], target
            )
    going = target == row // row_count
    inner, wanted = row % row_count, source % half
    for piece in range(pieces):
        chosen = as_float(going & (inner == piece * half + wanted)).astype(jnp.bfloat16)
        grad_ref[:, piece * width : (piece + 1) * width] = contract(
            chosen, late_ref[:, share + 2 * term_width :], 1, 0
        ).astype(jnp.bfloat16)


def call(kernel, outs, operands, scalars=0, whole=0, any_outs=0, scratch=(), vmem_bytes=0, cost=0):
    spaces = [pltpu.SMEM] * scalars + [pltpu.VMEM] * (len(operands) - scalars - whole)
    spaces += [pl.ANY] * whole
    return pl.pallas_call(
        kernel,
        out_shape=outs,
        in_specs=[pl.BlockSpec(memory_space=space) for space in spaces],
        out_specs=[
            pl.BlockSpec(memory_space=pl.ANY if place < any_outs else pltpu.VMEM)
            for place in range(len(outs))
        ],
        scratch_shapes=scratch,
        compiler_params=pltpu.CompilerParams(vmem_limit_bytes=vmem_bytes),
        cost_estimate=pl.CostEstimate(flops=0, bytes_accessed=cost, transcendentals=0),
    )(*operands)


def exchange(blocks):
    return lax.all_to_all(blocks, ("pipe", "dp"), split_axis=0, concat_axis=0, tiled=True)


def swapped(value, axis, mask):
    pairs = [(source, source ^ mask) for source in range(lax.axis_size(axis))]
    return lax.ppermute(value, axis, pairs)


def direct_pieces(payload, sections):
    masks = [mask for mask in range(1, sections) if mask & (mask - 1) == 0]
    return {mask: swapped(payload, "pipe", mask) for mask in masks}


def relayed_pieces(pieces, sections):
    pieces = dict(pieces)
    for mask in range(1, sections):
        low = mask & -mask
        if mask != low:
            pieces[mask] = swapped(pieces[mask - low], "pipe", low)
    return [pieces[mask] for mask in range(1, sections)]


def body(hidden, lengths, route, gain, key_weight, value_weight, cotangent):
    groups = lax.axis_size("dp")
    sections = lax.axis_size("pipe")
    group_index = lax.axis_index("dp")
    section_index = lax.axis_index("pipe")
    micro_count = lengths.shape[0]
    assert micro_count == sections
    source_rows, column_count = hidden.shape
    row_count = source_rows // micro_count
    feature_count = gain.shape[1]
    head_size = key_weight.shape[2]
    assert row_count * feature_count == head_size * head_size
    share = feature_count // groups
    width = column_count // pieces_of(column_count)
    devices = sections * groups

    line_width = 2 * head_size

    def share_of(turn, owner, arrays):
        parts = [
            lax.dynamic_slice(array, (turn, owner * share, 0), (1, share, head_size))[0]
            for array in arrays
        ]
        return jnp.concatenate(parts, axis=1)

    def own_rows(mask):
        start = lax.bitwise_xor(section_index, mask) * row_count
        rows = lax.dynamic_slice(hidden, (start, 0), (row_count, column_count))
        return fold(rows, line_width)

    slice_ = lax.dynamic_slice(gain, (0, group_index * share), (2, share))
    high = lax.reduce_precision(slice_, 8, 7)
    middle = lax.reduce_precision(slice_ - high, 8, 7)
    terms = jnp.stack([high, middle, slice_ - high - middle], axis=1).reshape(6, share)
    terms = jnp.pad(
        terms.astype(jnp.bfloat16), ((0, GAIN_LINES - 6), (0, line_width - share))
    )

    first = share_of(0, group_index, (key_weight, value_weight))
    came = [
        swapped(jnp.concatenate([first, own_rows(mask), terms], axis=0), "pipe", mask)
        for mask in range(1, sections)
    ]
    tags = jnp.concatenate([lengths, route], axis=1).astype(jnp.bfloat16)
    tags = jnp.pad(tags, ((0, -micro_count % 16), (0, line_width - tags.shape[1])))
    upstream = lax.dynamic_slice_in_dim(
        cotangent, section_index * row_count, row_count, 0
    ).astype(jnp.float32)
    tags, own_tail, upstream = lax.optimization_barrier(
        (tags, jnp.concatenate([own_rows(0), terms], axis=0), upstream)
    )
    _, *arrays = lax.optimization_barrier((tags, key_weight, value_weight))
    column = jnp.concatenate(
        [piece[:share] for piece in came]
        + [own_tail]
        + [piece[share:] for piece in came]
        + [tags],
        axis=0,
    )
    distant = share_of(1, lax.bitwise_xor(group_index, groups - 2), arrays)
    column, second, distant = lax.optimization_barrier(
        (column, share_of(1, group_index, arrays), distant)
    )
    chips = range(1, groups // 2)
    plane = jnp.stack([column] + [swapped(column, "dp", 2 * chip) for chip in chips])
    came = direct_pieces(second, sections)
    came[sections // 2], distant = lax.optimization_barrier((came[sections // 2], distant))
    came = relayed_pieces(came, sections)
    far = swapped(distant, "pipe", sections // 2)
    plane, came, far, distant = lax.optimization_barrier((plane, came, far, distant))
    first_shares = (plane, swapped(plane, "dp", 1))
    column = jnp.concatenate(came, axis=0)
    planes = [column] + [swapped(column, "dp", 2 * chip) for chip in chips[:-1]]
    far = relayed_pieces({**direct_pieces(distant, sections // 2), sections // 2: far}, sections)

    key_parts = key_weight.reshape(2, groups, share, head_size)
    value_parts = value_weight.reshape(2, groups, share, head_size)

    def layers_call(kernel, turns, outs, operands, shares, scratch, cost, vmem_bytes, whole, any_outs):
        weight = pltpu.VMEM((groups, sections * share, line_width), jnp.bfloat16)
        return call(
            kernel,
            outs,
            (*operands, key_parts, value_parts, *shares),
            whole=2 + len(shares) + whole,
            any_outs=any_outs,
            scratch=[
                *scratch,
                *[weight] * turns,
                pltpu.SemaphoreType.DMA((2, 4)),
            ],
            vmem_bytes=vmem_bytes,
            cost=cost,
        )

    def blocks_shape(columns):
        return jax.ShapeDtypeStruct((sections, groups, row_count, columns), jnp.bfloat16)

    def exchanged(blocks):
        columns = blocks.shape[3]
        got = exchange(blocks.reshape(devices, row_count, columns))
        return got.reshape(devices * row_count, columns)

    line = (row_count, state_width(feature_count, head_size))
    line_count = plane.shape[1] - (sections - 1) * share
    gain_scratch = pltpu.VMEM((2 * sections, feature_count), jnp.float32)
    state_shape = (sections + 2 + 2 * sections // row_count, *line)
    state, packed = layers_call(
        functools.partial(first_kernel, doc_count=lengths.shape[1]),
        1,
        [jax.ShapeDtypeStruct(state_shape, jnp.float32), blocks_shape(share)],
        (upstream,),
        first_shares,
        (
            pltpu.VMEM(state_shape, jnp.float32),
            pltpu.VMEM((2, groups // 2, line_count, line_width), jnp.bfloat16),
            pltpu.VMEM((sections, row_count, column_count), jnp.float32),
            pltpu.VMEM((groups, 2 * sections, share), jnp.float32),
            gain_scratch,
            pltpu.SemaphoreType.DMA((3,)),
        ),
        18 << 20,
        (8 << 20) + sections * feature_count * 2 * line_width + 1024 * devices * row_count,
        0,
        1,
    )
    state, planes, far = lax.optimization_barrier((state, planes, far))
    plane = jnp.stack(planes + [jnp.concatenate(far, axis=0)])
    plane, packed = lax.optimization_barrier((plane, packed))
    packed = exchanged(packed)
    second_shares = (plane, swapped(plane, "dp", 1))
    columns = share + 4 * head_size + width
    (late,) = layers_call(
        second_kernel,
        2,
        [blocks_shape(columns)],
        (state,),
        (*first_shares, *second_shares),
        (
            pltpu.VMEM(state_shape, jnp.float32),
            pltpu.VMEM((sections, *line), jnp.float32),
            gain_scratch,
            pltpu.SemaphoreType.DMA((1,)),
        ),
        48 << 20,
        47 << 20,
        1,
        0,
    )
    late, packed = lax.optimization_barrier((late, packed))
    late = exchanged(late)
    grad_shape = jax.ShapeDtypeStruct((2, share, head_size), jnp.float32)
    return tuple(
        call(
            functools.partial(last_kernel, groups=groups),
            [jax.ShapeDtypeStruct((source_rows, column_count), jnp.bfloat16)] + [grad_shape] * 2,
            (route, packed, late),
            scalars=1,
            vmem_bytes=(4 << 20) + 10000 * devices * row_count,
        )
    )


def solution(mesh):
    placed = (
        P("dp", "pipe"),
        P("dp", None),
        P("dp", None),
        P("pipe", None),
        P("pipe", None, None),
        P("pipe", None, None),
        P("dp", None),
    )
    return jax.shard_map(
        body,
        mesh=mesh,
        in_specs=placed,
        out_specs=(P("dp", "pipe"), P("pipe", "dp", None), P("pipe", "dp", None)),
        check_vma=False,
    )
```

```python
import functools

import jax
import jax.numpy as jnp
from jax import lax
from jax.experimental import pallas as pl
from jax.experimental.pallas import tpu as pltpu
from jax.sharding import PartitionSpec as P

ROPE_BASE = 500000.0
EPSILON = 1e-05
NEGATIVE = -1e30
LANES = 128
GAIN_LINES = 8


def iota(shape, dim):
    return lax.broadcasted_iota(jnp.int32, shape, dim)


def as_float(flags):
    return jnp.where(flags, 1.0, 0.0).astype(jnp.float32)


def contract(left, right, left_dim, right_dim):
    return lax.dot_general(
        left, right, (((left_dim,), (right_dim,)), ((), ())), preferred_element_type=jnp.float32
    )


def pieces_of(column_count):
    return 2 if column_count % (2 * LANES) == 0 else 1


def fold(rows, width):
    row_count, columns = rows.shape
    if columns >= width:
        return jnp.concatenate(
            [rows[:, start : start + width] for start in range(0, columns, width)], axis=0
        )
    lines = row_count * columns // width
    return jnp.concatenate(
        [rows[start : start + lines] for start in range(0, row_count, lines)], axis=1
    )


def unfold(lines, row_count, columns):
    width = lines.shape[1]
    if columns >= width:
        return jnp.concatenate(
            [lines[start : start + row_count] for start in range(0, lines.shape[0], row_count)],
            axis=1,
        )
    return jnp.concatenate(
        [lines[:, start : start + columns] for start in range(0, width, columns)], axis=0
    )


def choosers(source, groups, pieces):
    row_count = source.shape[0]
    half = row_count // 2
    shape = (row_count, groups * row_count)
    row, line = iota(shape, 0), iota(shape, 1)
    back = source.astype(jnp.int32) == line // row_count
    return [
        as_float(back & (line % row_count == piece * half + row % half)).astype(jnp.bfloat16)
        for piece in range(pieces)
    ]


def turned(vector, cosine, sine):
    return vector * cosine + pltpu.roll(vector, vector.shape[1] // 2, 1) * sine


def heads_down(rows, head_size):
    count = rows.shape[1] // head_size
    return jnp.concatenate(
        [rows[:, head * head_size : (head + 1) * head_size] for head in range(count)], axis=0
    )


def heads_across(stacked, row_count):
    count = stacked.shape[0] // row_count
    return jnp.concatenate(
        [stacked[head * row_count : (head + 1) * row_count] for head in range(count)], axis=1
    )


def turned_heads(rows, cosine, sine):
    stacked = heads_down(rows, cosine.shape[1])
    repeats = stacked.shape[0] // rows.shape[0]
    return turned(stacked, jnp.tile(cosine, (repeats, 1)), jnp.tile(sine, (repeats, 1)))


def forward_layer(rows, gain_row, weight, cosine, sine, allowed):
    row_count, feature_count = rows.shape
    head_size = cosine.shape[1]
    scale = lax.rsqrt(jnp.sum(rows * rows, axis=1, keepdims=True) / feature_count + EPSILON)
    normed = rows * scale * gain_row
    packed = normed.astype(jnp.bfloat16)
    pair = contract(packed, weight, 1, 0)
    queries = turned_heads(normed, cosine, sine).astype(jnp.bfloat16)
    keys = turned(pair[:, :head_size], cosine, sine).astype(jnp.bfloat16)
    values = pair[:, head_size:].astype(jnp.bfloat16)
    scores = contract(keys, queries, 1, 1) * head_size ** (-0.5)
    scores = jnp.where(allowed, scores, NEGATIVE)
    raised = jnp.exp(scores - jnp.max(scores, axis=0, keepdims=True))
    weights = raised / jnp.sum(raised, axis=0, keepdims=True)
    mixed = contract(weights.astype(jnp.bfloat16), values, 0, 0)
    kept = (scale, keys, values, weights)
    return rows + heads_across(mixed, row_count), packed, kept


def backward_layer(upstream, rows, gain_row, weight, cosine, sine, kept):
    scale, keys, values, weights = kept
    row_count, feature_count = rows.shape
    head_size = cosine.shape[1]
    queries = turned_heads(rows * scale * gain_row, cosine, sine).astype(jnp.bfloat16)
    stacked = heads_down(upstream, head_size).astype(jnp.bfloat16)
    d_weights = contract(values, stacked, 1, 1).astype(jnp.bfloat16).astype(jnp.float32)
    d_values = contract(weights.astype(jnp.bfloat16), stacked, 1, 0)
    d_scores = weights * (d_weights - jnp.sum(d_weights * weights, axis=0, keepdims=True))
    d_scores = (d_scores * head_size ** (-0.5)).astype(jnp.bfloat16)
    d_keys = contract(d_scores, queries, 1, 0)
    terms = jnp.concatenate([turned(d_keys, cosine, -sine), d_values], axis=1)
    terms = terms.astype(jnp.bfloat16)
    d_queries = contract(d_scores, keys, 0, 0)
    repeats = stacked.shape[0] // row_count
    d_queries = turned(d_queries, jnp.tile(cosine, (repeats, 1)), jnp.tile(-sine, (repeats, 1)))
    d_normed = contract(terms, weight, 1, 1) + heads_across(d_queries, row_count)
    scaled = d_normed * gain_row
    inner = jnp.sum(scaled * rows, axis=1, keepdims=True) / feature_count
    return upstream + scale * scaled - rows * (scale * scale * scale * inner), terms


def state_width(feature_count, head_size):
    return feature_count + 4 * head_size


def save_layer(index, rows, kept, state_ref):
    scale, keys, values, weights = kept
    feature_count, head_size = rows.shape[1], keys.shape[1]
    state_ref[index, :, :feature_count] = rows
    parts = (weights, keys, values, jnp.broadcast_to(scale, keys.shape))
    for place, part in enumerate(parts):
        start = feature_count + place * head_size
        state_ref[index, :, start : start + head_size] = part.astype(jnp.float32)


def load_layer(index, state_ref, feature_count):
    head_size = (state_ref.shape[2] - feature_count) // 4
    parts = []
    for place in range(4):
        start = feature_count + place * head_size
        parts.append(state_ref[index, :, start : start + head_size])
    weights, keys, values, scale = parts
    kept = (scale[:, 0:1], keys.astype(jnp.bfloat16), values.astype(jnp.bfloat16), weights)
    return state_ref[index, :, :feature_count], kept


def repeat_steps(count, step, carry):
    if count <= 8:
        for index in range(count):
            carry = step(index, carry)
        return carry
    return lax.fori_loop(0, count, step, carry)


def layer_inputs(index, gain_ref, weight_ref, sections):
    place = lax.bitwise_xor(lax.axis_index("pipe"), index)
    groups = weight_ref.shape[0]
    share = weight_ref.shape[1] // sections
    rows = pl.ds(pl.multiple_of(place * share, share), share)
    weight = []
    for owner in range(groups):
        mask = lax.bitwise_xor(lax.axis_index("dp"), owner)
        line = lax.rem(mask, 2) * (groups // 2) + lax.div(mask, 2)
        weight.append(weight_ref[jnp.where(place == 0, owner, line), rows, :])
    return gain_ref[pl.ds(place, 1), :], jnp.concatenate(weight, axis=0)


def forward_steps(rows, gain_ref, weight_ref, tables, state_ref, packed_ref):
    cosine, sine, allowed = tables
    sections, groups = packed_ref.shape[:2]
    share = weight_ref.shape[1] // sections

    def step(index, rows):
        gain_row, weight = layer_inputs(index, gain_ref, weight_ref, sections)
        after, packed, kept = forward_layer(rows, gain_row, weight, cosine, sine, allowed)
        for group in range(groups):
            packed_ref[index, group, :, :share] = packed[:, group * share : (group + 1) * share]
        save_layer(index, rows, kept, state_ref)
        return after

    return repeat_steps(sections, step, rows)


def backward_steps(upstream, gain_ref, weight_ref, tables, state_ref, terms_ref, start):
    cosine, sine, _ = tables
    sections, groups = terms_ref.shape[:2]
    width = weight_ref.shape[2]

    def step(back, upstream):
        index = sections - 1 - back
        gain_row, weight = layer_inputs(index, gain_ref, weight_ref, sections)
        rows, kept = load_layer(index, state_ref, upstream.shape[1])
        before, terms = backward_layer(upstream, rows, gain_row, weight, cosine, sine, kept)
        for group in range(groups):
            terms_ref[index, group, :, start : start + width] = terms
        return before

    return repeat_steps(sections, step, upstream)


def fill(turn, key_ref, value_ref, shares, weight_ref, sems):
    groups, share, head_size = key_ref.shape[1:]
    moved = weight_ref.shape[1] - share
    copies = [
        (key_ref.at[turn], weight_ref.at[:, :share, :head_size]),
        (value_ref.at[turn], weight_ref.at[:, :share, head_size:]),
    ]
    for core, ref in enumerate(shares):
        lines = pl.ds(core * (groups // 2), groups // 2)
        copies.append((ref.at[:, pl.ds(0, moved)], weight_ref.at[lines, pl.ds(share, moved)]))
    copies = [
        pltpu.make_async_copy(*pair, sems.at[turn, index]) for index, pair in enumerate(copies)
    ]
    for copy in copies:
        copy.start()
    return copies


def first_kernel(
    upstream_ref,
    key_ref,
    value_ref,
    share_ref,
    other_ref,
    state_out,
    packed_ref,
    state_ref,
    lines_ref,
    rows_ref,
    gains_ref,
    gain_ref,
    line_sems,
    weight_ref,
    sems,
    *,
    doc_count
):
    sections = packed_ref.shape[0]
    groups, share, head_size = key_ref.shape[1:]
    row_count, feature_count = upstream_ref.shape
    column_count = feature_count // sections
    chips, line_count, width = lines_ref.shape[1:]
    used = share_ref.shape[1] - line_count
    section, group = lax.axis_index("pipe"), lax.axis_index("dp")
    shares = (share_ref, other_ref)
    line_copies = [
        pltpu.make_async_copy(
            ref.at[:, pl.ds(used, line_count)], lines_ref.at[core], line_sems.at[core]
        )
        for core, ref in enumerate(shares)
    ]
    for copy in line_copies:
        copy.start()
    copies = fill(0, key_ref, value_ref, shares, weight_ref, sems)
    state_ref[sections + 1, :, :feature_count] = upstream_ref[...]
    for copy in line_copies:
        copy.wait()

    row = iota((row_count, 1), 0)
    offset = row.astype(jnp.float32)
    document = jnp.zeros((row_count, 1), jnp.float32)
    position = jnp.zeros((row_count, 1), jnp.float32)
    source = jnp.zeros((row_count, 1), jnp.float32)
    parts = [jnp.zeros((row_count, column_count), jnp.float32) for _ in range(sections)]
    folded = row_count * column_count // width
    tail = folded + GAIN_LINES
    for core in range(2):
        for chip in range(chips):
            lines = lines_ref[core, chip].astype(jnp.float32)
            tags = lines[sections * tail :]
            tags = jnp.sum(
                jnp.where(iota(tags.shape, 0) == section, tags, 0.0), axis=0, keepdims=True
            )
            target = jnp.where(
                row < row_count // 2,
                tags[:, doc_count : doc_count + 1],
                tags[:, doc_count + 1 : doc_count + 2],
            )
            came = as_float(target.astype(jnp.int32) == group)
            end = jnp.zeros((1, 1), jnp.float32)
            number = jnp.zeros((row_count, 1), jnp.float32)
            opening = jnp.zeros((row_count, 1), jnp.float32)
            for doc in range(doc_count - 1):
                end = end + tags[:, doc : doc + 1]
                passed = offset >= end
                number = number + as_float(passed)
                opening = jnp.where(passed, end, opening)
            owner = lax.bitwise_xor(group, 2 * chip + core)
            document += came * number
            position += came * (offset - opening)
            source += came * owner.astype(jnp.float32)
            gain_rows = []
            for mask in range(sections):
                piece = lines[mask * tail : mask * tail + folded]
                parts[mask] += came * unfold(piece, row_count, column_count)
                terms = lines[mask * tail + folded : (mask + 1) * tail, :share]
                gain_rows += [
                    terms[3 * turn : 3 * turn + 1]
                    + terms[3 * turn + 1 : 3 * turn + 2]
                    + terms[3 * turn + 2 : 3 * turn + 3]
                    for turn in range(2)
                ]
            gains_ref[owner] = jnp.concatenate(gain_rows[0::2] + gain_rows[1::2], axis=0)
    for owner in range(groups):
        gain_ref[:, owner * share : (owner + 1) * share] = gains_ref[owner]
    for start in range(0, 2 * sections, row_count):
        state_ref[sections + 2 + start // row_count, :, :feature_count] = gain_ref[
            start : start + row_count
        ]
    for mask in range(sections):
        rows_ref[lax.bitwise_xor(section, mask)] = parts[mask]
    rows = jnp.concatenate([rows_ref[index] for index in range(sections)], axis=1)

    lane = iota((1, head_size), 1)
    middle = head_size // 2
    exponent = (lane % middle).astype(jnp.float32) * (2.0 / head_size)
    angles = position * jnp.exp(exponent * -jnp.log(jnp.float32(ROPE_BASE)))
    cosine = jnp.cos(angles)
    sine = jnp.where(lane < middle, -jnp.sin(angles), jnp.sin(angles))
    shape = (row_count, row_count * feature_count // head_size)
    pick = as_float(iota(shape, 1) % row_count == iota(shape, 0))
    document_across = jnp.sum(document * pick, axis=0, keepdims=True)
    position_across = jnp.sum(position * pick, axis=0, keepdims=True)
    allowed = (document == document_across) & (position <= position_across)
    kept = (cosine, sine, as_float(allowed), jnp.broadcast_to(source, cosine.shape))
    for place, table in enumerate(kept):
        start = feature_count + place * head_size
        state_ref[sections, :, start : start + head_size] = table
    tables = (cosine, sine, allowed)
    for copy in copies:
        copy.wait()
    state_ref[sections, :, :feature_count] = forward_steps(
        rows, gain_ref.at[pl.ds(0, sections)], weight_ref, tables, state_ref, packed_ref
    )
    state_copy = pltpu.make_async_copy(state_ref, state_out, line_sems.at[2])
    state_copy.start()
    state_copy.wait()


def second_kernel(
    state_in,
    key_ref,
    value_ref,
    share_ref,
    other_ref,
    late_share_ref,
    late_other_ref,
    out_ref,
    first_ref,
    state_ref,
    gain_ref,
    state_sem,
    late_weight_ref,
    weight_ref,
    sems
):
    state_copy = pltpu.make_async_copy(state_in, first_ref, state_sem.at[0])
    state_copy.start()
    sections, groups, row_count, _ = out_ref.shape
    share, head_size = key_ref.shape[2:]
    feature_count, term_width = groups * share, 2 * head_size
    late_shares = (late_share_ref, late_other_ref)
    late_copies = fill(1, key_ref, value_ref, late_shares, late_weight_ref, sems)
    copies = fill(0, key_ref, value_ref, (share_ref, other_ref), weight_ref, sems)
    state_copy.wait()
    kept = []
    for place in range(4):
        start = feature_count + place * head_size
        kept.append(first_ref[sections, :, start : start + head_size])
    cosine, sine, allowed, source = kept
    tables = (cosine, sine, allowed > 0.5)
    for start in range(0, 2 * sections, row_count):
        gain_ref[start : start + row_count] = first_ref[
            sections + 2 + start // row_count, :, :feature_count
        ]
    late_gain = gain_ref.at[pl.ds(sections, sections)]
    for copy in late_copies:
        copy.wait()
    forward_steps(
        first_ref[sections, :, :feature_count],
        late_gain,
        late_weight_ref,
        tables,
        state_ref,
        out_ref,
    )
    upstream = backward_steps(
        first_ref[sections + 1, :, :feature_count],
        late_gain,
        late_weight_ref,
        tables,
        state_ref,
        out_ref,
        share + term_width,
    )
    for copy in copies:
        copy.wait()
    grads = backward_steps(
        upstream,
        gain_ref.at[pl.ds(0, sections)],
        weight_ref,
        tables,
        first_ref,
        out_ref,
        share,
    ).astype(jnp.bfloat16)
    column_count = feature_count // sections
    pieces = pieces_of(column_count)
    width = column_count // pieces
    chosen = choosers(source[:, 0:1], groups, pieces)
    for section in range(sections):
        start = section * column_count
        going = contract(chosen[0], grads[:, start : start + width], 0, 0)
        for piece in range(1, pieces):
            left = start + piece * width
            going += contract(chosen[piece], grads[:, left : left + width], 0, 0)
        going = going.astype(jnp.bfloat16)
        for group in range(groups):
            out_ref[section, group, :, share + 2 * term_width :] = going[
                group * row_count : (group + 1) * row_count
            ]


def last_kernel(
    route_ref, first_ref, late_ref, grad_ref, key_ref, value_ref, *, groups
):
    micro_count = route_ref.shape[0]
    source_rows, column_count = grad_ref.shape
    row_count = source_rows // micro_count
    half = row_count // 2
    share, head_size = key_ref.shape[1:]
    term_width = 2 * head_size
    width = late_ref.shape[1] - share - 2 * term_width
    pieces = column_count // width
    for index, packed in enumerate((first_ref[...], late_ref[:, :share])):
        start = share + index * term_width
        total = contract(packed, late_ref[:, start : start + term_width], 0, 0)
        key_ref[index] = total[:, :head_size]
        value_ref[index] = total[:, head_size:]
    shape = (source_rows, late_ref.shape[0])
    row, source = iota(shape, 1), iota(shape, 0)
    slot = source // half
    target = jnp.full(shape, -1, jnp.int32)
    for micro in range(micro_count):
        for side in range(2):
            target = jnp.where(
                slot == 2 * micro + side, micro * groups + route_ref[micro, side], target
            )
    going = target == row // row_count
    inner, wanted = row % row_count, source % half
    for piece in range(pieces):
        chosen = as_float(going & (inner == piece * half + wanted)).astype(jnp.bfloat16)
        grad_ref[:, piece * width : (piece + 1) * width] = contract(
            chosen, late_ref[:, share + 2 * term_width :], 1, 0
        ).astype(jnp.bfloat16)


def call(kernel, outs, operands, scalars=0, whole=0, any_outs=0, scratch=(), vmem_bytes=0, cost=0):
    spaces = [pltpu.SMEM] * scalars + [pltpu.VMEM] * (len(operands) - scalars - whole)
    spaces += [pl.ANY] * whole
    return pl.pallas_call(
        kernel,
        out_shape=outs,
        in_specs=[pl.BlockSpec(memory_space=space) for space in spaces],
        out_specs=[
            pl.BlockSpec(memory_space=pl.ANY if place < any_outs else pltpu.VMEM)
            for place in range(len(outs))
        ],
        scratch_shapes=scratch,
        compiler_params=pltpu.CompilerParams(vmem_limit_bytes=vmem_bytes),
        cost_estimate=pl.CostEstimate(flops=0, bytes_accessed=cost, transcendentals=0),
    )(*operands)


def exchange(blocks):
    return lax.all_to_all(blocks, ("pipe", "dp"), split_axis=0, concat_axis=0, tiled=True)


def swapped(value, axis, mask):
    pairs = [(source, source ^ mask) for source in range(lax.axis_size(axis))]
    return lax.ppermute(value, axis, pairs)


def direct_pieces(payload, sections):
    masks = [mask for mask in range(1, sections) if mask & (mask - 1) == 0]
    return {mask: swapped(payload, "pipe", mask) for mask in masks}


def relayed_pieces(pieces, sections):
    pieces = dict(pieces)
    for mask in range(1, sections):
        low = mask & -mask
        if mask != low:
            pieces[mask] = swapped(pieces[mask - low], "pipe", low)
    return [pieces[mask] for mask in range(1, sections)]


def body(hidden, lengths, route, gain, key_weight, value_weight, cotangent):
    groups = lax.axis_size("dp")
    sections = lax.axis_size("pipe")
    group_index = lax.axis_index("dp")
    section_index = lax.axis_index("pipe")
    micro_count = lengths.shape[0]
    assert micro_count == sections
    source_rows, column_count = hidden.shape
    row_count = source_rows // micro_count
    feature_count = gain.shape[1]
    head_size = key_weight.shape[2]
    assert row_count * feature_count == head_size * head_size
    share = feature_count // groups
    width = column_count // pieces_of(column_count)
    devices = sections * groups

    line_width = 2 * head_size

    def share_of(turn, owner, arrays):
        parts = [
            lax.dynamic_slice(array, (turn, owner * share, 0), (1, share, head_size))[0]
            for array in arrays
        ]
        return jnp.concatenate(parts, axis=1)

    def own_rows(mask):
        start = lax.bitwise_xor(section_index, mask) * row_count
        rows = lax.dynamic_slice(hidden, (start, 0), (row_count, column_count))
        return fold(rows, line_width)

    slice_ = lax.dynamic_slice(gain, (0, group_index * share), (2, share))
    high = lax.reduce_precision(slice_, 8, 7)
    middle = lax.reduce_precision(slice_ - high, 8, 7)
    terms = jnp.stack([high, middle, slice_ - high - middle], axis=1).reshape(6, share)
    terms = jnp.pad(
        terms.astype(jnp.bfloat16), ((0, GAIN_LINES - 6), (0, line_width - share))
    )

    first = share_of(0, group_index, (key_weight, value_weight))
    came = [
        swapped(jnp.concatenate([first, own_rows(mask), terms], axis=0), "pipe", mask)
        for mask in range(1, sections)
    ]
    tags = jnp.concatenate([lengths, route], axis=1).astype(jnp.bfloat16)
    tags = jnp.pad(tags, ((0, -micro_count % 16), (0, line_width - tags.shape[1])))
    upstream = lax.dynamic_slice_in_dim(
        cotangent, section_index * row_count, row_count, 0
    ).astype(jnp.float32)
    tags, own_tail, upstream = lax.optimization_barrier(
        (tags, jnp.concatenate([own_rows(0), terms], axis=0), upstream)
    )
    _, *arrays = lax.optimization_barrier((tags, key_weight, value_weight))
    column = jnp.concatenate(
        [piece[:share] for piece in came]
        + [own_tail]
        + [piece[share:] for piece in came]
        + [tags],
        axis=0,
    )
    distant = share_of(1, lax.bitwise_xor(group_index, groups - 2), arrays)
    column, second, distant = lax.optimization_barrier(
        (column, share_of(1, group_index, arrays), distant)
    )
    chips = range(1, groups // 2)
    plane = jnp.stack([column] + [swapped(column, "dp", 2 * chip) for chip in chips])
    came = direct_pieces(second, sections)
    came[sections // 2], distant = lax.optimization_barrier((came[sections // 2], distant))
    came = relayed_pieces(came, sections)
    far = swapped(distant, "pipe", sections // 2)
    plane, came, far, distant = lax.optimization_barrier((plane, came, far, distant))
    first_shares = (plane, swapped(plane, "dp", 1))
    column = jnp.concatenate(came, axis=0)
    planes = [column] + [swapped(column, "dp", 2 * chip) for chip in chips[:-1]]
    far = relayed_pieces({**direct_pieces(distant, sections // 2), sections // 2: far}, sections)

    key_parts = key_weight.reshape(2, groups, share, head_size)
    value_parts = value_weight.reshape(2, groups, share, head_size)

    def layers_call(kernel, turns, outs, operands, shares, scratch, cost, vmem_bytes, whole, any_outs):
        weight = pltpu.VMEM((groups, sections * share, line_width), jnp.bfloat16)
        return call(
            kernel,
            outs,
            (*operands, key_parts, value_parts, *shares),
            whole=2 + len(shares) + whole,
            any_outs=any_outs,
            scratch=[
                *scratch,
                *[weight] * turns,
                pltpu.SemaphoreType.DMA((2, 4)),
            ],
            vmem_bytes=vmem_bytes,
            cost=cost,
        )

    def blocks_shape(columns):
        return jax.ShapeDtypeStruct((sections, groups, row_count, columns), jnp.bfloat16)

    def exchanged(blocks):
        columns = blocks.shape[3]
        got = exchange(blocks.reshape(devices, row_count, columns))
        return got.reshape(devices * row_count, columns)

    line = (row_count, state_width(feature_count, head_size))
    line_count = plane.shape[1] - (sections - 1) * share
    gain_scratch = pltpu.VMEM((2 * sections, feature_count), jnp.float32)
    state_shape = (sections + 2 + 2 * sections // row_count, *line)
    state, packed = layers_call(
        functools.partial(first_kernel, doc_count=lengths.shape[1]),
        1,
        [jax.ShapeDtypeStruct(state_shape, jnp.float32), blocks_shape(share)],
        (upstream,),
        first_shares,
        (
            pltpu.VMEM(state_shape, jnp.float32),
            pltpu.VMEM((2, groups // 2, line_count, line_width), jnp.bfloat16),
            pltpu.VMEM((sections, row_count, column_count), jnp.float32),
            pltpu.VMEM((groups, 2 * sections, share), jnp.float32),
            gain_scratch,
            pltpu.SemaphoreType.DMA((3,)),
        ),
        18 << 20,
        (8 << 20) + sections * feature_count * 2 * line_width + 1024 * devices * row_count,
        0,
        1,
    )
    state, planes, far = lax.optimization_barrier((state, planes, far))
    plane = jnp.stack(planes + [jnp.concatenate(far, axis=0)])
    plane, packed = lax.optimization_barrier((plane, packed))
    packed = exchanged(packed)
    second_shares = (plane, swapped(plane, "dp", 1))
    columns = share + 4 * head_size + width
    (late,) = layers_call(
        second_kernel,
        2,
        [blocks_shape(columns)],
        (state,),
        (*first_shares, *second_shares),
        (
            pltpu.VMEM(state_shape, jnp.float32),
            pltpu.VMEM((sections, *line), jnp.float32),
            gain_scratch,
            pltpu.SemaphoreType.DMA((1,)),
        ),
        48 << 20,
        48 << 20,
        1,
        0,
    )
    late, packed = lax.optimization_barrier((late, packed))
    late = exchanged(late)
    grad_shape = jax.ShapeDtypeStruct((2, share, head_size), jnp.float32)
    return tuple(
        call(
            functools.partial(last_kernel, groups=groups),
            [jax.ShapeDtypeStruct((source_rows, column_count), jnp.bfloat16)] + [grad_shape] * 2,
            (route, packed, late),
            scalars=1,
            vmem_bytes=(4 << 20) + 10000 * devices * row_count,
        )
    )


def solution(mesh):
    placed = (
        P("dp", "pipe"),
        P("dp", None),
        P("dp", None),
        P("pipe", None),
        P("pipe", None, None),
        P("pipe", None, None),
        P("dp", None),
    )
    return jax.shard_map(
        body,
        mesh=mesh,
        in_specs=placed,
        out_specs=(P("dp", "pipe"), P("pipe", "dp", None), P("pipe", "dp", None)),
        check_vma=False,
    )
```
